32 devices in a mesh: tm: 8 (over z, x), space: 4 (over y, core).
Axes of the slice: x: 2, y: 2, z: 4, core: 2. Of those that a mesh axis runs over, the one named last changes fastest.
Arguments:
- state: float32 [16, 3, 128, 1024], P('tm', None, 'space'), may hold values from -2.5 to 2.5
- initial: float32 [3, 128, 1024], P(None, 'space'), may hold values from -2.5 to 2.5
Outputs:
- updated: float32 [16, 3, 128, 1024], P('tm', None, 'space')
The draws below stay inside these ranges and needn't reach their ends.
All inputs are finite; a program needn't handle non-finite values.
Results may differ from the reference program's by a relative error of at most 0.0003.
Values sent between devices are 32-bit elements; how exact they have to be, the bound alone decides.
No kernel may reach another device: no remote copies, remote signals or barrier semaphores. Data moves between devices by JAX's collectives and lax.ppermute only.
A program may use at most 128 MiB of HBM per device.

```python
import math
import jax
import jax.numpy as jnp
from jax import lax

NX = 1024
SWEEPS = 4
NT = 16
NY = 128


def shard_levels(own_key, dims, cuts, least, high):
    factor_of = 1.0
    for axis_at, blocks in cuts:
        steps = jax.random.uniform(jax.random.fold_in(jax.random.fold_in(own_key, 6), axis_at), (blocks,), jnp.float32, least / len(cuts), high / len(cuts))
        factor_of = factor_of * jnp.repeat(jnp.exp(steps), dims[axis_at] // blocks).reshape((-1,) + (1,) * (len(dims) - 1 - axis_at))
    return factor_of


def scatter_about(rng, extent, spread, bound, pieces=(), kind=jnp.bfloat16):
    drawn = jax.random.normal(rng, extent, jnp.float32) * spread
    if len(pieces) > 0:
        drawn = shard_levels(rng, extent, pieces, -0.22, 0.18) * drawn
    return jnp.clip(drawn, min=-bound, max=bound).astype(kind)


def setup_inputs(seed: int = 0) -> dict:
    arg_keys = jax.random.split(jax.random.key(seed), 3)
    state = scatter_about(arg_keys[0], (NT, 3, NY, NX), 0.3, 2.5, ((0, 8), (2, 4)), jnp.float32)
    initial = scatter_about(arg_keys[1], (3, NY, NX), 0.3, 2.5, ((1, 4),), jnp.float32)
    return {"state": state, "initial": initial}


circulant_alpha = 0.1
time_step = 0.5
coriolis = 0.3
viscous = 0.2
highest = lax.Precision.HIGHEST


def interior(values):
    return values[..., 1:-1, :]


def column_diff(values):
    return 0.5 * (jnp.roll(values, -1, axis=-1) - jnp.roll(values, 1, axis=-1))[..., 1:-1, :]


def row_diff(values):
    return 0.5 * (values[..., 2:, :] - values[..., :-2, :])


def laplace(values):
    return (values[..., 2:, :] + values[..., :-2, :] + jnp.roll(values, -1, axis=-1)[..., 1:-1, :]
            + jnp.roll(values, 1, axis=-1)[..., 1:-1, :] - 4.0 * values[..., 1:-1, :])


def wrap_rows(values, width):
    return jnp.concatenate([values[..., -width:, :], values, values[..., :width, :]], axis=-2)


def tendency(padded):
    surface = padded[..., 0, :, :]
    eastward = padded[..., 1, :, :]
    northward = padded[..., 2, :, :]
    column_depth = 1.0 + surface
    east_inner = interior(eastward)
    north_inner = interior(northward)
    mass_change = time_step * (column_diff(column_depth * eastward) + row_diff(column_depth * northward)) - viscous * laplace(surface)
    east_change = time_step * (east_inner * column_diff(eastward) + north_inner * row_diff(eastward) + column_diff(surface)) - coriolis * north_inner - viscous * laplace(eastward)
    north_change = time_step * (east_inner * column_diff(northward) + north_inner * row_diff(northward) + row_diff(surface)) + coriolis * east_inner - viscous * laplace(northward)
    return jnp.stack([mass_change, east_change, north_change], axis=-3)


def linear_part(padded):
    surface = padded[..., 0, :, :]
    eastward = padded[..., 1, :, :]
    northward = padded[..., 2, :, :]
    mass_change = time_step * (column_diff(eastward) + row_diff(northward)) - viscous * laplace(surface)
    east_change = time_step * column_diff(surface) - coriolis * interior(northward) - viscous * laplace(eastward)
    north_change = time_step * row_diff(surface) + coriolis * interior(eastward) - viscous * laplace(northward)
    return jnp.stack([mass_change, east_change, north_change], axis=-3)


def pair_apply(factors, values):
    factor = factors[:, :, None, None, None]
    return jnp.stack([factor[0] * values[0] - factor[1] * values[1], factor[2] * values[1] + factor[3] * values[0]])


def sweep_weights():
    return [1.0 / (1.15 - 0.85 * math.cos(math.pi * (2 * sweep + 1) / (2 * SWEEPS))) for sweep in range(SWEEPS)]


def slot_factors(slot_index, total_steps, packed):
    decay_base = circulant_alpha ** (1.0 / total_steps)
    angles = (2.0 * math.pi / total_steps) * slot_index.astype(jnp.float32)
    real_eigen = 1.0 - decay_base * jnp.cos(angles)
    imaginary_eigen = decay_base * jnp.sin(angles)
    real_shift = real_eigen + 4.0 * viscous
    modulus = real_shift * real_shift + imaginary_eigen * imaginary_eigen
    eigen = jnp.stack([real_eigen, imaginary_eigen, real_eigen, imaginary_eigen])
    jacobi = jnp.stack([real_shift / modulus, -imaginary_eigen / modulus, real_shift / modulus, -imaginary_eigen / modulus])
    if packed:
        leading = (slot_index == 0)[None, :]
        zero_part = jnp.zeros_like(real_eigen)
        packed_eigen = jnp.stack([zero_part + (1.0 - decay_base), zero_part, zero_part + (1.0 + decay_base), zero_part])
        packed_jacobi = jnp.stack([zero_part + 1.0 / (1.0 - decay_base + 4.0 * viscous), zero_part,
                                   zero_part + 1.0 / (1.0 + decay_base + 4.0 * viscous), zero_part])
        eigen = jnp.where(leading, packed_eigen, eigen)
        jacobi = jnp.where(leading, packed_jacobi, jacobi)
    return eigen, jacobi


def time_tables(total_steps, packed):
    slot_total = total_steps // 2 if packed else total_steps
    step_ids = jnp.arange(total_steps, dtype=jnp.int32)
    slot_ids = jnp.arange(slot_total, dtype=jnp.int32)
    phase = (slot_ids[:, None] * step_ids[None, :]) % total_steps
    angles = (2.0 * math.pi / total_steps) * phase.astype(jnp.float32)
    decay_base = circulant_alpha ** (1.0 / total_steps)
    growth = decay_base ** step_ids.astype(jnp.float32)
    cosine = jnp.cos(angles)
    sines = jnp.sin(angles)
    forward_real = cosine * growth[None, :]
    forward_imaginary = -sines * growth[None, :]
    inverse_real = cosine
    inverse_imaginary = -sines
    if packed:
        alternate = 1.0 - 2.0 * (step_ids % 2).astype(jnp.float32)
        leading = (slot_ids == 0)[:, None]
        forward_imaginary = jnp.where(leading, (alternate * growth)[None, :], forward_imaginary)
        inverse_real = jnp.where(leading, 1.0, 2.0 * cosine)
        inverse_imaginary = jnp.where(leading, alternate[None, :], -2.0 * sines)
    forward = jnp.concatenate([forward_real, forward_imaginary], axis=0)
    inverse = jnp.concatenate([inverse_real, inverse_imaginary], axis=0).T
    inverse = inverse * (1.0 / (total_steps * growth))[:, None]
    return forward, inverse


def relax(rhs, eigen, jacobi):
    weights = sweep_weights()
    iterate = weights[0] * pair_apply(jacobi, rhs)
    for sweep in range(1, SWEEPS):
        applied = pair_apply(eigen, iterate) + linear_part(wrap_rows(iterate, 1))
        iterate = iterate + weights[sweep] * pair_apply(jacobi, rhs - applied)
    return iterate


def reference(state, initial):
    before = jnp.concatenate([initial[None], state[:-1]], axis=0)

    def one_step(pair):
        current, earlier = pair
        return current - earlier + tendency(wrap_rows(current, 1))

    residual = lax.map(one_step, (state, before))
    forward, inverse = time_tables(NT, False)
    spectrum = jnp.dot(forward, residual.reshape(NT, 3 * NY * NX), precision=highest).reshape(2, NT, 3, NY, NX)
    eigen, jacobi = slot_factors(jnp.arange(NT, dtype=jnp.int32), NT, False)

    def solve_one(item):
        rhs, eigen_one, jacobi_one = item
        return relax(rhs[:, None], eigen_one[:, None], jacobi_one[:, None])[:, 0]

    solution = lax.map(solve_one, (jnp.moveaxis(spectrum, 1, 0), eigen.T, jacobi.T))
    solution = jnp.moveaxis(solution, 0, 1).reshape(2 * NT, 3 * NY * NX)
    correction = jnp.dot(inverse, solution, precision=highest).reshape(NT, 3, NY, NX)
    return state - correction
```

```python
import functools
import math

import jax
import jax.numpy as jnp
from jax import lax
from jax.experimental import pallas as pl
from jax.experimental.pallas import tpu as pltpu
from jax.sharding import PartitionSpec as P

SWEEPS = 4


circulant_alpha = 0.1
time_step = 0.5
coriolis = 0.3
viscous = 0.2
highest = lax.Precision.HIGHEST


def from_behind(block, axis, distance):
    devices = range(lax.axis_size(axis))
    route = [(i - distance, i) for i in devices if i - distance in devices]
    return lax.ppermute(block, axis, route)


def extended(cells, sides, width):
    for axis, dim in sides:
        count = lax.axis_size(axis)
        head = lax.slice_in_dim(cells, 0, width, axis=dim)
        tail = lax.slice_in_dim(cells, cells.shape[dim] - width, cells.shape[dim], axis=dim)
        cells = jnp.concatenate(
            [
                lax.ppermute(tail, axis, [(i, (i + 1) % count) for i in range(count)]),
                cells,
                lax.ppermute(head, axis, [((i + 1) % count, i) for i in range(count)]),
            ],
            axis=dim,
        )
    return cells


def interior(values):
    return values[..., 1:-1, :]


def column_diff(values):
    return 0.5 * (jnp.roll(values, -1, axis=-1) - jnp.roll(values, 1, axis=-1))[..., 1:-1, :]


def row_diff(values):
    return 0.5 * (values[..., 2:, :] - values[..., :-2, :])


def laplace(values):
    return (
        values[..., 2:, :]
        + values[..., :-2, :]
        + jnp.roll(values, -1, axis=-1)[..., 1:-1, :]
        + jnp.roll(values, 1, axis=-1)[..., 1:-1, :]
        - 4.0 * values[..., 1:-1, :]
    )


def tendency(padded):
    surface = padded[..., 0, :, :]
    eastward = padded[..., 1, :, :]
    northward = padded[..., 2, :, :]
    column_depth = 1.0 + surface
    east_inner = interior(eastward)
    north_inner = interior(northward)
    mass_change = time_step * (
        column_diff(column_depth * eastward) + row_diff(column_depth * northward)
    ) - viscous * laplace(surface)
    east_change = (
        time_step
        * (
            east_inner * column_diff(eastward)
            + north_inner * row_diff(eastward)
            + column_diff(surface)
        )
        - coriolis * north_inner
        - viscous * laplace(eastward)
    )
    north_change = (
        time_step
        * (
            east_inner * column_diff(northward)
            + north_inner * row_diff(northward)
            + row_diff(surface)
        )
        + coriolis * east_inner
        - viscous * laplace(northward)
    )
    return jnp.stack([mass_change, east_change, north_change], axis=-3)


def linear_part(padded):
    surface = padded[..., 0, :, :]
    eastward = padded[..., 1, :, :]
    northward = padded[..., 2, :, :]
    mass_change = time_step * (column_diff(eastward) + row_diff(northward)) - viscous * laplace(
        surface
    )
    east_change = (
        time_step * column_diff(surface)
        - coriolis * interior(northward)
        - viscous * laplace(eastward)
    )
    north_change = (
        time_step * row_diff(surface) + coriolis * interior(eastward) - viscous * laplace(northward)
    )
    return jnp.stack([mass_change, east_change, north_change], axis=-3)


def pair_apply(factors, values):
    factor = factors[:, :, None, None, None]
    return jnp.stack(
        [
            factor[0] * values[0] - factor[1] * values[1],
            factor[2] * values[1] + factor[3] * values[0],
        ]
    )


def sweep_weights():
    return [
        1.0 / (1.15 - 0.85 * math.cos(math.pi * (2 * sweep + 1) / (2 * SWEEPS)))
        for sweep in range(SWEEPS)
    ]


def slot_factors(slot_index, total_steps):
    decay_base = circulant_alpha ** (1.0 / total_steps)
    angles = 2.0 * math.pi / total_steps * slot_index.astype(jnp.float32)
    real_eigen = 1.0 - decay_base * jnp.cos(angles)
    imaginary_eigen = decay_base * jnp.sin(angles)
    real_shift = real_eigen + 4.0 * viscous
    modulus = real_shift * real_shift + imaginary_eigen * imaginary_eigen
    eigen = jnp.stack([real_eigen, imaginary_eigen, real_eigen, imaginary_eigen])
    jacobi = jnp.stack(
        [
            real_shift / modulus,
            -imaginary_eigen / modulus,
            real_shift / modulus,
            -imaginary_eigen / modulus,
        ]
    )
    leading = (slot_index == 0)[None, :]
    zero_part = jnp.zeros_like(real_eigen)
    packed_eigen = jnp.stack(
        [zero_part + (1.0 - decay_base), zero_part, zero_part + (1.0 + decay_base), zero_part]
    )
    packed_jacobi = jnp.stack(
        [
            zero_part + 1.0 / (1.0 - decay_base + 4.0 * viscous),
            zero_part,
            zero_part + 1.0 / (1.0 + decay_base + 4.0 * viscous),
            zero_part,
        ]
    )
    eigen = jnp.where(leading, packed_eigen, eigen)
    jacobi = jnp.where(leading, packed_jacobi, jacobi)
    return (eigen, jacobi)


def time_tables(total_steps):
    slot_total = total_steps // 2
    step_ids = jnp.arange(total_steps, dtype=jnp.int32)
    slot_ids = jnp.arange(slot_total, dtype=jnp.int32)
    phase = slot_ids[:, None] * step_ids[None, :] % total_steps
    angles = 2.0 * math.pi / total_steps * phase.astype(jnp.float32)
    decay_base = circulant_alpha ** (1.0 / total_steps)
    growth = decay_base ** step_ids.astype(jnp.float32)
    cosine = jnp.cos(angles)
    sines = jnp.sin(angles)
    forward_real = cosine * growth[None, :]
    forward_imaginary = -sines * growth[None, :]
    inverse_imaginary = -sines
    alternate = 1.0 - 2.0 * (step_ids % 2).astype(jnp.float32)
    leading = (slot_ids == 0)[:, None]
    forward_imaginary = jnp.where(leading, (alternate * growth)[None, :], forward_imaginary)
    inverse_real = jnp.where(leading, 1.0, 2.0 * cosine)
    inverse_imaginary = jnp.where(leading, alternate[None, :], -2.0 * sines)
    forward = jnp.concatenate([forward_real, forward_imaginary], axis=0)
    inverse = jnp.concatenate([inverse_real, inverse_imaginary], axis=0).T
    inverse = inverse * (1.0 / (total_steps * growth))[:, None]
    return (forward, inverse)


def on_device(state, initial):
    steps_dev, fields, band_rows, columns = state.shape
    width_tm = lax.axis_size("tm")
    total_steps = steps_dev * width_tm
    previous = from_behind(state[-1], "tm", 1)
    previous = jnp.where(lax.axis_index("tm") == 0, initial, previous)
    before = jnp.concatenate([previous[None], state[:-1]], axis=0)
    padded = extended(state, (("space", 2),), 1)
    residual = state - before + tendency(padded)
    forward, inverse = time_tables(total_steps)
    slot_total = forward.shape[0] // 2
    per_device = slot_total // width_tm
    spectrum = jnp.einsum(
        "rj,jnc->rnc",
        forward,
        lax.all_to_all(
            residual.reshape(steps_dev, fields, band_rows * columns),
            "tm",
            split_axis=2,
            concat_axis=0,
            tiled=True,
        ),
        precision=highest,
    )
    spectrum = spectrum.reshape(2, slot_total, fields, spectrum.shape[-1])
    banded = lax.all_to_all(spectrum, "tm", split_axis=1, concat_axis=3, tiled=True).reshape(
        2, per_device, fields, band_rows, columns
    )
    slot_index = lax.axis_index("tm") * per_device + jnp.arange(per_device, dtype=jnp.int32)
    eigen, jacobi = slot_factors(slot_index, total_steps)
    weights = sweep_weights()
    iterate = weights[0] * pair_apply(jacobi, banded)
    for sweep in range(1, SWEEPS):
        border = extended(iterate, (("space", 3),), 1)
        applied = pair_apply(eigen, iterate) + linear_part(border)
        iterate = iterate + weights[sweep] * pair_apply(jacobi, banded - applied)
    flat_solution = iterate.reshape(2, per_device, fields, band_rows * columns)
    blocks = lax.all_to_all(flat_solution, "tm", split_axis=3, concat_axis=1, tiled=True)
    merged = blocks.reshape(2 * blocks.shape[1], blocks.shape[2], blocks.shape[3])
    all_steps = jnp.einsum("jr,rnc->jnc", inverse, merged, precision=highest)
    correction = lax.all_to_all(all_steps, "tm", split_axis=0, concat_axis=2, tiled=True)
    return state - correction.reshape(state.shape)


LANES = 128
HALO = SWEEPS
GROUP = 2 * HALO
ROW0 = 8
MAIN = ROW0 + HALO
SHIFT = 1.0 + 4.0 * viscous
VMEM_BYTES = 48 * 1024 * 1024


def fits_fast_plan(state, width_tm):
    steps_dev, fields, band_rows, columns = state.shape
    total_steps = steps_dev * width_tm
    return (
        columns == LANES * width_tm
        and GROUP * total_steps == LANES
        and width_tm & (width_tm - 1) == 0
        and band_rows % 8 == 0
        and fields == 3
    )


def lanes():
    return lax.broadcasted_iota(jnp.int32, (8, LANES), 1)


def step_of_lane(lane):
    return ((lane + HALO) & (LANES - 1)) // GROUP


def turn(values, shift):
    return pltpu.roll(values, shift % LANES, 1)


def tile_at(index):
    return pl.ds(pl.multiple_of(index * LANES, LANES), LANES)


def pack_kernel(count, state_ref, *outs):
    steps_dev, fields, rows, _ = state_ref.shape
    me = lax.axis_index("tm")
    lane = lanes()
    step = step_of_lane(lane)
    blocks = rows // 8
    main = steps_dev * fields * rows
    for b in range(count):
        tile = me ^ b
        here = tile_at(tile)
        after = tile_at((tile + 1) & (count - 1))
        prior = tile_at((tile + count - 1) & (count - 1))
        out = outs[b]
        for i in range(steps_dev):
            for f in range(fields):
                at = (i * fields + f) * rows
                out[at : at + rows, :] = state_ref[i, f, :, here]
        for first in range(0, fields * blocks, count):
            packed = jnp.zeros((8, LANES), jnp.float32)
            for g in range(first, min(first + count, fields * blocks)):
                f, r = divmod(g, blocks)
                for i in range(steps_dev):
                    slot = steps_dev * (g - first) + i
                    sides = jnp.where(
                        lane < LANES // 2,
                        state_ref[i, f, 8 * r : 8 * r + 8, after],
                        state_ref[i, f, 8 * r : 8 * r + 8, prior],
                    )
                    packed = jnp.where(step == slot, turn(sides, GROUP * slot), packed)
            at = main + 8 * (first // count)
            out[at : at + 8, :] = packed


def edge_kernel(count, steps_dev, *refs):
    pieces, initial_ref = refs[:count], refs[count]
    up, down, side, side_initial = refs[count + 1 :]
    fields, rows, _ = initial_ref.shape
    me = lax.axis_index("tm")
    lane = lanes()
    owner = step_of_lane(lane) // steps_dev
    blocks = rows // 8
    main = steps_dev * fields * rows
    here = tile_at(me)
    after = tile_at((me + 1) & (count - 1))
    prior = tile_at((me + count - 1) & (count - 1))
    for g in range(fields * blocks):
        f, r = divmod(g, blocks)
        word, place = divmod(g, count)
        found = jnp.zeros((8, LANES), jnp.float32)
        for b in range(count):
            source = me ^ b
            value = pieces[b][main + 8 * word : main + 8 * word + 8, :]
            shift = (GROUP * steps_dev * (source - place)) & (LANES - 1)
            found = jnp.where(owner == source, pltpu.roll(value, shift, 1), found)
        side[f, 8 * r : 8 * r + 8, :] = found
        side_initial[f, 8 * r : 8 * r + 8, :] = jnp.where(
            lane < LANES // 2,
            initial_ref[f, 8 * r : 8 * r + 8, after],
            initial_ref[f, 8 * r : 8 * r + 8, prior],
        )
    low, high = slice(0, HALO), slice(rows - HALO, rows)
    for out, part in ((up, low), (down, high)):
        k = 0
        for b in range(count):
            for at in range(0, main, rows):
                out[k : k + HALO, :] = pieces[b][at + part.start : at + part.stop, :]
                k += HALO
        for f in range(fields):
            out[k : k + HALO, :] = initial_ref[f, part, here]
            k += HALO
        for f in range(fields):
            out[k : k + HALO, :] = side[f, part, :]
            k += HALO
        for f in range(fields):
            out[k : k + HALO, :] = side_initial[f, part, :]
            k += HALO


def full_tendency(own, east, west, north, south):
    e, u, v = own
    around = [east[f] + west[f] + (north[f] + south[f]) for f in range(3)]
    quarter = 0.5 * time_step
    flux = ((1.0 + east[0]) * east[1] - (1.0 + west[0]) * west[1]) + (
        (1.0 + south[0]) * south[2] - (1.0 + north[0]) * north[2]
    )
    carry1 = u * (east[1] - west[1]) + v * (south[1] - north[1]) + (east[0] - west[0])
    carry2 = u * (east[2] - west[2]) + v * (south[2] - north[2]) + (south[0] - north[0])
    diagonal = 1.0 + 4.0 * viscous
    return (
        diagonal * e + quarter * flux - viscous * around[0],
        diagonal * u + quarter * carry1 - coriolis * v - viscous * around[1],
        diagonal * v + quarter * carry2 + coriolis * u - viscous * around[2],
    )


def off_diagonal(own, east, west, north, south):
    _, u, v = own
    around = [east[f] + west[f] + (north[f] + south[f]) for f in range(3)]
    quarter = 0.5 * time_step
    return (
        viscous * around[0] - quarter * ((east[1] - west[1]) + (south[2] - north[2])),
        viscous * around[1] - quarter * (east[0] - west[0]) + coriolis * v,
        viscous * around[2] - quarter * (south[0] - north[0]) - coriolis * u,
    )


def solve_kernel(count, steps_dev, *refs):
    pieces, initial_ref = refs[:count], refs[count]
    side_in, side_initial_in, above, below = refs[count + 1 : count + 5]
    outs = refs[count + 5 : 2 * count + 5]
    state, rhs, ya, yb, hstate, hbefore, hrhs, hya, hyb = refs[2 * count + 5 :]
    fields, rows, _ = initial_ref.shape
    total = count * steps_dev
    me = lax.axis_index("tm")
    lane = lanes()
    step = step_of_lane(lane)
    is_first, is_last = lane == 0, lane == LANES - 1
    after_seam, before_seam = (lane & (GROUP - 1)) == 0, (lane & (GROUP - 1)) == GROUP - 1
    q = 1.0 / SHIFT
    wrap = circulant_alpha * q**total
    wrap = wrap / (1.0 - wrap)
    weights = sweep_weights()
    body = slice(MAIN, MAIN + rows)
    top, bottom = slice(ROW0, MAIN), slice(MAIN + rows, MAIN + rows + HALO)

    k = 0
    for b in range(count):
        for i in range(steps_dev):
            n = steps_dev * (me ^ b) + i
            for f in range(fields):
                at = (i * fields + f) * rows
                state[n + 1, f, body, :] = pieces[b][at : at + rows, :]
                state[n + 1, f, top, :] = above[k : k + HALO, :]
                state[n + 1, f, bottom, :] = below[k : k + HALO, :]
                k += HALO
    for f in range(fields):
        state[0, f, body, :] = initial_ref[f, :, tile_at(me)]
        state[0, f, top, :] = above[k : k + HALO, :]
        state[0, f, bottom, :] = below[k : k + HALO, :]
        k += HALO
    for held, given in ((hstate, side_in), (hbefore, side_initial_in)):
        for f in range(fields):
            held[f, body, :] = given[f, :, :]
            held[f, top, :] = above[k : k + HALO, :]
            held[f, bottom, :] = below[k : k + HALO, :]
            k += HALO

    def around(load, halves):
        own = [load(f, 0) for f in range(fields)]
        north = [load(f, -1) for f in range(fields)]
        south = [load(f, 1) for f in range(fields)]
        east, west = halves(own)
        return own, east, west, north, south

    def main_sides(seam, n):
        def halves(own):
            across = [turn(seam[f], -GROUP * n) for f in range(fields)]
            east = [jnp.where(is_last, across[f], turn(own[f], -1)) for f in range(fields)]
            west = [jnp.where(is_first, across[f], turn(own[f], 1)) for f in range(fields)]
            return east, west

        return halves

    def side_sides(ends):
        def halves(own):
            east = [jnp.where(before_seam, turn(ends[f], -1), turn(own[f], -1)) for f in range(fields)]
            west = [jnp.where(after_seam, turn(ends[f], 1), turn(own[f], 1)) for f in range(fields)]
            return east, west

        return halves

    def seam_of(held, start):
        values = [held[f, pl.ds(start, 8), :] for f in range(fields)]
        return [jnp.where(after_seam, turn(v, 1), turn(v, -1)) for v in values]

    def lane_sums(value):
        reach = 1
        while reach < total:
            value = value + jnp.where(step >= reach, turn(value, GROUP * reach), 0.0)
            reach *= 2
        last = jnp.where(step == total - 1, value, 0.0)
        reach = 1
        while reach < total:
            last = last + turn(last, -GROUP * reach)
            reach *= 2
        return value + wrap * last

    lane_growth = jnp.exp(step.astype(jnp.float32) * math.log(SHIFT))
    blocks = (rows + 2 * HALO) // 8

    @pl.loop(0, blocks)
    def _(t):
        start = ROW0 + 8 * t
        seam = seam_of(hstate, start)
        ends = [jnp.zeros((8, LANES), jnp.float32)] * fields
        sums = [jnp.zeros((8, LANES), jnp.float32)] * fields
        for n in range(total):
            load = lambda f, d: state[n + 1, f, pl.ds(start + d, 8), :]
            parts = around(load, main_sides(seam, n))
            value = full_tendency(*parts)
            for f in range(fields):
                ends[f] = jnp.where(step == n, turn(parts[0][f], GROUP * n), ends[f])
                value_f = (value[f] - state[n, f, pl.ds(start, 8), :]) * SHIFT**n
                rhs[n, f, pl.ds(start, 8), :] = value_f
                sums[f] = sums[f] + value_f
                ya[n, f, pl.ds(start, 8), :] = sums[f]
        extra = [wrap * sums[f] for f in range(fields)]
        for n in range(total):
            for f in range(fields):
                at = (n, f, pl.ds(start, 8), slice(None))
                ya[at] = (weights[0] * q) * (ya[at] + extra[f])
        load = lambda f, d: hstate[f, pl.ds(start + d, 8), :]
        parts = around(load, side_sides(ends))
        value = full_tendency(*parts)
        for f in range(fields):
            before = jnp.where(step == 0, hbefore[f, pl.ds(start, 8), :], turn(parts[0][f], GROUP))
            value_f = (value[f] - before) * lane_growth
            hrhs[f, pl.ds(start, 8), :] = value_f
            hya[f, pl.ds(start, 8), :] = (weights[0] * q) * lane_sums(value_f)

    def sweep(weight, old, hold, new, hnew, final):
        first = MAIN if final else ROW0

        @pl.loop(0, rows // 8 if final else blocks)
        def _(t):
            start = first + 8 * t
            seam = seam_of(hold, start)
            ends = [jnp.zeros((8, LANES), jnp.float32)] * fields
            sums = [jnp.zeros((8, LANES), jnp.float32)] * fields
            for n in range(total):
                load = lambda f, d: old[n, f, pl.ds(start + d, 8), :]
                parts = around(load, main_sides(seam, n))
                value = off_diagonal(*parts)
                for f in range(fields):
                    if not final:
                        ends[f] = jnp.where(step == n, turn(parts[0][f], GROUP * n), ends[f])
                    sums[f] = sums[f] + (value[f] + rhs[n, f, pl.ds(start, 8), :])
                    new[n, f, pl.ds(start, 8), :] = sums[f]
            extra = [wrap * sums[f] for f in range(fields)]
            for n in range(total):
                for f in range(fields):
                    at = (n, f, pl.ds(start, 8), slice(None))
                    value_f = (1.0 - weight) * old[at] + (weight * q) * (new[at] + extra[f])
                    if final:
                        value_f = state[n + 1, f, pl.ds(start, 8), :] - value_f * q**n
                    new[at] = value_f
            if not final:
                load = lambda f, d: hold[f, pl.ds(start + d, 8), :]
                parts = around(load, side_sides(ends))
                value = off_diagonal(*parts)
                for f in range(fields):
                    total_f = lane_sums(value[f] + hrhs[f, pl.ds(start, 8), :])
                    hnew[f, pl.ds(start, 8), :] = (1.0 - weight) * parts[0][f] + (weight * q) * total_f

    buffers = [(ya, hya), (yb, hyb)]
    for m in range(1, SWEEPS):
        (old, hold), (new, hnew) = buffers[(m + 1) % 2], buffers[m % 2]
        sweep(weights[m], old, hold, new, hnew, m == SWEEPS - 1)
    result = buffers[(SWEEPS - 1) % 2][0]
    for b in range(count):
        for i in range(steps_dev):
            n = steps_dev * (me ^ b) + i
            for f in range(fields):
                at = (i * fields + f) * rows
                outs[b][at : at + rows, :] = result[n, f, body, :]


def unpack_kernel(count, *refs):
    pieces, out = refs[:count], refs[count]
    steps_dev, fields, rows, _ = out.shape
    me = lax.axis_index("tm")
    for b in range(count):
        here = tile_at(me ^ b)
        for i in range(steps_dev):
            for f in range(fields):
                at = (i * fields + f) * rows
                out[i, f, :, here] = pieces[b][at : at + rows, :]


def call(kernel, out_shapes, operands, scratch=()):
    whole = pl.BlockSpec(memory_space=pltpu.VMEM)
    shapes = [jax.ShapeDtypeStruct(shape, jnp.float32) for shape in out_shapes]
    moved = 4 * sum(math.prod(x.shape) for x in list(shapes) + list(operands))
    return pl.pallas_call(
        kernel,
        out_shape=shapes,
        in_specs=[whole] * len(operands),
        out_specs=[whole] * len(shapes),
        scratch_shapes=[pltpu.VMEM(shape, jnp.float32) for shape in scratch],
        compiler_params=pltpu.CompilerParams(vmem_limit_bytes=VMEM_BYTES),
        cost_estimate=pl.CostEstimate(flops=moved, bytes_accessed=moved, transcendentals=0),
    )(*operands)


def exchange(pieces):
    count = len(pieces)
    found = list(pieces)
    for b in reversed(range(1, count)):
        found[b] = lax.ppermute(pieces[b], "tm", [(k, k ^ b) for k in range(count)])
    return found


def fast_on_device(state, initial):
    steps_dev, fields, rows, columns = state.shape
    count = lax.axis_size("tm")
    bands = lax.axis_size("space")
    total = steps_dev * count
    main = steps_dev * fields * rows
    words = -(-fields * rows // 8 // count)
    pieces = call(
        functools.partial(pack_kernel, count), [(main + 8 * words, LANES)] * count, [state]
    )
    pieces = exchange(pieces)
    edge_rows = -(-HALO * fields * (total + 3) // 8) * 8
    up, down, side, side_initial = call(
        functools.partial(edge_kernel, count, steps_dev),
        [(edge_rows, LANES)] * 2 + [(fields, rows, LANES)] * 2,
        pieces + [initial],
    )
    above = lax.ppermute(down, "space", [(i, (i + 1) % bands) for i in range(bands)])
    below = lax.ppermute(up, "space", [((i + 1) % bands, i) for i in range(bands)])
    tall = rows + 2 * HALO + 2 * ROW0
    results = call(
        functools.partial(solve_kernel, count, steps_dev),
        [(main, LANES)] * count,
        pieces + [initial, side, side_initial, above, below],
        [(total + 1, fields, tall, LANES)]
        + [(total, fields, tall, LANES)] * 3
        + [(fields, tall, LANES)] * 5,
    )
    results = exchange(results)
    (updated,) = call(functools.partial(unpack_kernel, count), [state.shape], results)
    return updated


def choose(state, initial):
    if fits_fast_plan(state, lax.axis_size("tm")):
        return fast_on_device(state, initial)
    return on_device(state, initial)


def solution(mesh):
    in_specs = (P("tm", None, "space", None), P(None, "space", None))
    out_specs = P("tm", None, "space", None)
    return jax.shard_map(
        choose, mesh=mesh, in_specs=in_specs, out_specs=out_specs, check_vma=False
    )
```

```python
import functools
import math

import jax
import jax.numpy as jnp
from jax import lax
from jax.experimental import pallas as pl
from jax.experimental.pallas import tpu as pltpu
from jax.sharding import PartitionSpec as P

SWEEPS = 4


circulant_alpha = 0.1
time_step = 0.5
coriolis = 0.3
viscous = 0.2
highest = lax.Precision.HIGHEST


def from_behind(block, axis, distance):
    devices = range(lax.axis_size(axis))
    route = [(i - distance, i) for i in devices if i - distance in devices]
    return lax.ppermute(block, axis, route)


def extended(cells, sides, width):
    for axis, dim in sides:
        count = lax.axis_size(axis)
        head = lax.slice_in_dim(cells, 0, width, axis=dim)
        tail = lax.slice_in_dim(cells, cells.shape[dim] - width, cells.shape[dim], axis=dim)
        cells = jnp.concatenate(
            [
                lax.ppermute(tail, axis, [(i, (i + 1) % count) for i in range(count)]),
                cells,
                lax.ppermute(head, axis, [((i + 1) % count, i) for i in range(count)]),
            ],
            axis=dim,
        )
    return cells


def interior(values):
    return values[..., 1:-1, :]


def column_diff(values):
    return 0.5 * (jnp.roll(values, -1, axis=-1) - jnp.roll(values, 1, axis=-1))[..., 1:-1, :]


def row_diff(values):
    return 0.5 * (values[..., 2:, :] - values[..., :-2, :])


def laplace(values):
    return (
        values[..., 2:, :]
        + values[..., :-2, :]
        + jnp.roll(values, -1, axis=-1)[..., 1:-1, :]
        + jnp.roll(values, 1, axis=-1)[..., 1:-1, :]
        - 4.0 * values[..., 1:-1, :]
    )


def tendency(padded):
    surface = padded[..., 0, :, :]
    eastward = padded[..., 1, :, :]
    northward = padded[..., 2, :, :]
    column_depth = 1.0 + surface
    east_inner = interior(eastward)
    north_inner = interior(northward)
    mass_change = time_step * (
        column_diff(column_depth * eastward) + row_diff(column_depth * northward)
    ) - viscous * laplace(surface)
    east_change = (
        time_step
        * (
            east_inner * column_diff(eastward)
            + north_inner * row_diff(eastward)
            + column_diff(surface)
        )
        - coriolis * north_inner
        - viscous * laplace(eastward)
    )
    north_change = (
        time_step
        * (
            east_inner * column_diff(northward)
            + north_inner * row_diff(northward)
            + row_diff(surface)
        )
        + coriolis * east_inner
        - viscous * laplace(northward)
    )
    return jnp.stack([mass_change, east_change, north_change], axis=-3)


def linear_part(padded):
    surface = padded[..., 0, :, :]
    eastward = padded[..., 1, :, :]
    northward = padded[..., 2, :, :]
    mass_change = time_step * (column_diff(eastward) + row_diff(northward)) - viscous * laplace(
        surface
    )
    east_change = (
        time_step * column_diff(surface)
        - coriolis * interior(northward)
        - viscous * laplace(eastward)
    )
    north_change = (
        time_step * row_diff(surface) + coriolis * interior(eastward) - viscous * laplace(northward)
    )
    return jnp.stack([mass_change, east_change, north_change], axis=-3)


def pair_apply(factors, values):
    factor = factors[:, :, None, None, None]
    return jnp.stack(
        [
            factor[0] * values[0] - factor[1] * values[1],
            factor[2] * values[1] + factor[3] * values[0],
        ]
    )


def sweep_weights():
    return [
        1.0 / (1.15 - 0.85 * math.cos(math.pi * (2 * sweep + 1) / (2 * SWEEPS)))
        for sweep in range(SWEEPS)
    ]


def slot_factors(slot_index, total_steps):
    decay_base = circulant_alpha ** (1.0 / total_steps)
    angles = 2.0 * math.pi / total_steps * slot_index.astype(jnp.float32)
    real_eigen = 1.0 - decay_base * jnp.cos(angles)
    imaginary_eigen = decay_base * jnp.sin(angles)
    real_shift = real_eigen + 4.0 * viscous
    modulus = real_shift * real_shift + imaginary_eigen * imaginary_eigen
    eigen = jnp.stack([real_eigen, imaginary_eigen, real_eigen, imaginary_eigen])
    jacobi = jnp.stack(
        [
            real_shift / modulus,
            -imaginary_eigen / modulus,
            real_shift / modulus,
            -imaginary_eigen / modulus,
        ]
    )
    leading = (slot_index == 0)[None, :]
    zero_part = jnp.zeros_like(real_eigen)
    packed_eigen = jnp.stack(
        [zero_part + (1.0 - decay_base), zero_part, zero_part + (1.0 + decay_base), zero_part]
    )
    packed_jacobi = jnp.stack(
        [
            zero_part + 1.0 / (1.0 - decay_base + 4.0 * viscous),
            zero_part,
            zero_part + 1.0 / (1.0 + decay_base + 4.0 * viscous),
            zero_part,
        ]
    )
    eigen = jnp.where(leading, packed_eigen, eigen)
    jacobi = jnp.where(leading, packed_jacobi, jacobi)
    return (eigen, jacobi)


def time_tables(total_steps):
    slot_total = total_steps // 2
    step_ids = jnp.arange(total_steps, dtype=jnp.int32)
    slot_ids = jnp.arange(slot_total, dtype=jnp.int32)
    phase = slot_ids[:, None] * step_ids[None, :] % total_steps
    angles = 2.0 * math.pi / total_steps * phase.astype(jnp.float32)
    decay_base = circulant_alpha ** (1.0 / total_steps)
    growth = decay_base ** step_ids.astype(jnp.float32)
    cosine = jnp.cos(angles)
    sines = jnp.sin(angles)
    forward_real = cosine * growth[None, :]
    forward_imaginary = -sines * growth[None, :]
    inverse_imaginary = -sines
    alternate = 1.0 - 2.0 * (step_ids % 2).astype(jnp.float32)
    leading = (slot_ids == 0)[:, None]
    forward_imaginary = jnp.where(leading, (alternate * growth)[None, :], forward_imaginary)
    inverse_real = jnp.where(leading, 1.0, 2.0 * cosine)
    inverse_imaginary = jnp.where(leading, alternate[None, :], -2.0 * sines)
    forward = jnp.concatenate([forward_real, forward_imaginary], axis=0)
    inverse = jnp.concatenate([inverse_real, inverse_imaginary], axis=0).T
    inverse = inverse * (1.0 / (total_steps * growth))[:, None]
    return (forward, inverse)


def on_device(state, initial):
    steps_dev, fields, band_rows, columns = state.shape
    width_tm = lax.axis_size("tm")
    total_steps = steps_dev * width_tm
    previous = from_behind(state[-1], "tm", 1)
    previous = jnp.where(lax.axis_index("tm") == 0, initial, previous)
    before = jnp.concatenate([previous[None], state[:-1]], axis=0)
    padded = extended(state, (("space", 2),), 1)
    residual = state - before + tendency(padded)
    forward, inverse = time_tables(total_steps)
    slot_total = forward.shape[0] // 2
    per_device = slot_total // width_tm
    spectrum = jnp.einsum(
        "rj,jnc->rnc",
        forward,
        lax.all_to_all(
            residual.reshape(steps_dev, fields, band_rows * columns),
            "tm",
            split_axis=2,
            concat_axis=0,
            tiled=True,
        ),
        precision=highest,
    )
    spectrum = spectrum.reshape(2, slot_total, fields, spectrum.shape[-1])
    banded = lax.all_to_all(spectrum, "tm", split_axis=1, concat_axis=3, tiled=True).reshape(
        2, per_device, fields, band_rows, columns
    )
    slot_index = lax.axis_index("tm") * per_device + jnp.arange(per_device, dtype=jnp.int32)
    eigen, jacobi = slot_factors(slot_index, total_steps)
    weights = sweep_weights()
    iterate = weights[0] * pair_apply(jacobi, banded)
    for sweep in range(1, SWEEPS):
        border = extended(iterate, (("space", 3),), 1)
        applied = pair_apply(eigen, iterate) + linear_part(border)
        iterate = iterate + weights[sweep] * pair_apply(jacobi, banded - applied)
    flat_solution = iterate.reshape(2, per_device, fields, band_rows * columns)
    blocks = lax.all_to_all(flat_solution, "tm", split_axis=3, concat_axis=1, tiled=True)
    merged = blocks.reshape(2 * blocks.shape[1], blocks.shape[2], blocks.shape[3])
    all_steps = jnp.einsum("jr,rnc->jnc", inverse, merged, precision=highest)
    correction = lax.all_to_all(all_steps, "tm", split_axis=0, concat_axis=2, tiled=True)
    return state - correction.reshape(state.shape)


LANES = 128
HALO = SWEEPS
GROUP = 2 * HALO
ROW0 = 8
MAIN = ROW0 + HALO
SHIFT = 1.0 + 4.0 * viscous
VMEM_BYTES = 48 * 1024 * 1024


def fits_fast_plan(state, width_tm):
    steps_dev, fields, band_rows, columns = state.shape
    total_steps = steps_dev * width_tm
    return (
        columns == LANES * width_tm
        and GROUP * total_steps == LANES
        and width_tm & (width_tm - 1) == 0
        and band_rows % 8 == 0
        and fields == 3
    )


def lanes():
    return lax.broadcasted_iota(jnp.int32, (8, LANES), 1)


def step_of_lane(lane):
    return ((lane + HALO) & (LANES - 1)) // GROUP


def turn(values, shift):
    return pltpu.roll(values, shift % LANES, 1)


def tile_at(index):
    return pl.ds(pl.multiple_of(index * LANES, LANES), LANES)


def pack_kernel(count, state_ref, *outs):
    steps_dev, fields, rows, _ = state_ref.shape
    me = lax.axis_index("tm")
    lane = lanes()
    step = step_of_lane(lane)
    blocks = rows // 8
    main = steps_dev * fields * rows
    for b in range(count):
        tile = me ^ b
        here = tile_at(tile)
        after = tile_at((tile + 1) & (count - 1))
        prior = tile_at((tile + count - 1) & (count - 1))
        out = outs[b]
        for i in range(steps_dev):
            for f in range(fields):
                at = (i * fields + f) * rows
                out[at : at + rows, :] = state_ref[i, f, :, here]
        for first in range(0, fields * blocks, count):
            packed = jnp.zeros((8, LANES), jnp.float32)
            for g in range(first, min(first + count, fields * blocks)):
                f, r = divmod(g, blocks)
                for i in range(steps_dev):
                    slot = steps_dev * (g - first) + i
                    sides = jnp.where(
                        lane < LANES // 2,
                        state_ref[i, f, 8 * r : 8 * r + 8, after],
                        state_ref[i, f, 8 * r : 8 * r + 8, prior],
                    )
                    packed = jnp.where(step == slot, turn(sides, GROUP * slot), packed)
            at = main + 8 * (first // count)
            out[at : at + 8, :] = packed


def edge_kernel(count, steps_dev, *refs):
    pieces, initial_ref = refs[:count], refs[count]
    up, down, side, side_initial = refs[count + 1 :]
    fields, rows, _ = initial_ref.shape
    me = lax.axis_index("tm")
    lane = lanes()
    owner = step_of_lane(lane) // steps_dev
    blocks = rows // 8
    main = steps_dev * fields * rows
    here = tile_at(me)
    after = tile_at((me + 1) & (count - 1))
    prior = tile_at((me + count - 1) & (count - 1))
    for g in range(fields * blocks):
        f, r = divmod(g, blocks)
        word, place = divmod(g, count)
        found = jnp.zeros((8, LANES), jnp.float32)
        for b in range(count):
            source = me ^ b
            value = pieces[b][main + 8 * word : main + 8 * word + 8, :]
            shift = (GROUP * steps_dev * (source - place)) & (LANES - 1)
            found = jnp.where(owner == source, pltpu.roll(value, shift, 1), found)
        side[f, 8 * r : 8 * r + 8, :] = found
        side_initial[f, 8 * r : 8 * r + 8, :] = jnp.where(
            lane < LANES // 2,
            initial_ref[f, 8 * r : 8 * r + 8, after],
            initial_ref[f, 8 * r : 8 * r + 8, prior],
        )
    low, high = slice(0, HALO), slice(rows - HALO, rows)
    for out, part in ((up, low), (down, high)):
        k = 0
        for b in range(count):
            for at in range(0, main, rows):
                out[k : k + HALO, :] = pieces[b][at + part.start : at + part.stop, :]
                k += HALO
        for f in range(fields):
            out[k : k + HALO, :] = initial_ref[f, part, here]
            k += HALO
        for f in range(fields):
            out[k : k + HALO, :] = side[f, part, :]
            k += HALO
        for f in range(fields):
            out[k : k + HALO, :] = side_initial[f, part, :]
            k += HALO


def full_tendency(own, east, west, north, south):
    e, u, v = own
    around = [east[f] + west[f] + (north[f] + south[f]) for f in range(3)]
    quarter = 0.5 * time_step
    flux = ((1.0 + east[0]) * east[1] - (1.0 + west[0]) * west[1]) + (
        (1.0 + south[0]) * south[2] - (1.0 + north[0]) * north[2]
    )
    carry1 = u * (east[1] - west[1]) + v * (south[1] - north[1]) + (east[0] - west[0])
    carry2 = u * (east[2] - west[2]) + v * (south[2] - north[2]) + (south[0] - north[0])
    diagonal = 1.0 + 4.0 * viscous
    return (
        diagonal * e + quarter * flux - viscous * around[0],
        diagonal * u + quarter * carry1 - coriolis * v - viscous * around[1],
        diagonal * v + quarter * carry2 + coriolis * u - viscous * around[2],
    )


def off_diagonal(own, east, west, north, south):
    _, u, v = own
    around = [east[f] + west[f] + (north[f] + south[f]) for f in range(3)]
    quarter = 0.5 * time_step
    return (
        viscous * around[0] - quarter * ((east[1] - west[1]) + (south[2] - north[2])),
        viscous * around[1] - quarter * (east[0] - west[0]) + coriolis * v,
        viscous * around[2] - quarter * (south[0] - north[0]) - coriolis * u,
    )


def solve_kernel(count, steps_dev, *refs):
    pieces, initial_ref = refs[:count], refs[count]
    side_in, side_initial_in, above, below = refs[count + 1 : count + 5]
    outs = refs[count + 5 : 2 * count + 5]
    state, rhs, ya, yb, hstate, hbefore, hrhs, hya, hyb, ends, seams = refs[2 * count + 5 :]
    fields, rows, _ = initial_ref.shape
    total = count * steps_dev
    me = lax.axis_index("tm")
    lane = lanes()
    step = step_of_lane(lane)
    is_first, is_last = lane == 0, lane == LANES - 1
    q = 1.0 / SHIFT
    wrap = circulant_alpha * q**total
    wrap = wrap / (1.0 - wrap)
    weights = sweep_weights()
    body = slice(MAIN, MAIN + rows)
    top, bottom = slice(ROW0, MAIN), slice(MAIN + rows, MAIN + rows + HALO)

    k = 0
    for b in range(count):
        for i in range(steps_dev):
            n = steps_dev * (me ^ b) + i
            for f in range(fields):
                at = (i * fields + f) * rows
                state[n + 1, f, body, :] = pieces[b][at : at + rows, :]
                state[n + 1, f, top, :] = above[k : k + HALO, :]
                state[n + 1, f, bottom, :] = below[k : k + HALO, :]
                k += HALO
    for f in range(fields):
        state[0, f, body, :] = initial_ref[f, :, tile_at(me)]
        state[0, f, top, :] = above[k : k + HALO, :]
        state[0, f, bottom, :] = below[k : k + HALO, :]
        k += HALO
    for held, given in ((hstate, side_in), (hbefore, side_initial_in)):
        for f in range(fields):
            held[f, body, :] = given[f, :, :]
            held[f, top, :] = above[k : k + HALO, :]
            held[f, bottom, :] = below[k : k + HALO, :]
            k += HALO

    def around(load, halves):
        own = [load(f, 0) for f in range(fields)]
        north = [load(f, -1) for f in range(fields)]
        south = [load(f, 1) for f in range(fields)]
        east, west = halves(own)
        return own, east, west, north, south

    def main_sides(seam, n):
        def halves(own):
            across = [turn(seam[f], -GROUP * n) for f in range(fields)]
            east = [jnp.where(is_last, across[f], turn(own[f], -1)) for f in range(fields)]
            west = [jnp.where(is_first, across[f], turn(own[f], 1)) for f in range(fields)]
            return east, west

        return halves

    blocks = (rows + 2 * HALO) // 8
    whole = slice(ROW0, ROW0 + 8 * blocks)
    wide = lax.broadcasted_iota(jnp.int32, (8 * blocks, LANES), 1)
    wide_step = step_of_lane(wide)
    wide_after = (wide & (GROUP - 1)) == 0
    wide_before = (wide & (GROUP - 1)) == GROUP - 1
    source = lax.broadcasted_iota(jnp.int32, (LANES, LANES), 0)
    target = lax.broadcasted_iota(jnp.int32, (LANES, LANES), 1)
    same = ((source - target) & (GROUP - 1)) == 0
    running = jnp.where(
        same, jnp.where(step_of_lane(source) <= step_of_lane(target), 1.0 + wrap, wrap), 0.0
    ).astype(jnp.float32)

    def side_parts(held):
        own, north, south = (
            [held[f, ROW0 + d : ROW0 + d + 8 * blocks, :] for f in range(fields)] for d in (0, -1, 1)
        )
        last = [ends[f, whole, :] for f in range(fields)]
        east = [jnp.where(wide_before, turn(last[f], -1), turn(own[f], -1)) for f in range(fields)]
        west = [jnp.where(wide_after, turn(last[f], 1), turn(own[f], 1)) for f in range(fields)]
        return own, east, west, north, south

    def running_sums(values):
        tall_sums = jnp.dot(
            jnp.concatenate(values, axis=0),
            running,
            precision=highest,
            preferred_element_type=jnp.float32,
        )
        return [tall_sums[8 * blocks * f : 8 * blocks * (f + 1), :] for f in range(fields)]

    def set_seam(values):
        for f in range(fields):
            seams[f, whole, :] = jnp.where(wide_after, turn(values[f], 1), turn(values[f], -1))

    set_seam([hstate[f, whole, :] for f in range(fields)])

    @pl.loop(0, blocks)
    def _(t):
        start = ROW0 + 8 * t
        seam = [seams[f, pl.ds(start, 8), :] for f in range(fields)]
        last = [jnp.zeros((8, LANES), jnp.float32)] * fields
        sums = [jnp.zeros((8, LANES), jnp.float32)] * fields
        for n in range(total):
            load = lambda f, d: state[n + 1, f, pl.ds(start + d, 8), :]
            parts = around(load, main_sides(seam, n))
            value = full_tendency(*parts)
            for f in range(fields):
                last[f] = jnp.where(step == n, turn(parts[0][f], GROUP * n), last[f])
                value_f = (value[f] - state[n, f, pl.ds(start, 8), :]) * SHIFT**n
                rhs[n, f, pl.ds(start, 8), :] = value_f
                sums[f] = sums[f] + value_f
                ya[n, f, pl.ds(start, 8), :] = sums[f]
        for f in range(fields):
            ends[f, pl.ds(start, 8), :] = last[f]
        extra = [wrap * sums[f] for f in range(fields)]
        for n in range(total):
            for f in range(fields):
                at = (n, f, pl.ds(start, 8), slice(None))
                ya[at] = (weights[0] * q) * (ya[at] + extra[f])

    parts = side_parts(hstate)
    value = full_tendency(*parts)
    lane_growth = jnp.exp(wide_step.astype(jnp.float32) * math.log(SHIFT))
    side_rhs = []
    for f in range(fields):
        before = jnp.where(wide_step == 0, hbefore[f, whole, :], turn(parts[0][f], GROUP))
        side_rhs.append((value[f] - before) * lane_growth)
        hrhs[f, whole, :] = side_rhs[f]
    side_new = [(weights[0] * q) * x for x in running_sums(side_rhs)]
    for f in range(fields):
        hya[f, whole, :] = side_new[f]
    set_seam(side_new)

    def sweep(weight, old, hold, new, hnew, final):
        first = MAIN if final else ROW0

        @pl.loop(0, rows // 8 if final else blocks)
        def _(t):
            start = first + 8 * t
            seam = [seams[f, pl.ds(start, 8), :] for f in range(fields)]
            last = [jnp.zeros((8, LANES), jnp.float32)] * fields
            sums = [jnp.zeros((8, LANES), jnp.float32)] * fields
            for n in range(total):
                load = lambda f, d: old[n, f, pl.ds(start + d, 8), :]
                parts = around(load, main_sides(seam, n))
                value = off_diagonal(*parts)
                for f in range(fields):
                    if not final:
                        last[f] = jnp.where(step == n, turn(parts[0][f], GROUP * n), last[f])
                    sums[f] = sums[f] + (value[f] + rhs[n, f, pl.ds(start, 8), :])
                    new[n, f, pl.ds(start, 8), :] = sums[f]
            if not final:
                for f in range(fields):
                    ends[f, pl.ds(start, 8), :] = last[f]
            extra = [wrap * sums[f] for f in range(fields)]
            for n in range(total):
                for f in range(fields):
                    at = (n, f, pl.ds(start, 8), slice(None))
                    value_f = (1.0 - weight) * old[at] + (weight * q) * (new[at] + extra[f])
                    if final:
                        value_f = state[n + 1, f, pl.ds(start, 8), :] - value_f * q**n
                    new[at] = value_f

        if not final:
            parts = side_parts(hold)
            value = off_diagonal(*parts)
            total_sums = running_sums([value[f] + hrhs[f, whole, :] for f in range(fields)])
            side_next = [
                (1.0 - weight) * parts[0][f] + (weight * q) * total_sums[f] for f in range(fields)
            ]
            for f in range(fields):
                hnew[f, whole, :] = side_next[f]
            set_seam(side_next)

    buffers = [(ya, hya), (yb, hyb)]
    for m in range(1, SWEEPS):
        (old, hold), (new, hnew) = buffers[(m + 1) % 2], buffers[m % 2]
        sweep(weights[m], old, hold, new, hnew, m == SWEEPS - 1)
    result = buffers[(SWEEPS - 1) % 2][0]
    for b in range(count):
        for i in range(steps_dev):
            n = steps_dev * (me ^ b) + i
            for f in range(fields):
                at = (i * fields + f) * rows
                outs[b][at : at + rows, :] = result[n, f, body, :]


def unpack_kernel(count, *refs):
    pieces, out = refs[:count], refs[count]
    steps_dev, fields, rows, _ = out.shape
    me = lax.axis_index("tm")
    for b in range(count):
        here = tile_at(me ^ b)
        for i in range(steps_dev):
            for f in range(fields):
                at = (i * fields + f) * rows
                out[i, f, :, here] = pieces[b][at : at + rows, :]


def call(kernel, out_shapes, operands, scratch=()):
    whole = pl.BlockSpec(memory_space=pltpu.VMEM)
    shapes = [jax.ShapeDtypeStruct(shape, jnp.float32) for shape in out_shapes]
    moved = 4 * sum(math.prod(x.shape) for x in list(shapes) + list(operands))
    return pl.pallas_call(
        kernel,
        out_shape=shapes,
        in_specs=[whole] * len(operands),
        out_specs=[whole] * len(shapes),
        scratch_shapes=[pltpu.VMEM(shape, jnp.float32) for shape in scratch],
        compiler_params=pltpu.CompilerParams(vmem_limit_bytes=VMEM_BYTES),
        cost_estimate=pl.CostEstimate(flops=moved, bytes_accessed=moved, transcendentals=0),
    )(*operands)


def exchange(pieces):
    count = len(pieces)
    found = list(pieces)
    for b in reversed(range(1, count)):
        found[b] = lax.ppermute(pieces[b], "tm", [(k, k ^ b) for k in range(count)])
    return found


def fast_on_device(state, initial):
    steps_dev, fields, rows, columns = state.shape
    count = lax.axis_size("tm")
    bands = lax.axis_size("space")
    total = steps_dev * count
    main = steps_dev * fields * rows
    words = -(-fields * rows // 8 // count)
    pieces = call(
        functools.partial(pack_kernel, count), [(main + 8 * words, LANES)] * count, [state]
    )
    pieces = exchange(pieces)
    edge_rows = -(-HALO * fields * (total + 3) // 8) * 8
    up, down, side, side_initial = call(
        functools.partial(edge_kernel, count, steps_dev),
        [(edge_rows, LANES)] * 2 + [(fields, rows, LANES)] * 2,
        pieces + [initial],
    )
    above = lax.ppermute(down, "space", [(i, (i + 1) % bands) for i in range(bands)])
    below = lax.ppermute(up, "space", [((i + 1) % bands, i) for i in range(bands)])
    tall = rows + 2 * HALO + 2 * ROW0
    results = call(
        functools.partial(solve_kernel, count, steps_dev),
        [(main, LANES)] * count,
        pieces + [initial, side, side_initial, above, below],
        [(total + 1, fields, tall, LANES)]
        + [(total, fields, tall, LANES)] * 3
        + [(fields, tall, LANES)] * 7,
    )
    results = exchange(results)
    (updated,) = call(functools.partial(unpack_kernel, count), [state.shape], results)
    return updated


def choose(state, initial):
    if fits_fast_plan(state, lax.axis_size("tm")):
        return fast_on_device(state, initial)
    return on_device(state, initial)


def solution(mesh):
    in_specs = (P("tm", None, "space", None), P(None, "space", None))
    out_specs = P("tm", None, "space", None)
    return jax.shard_map(
        choose, mesh=mesh, in_specs=in_specs, out_specs=out_specs, check_vma=False
    )
```

```python
import functools
import math

import jax
import jax.numpy as jnp
from jax import lax
from jax.experimental import pallas as pl
from jax.experimental.pallas import tpu as pltpu
from jax.sharding import PartitionSpec as P

SWEEPS = 4


circulant_alpha = 0.1
time_step = 0.5
coriolis = 0.3
viscous = 0.2
highest = lax.Precision.HIGHEST


def from_behind(block, axis, distance):
    devices = range(lax.axis_size(axis))
    route = [(i - distance, i) for i in devices if i - distance in devices]
    return lax.ppermute(block, axis, route)


def extended(cells, sides, width):
    for axis, dim in sides:
        count = lax.axis_size(axis)
        head = lax.slice_in_dim(cells, 0, width, axis=dim)
        tail = lax.slice_in_dim(cells, cells.shape[dim] - width, cells.shape[dim], axis=dim)
        cells = jnp.concatenate(
            [
                lax.ppermute(tail, axis, [(i, (i + 1) % count) for i in range(count)]),
                cells,
                lax.ppermute(head, axis, [((i + 1) % count, i) for i in range(count)]),
            ],
            axis=dim,
        )
    return cells


def interior(values):
    return values[..., 1:-1, :]


def column_diff(values):
    return 0.5 * (jnp.roll(values, -1, axis=-1) - jnp.roll(values, 1, axis=-1))[..., 1:-1, :]


def row_diff(values):
    return 0.5 * (values[..., 2:, :] - values[..., :-2, :])


def laplace(values):
    return (
        values[..., 2:, :]
        + values[..., :-2, :]
        + jnp.roll(values, -1, axis=-1)[..., 1:-1, :]
        + jnp.roll(values, 1, axis=-1)[..., 1:-1, :]
        - 4.0 * values[..., 1:-1, :]
    )


def tendency(padded):
    surface = padded[..., 0, :, :]
    eastward = padded[..., 1, :, :]
    northward = padded[..., 2, :, :]
    column_depth = 1.0 + surface
    east_inner = interior(eastward)
    north_inner = interior(northward)
    mass_change = time_step * (
        column_diff(column_depth * eastward) + row_diff(column_depth * northward)
    ) - viscous * laplace(surface)
    east_change = (
        time_step
        * (
            east_inner * column_diff(eastward)
            + north_inner * row_diff(eastward)
            + column_diff(surface)
        )
        - coriolis * north_inner
        - viscous * laplace(eastward)
    )
    north_change = (
        time_step
        * (
            east_inner * column_diff(northward)
            + north_inner * row_diff(northward)
            + row_diff(surface)
        )
        + coriolis * east_inner
        - viscous * laplace(northward)
    )
    return jnp.stack([mass_change, east_change, north_change], axis=-3)


def linear_part(padded):
    surface = padded[..., 0, :, :]
    eastward = padded[..., 1, :, :]
    northward = padded[..., 2, :, :]
    mass_change = time_step * (column_diff(eastward) + row_diff(northward)) - viscous * laplace(
        surface
    )
    east_change = (
        time_step * column_diff(surface)
        - coriolis * interior(northward)
        - viscous * laplace(eastward)
    )
    north_change = (
        time_step * row_diff(surface) + coriolis * interior(eastward) - viscous * laplace(northward)
    )
    return jnp.stack([mass_change, east_change, north_change], axis=-3)


def pair_apply(factors, values):
    factor = factors[:, :, None, None, None]
    return jnp.stack(
        [
            factor[0] * values[0] - factor[1] * values[1],
            factor[2] * values[1] + factor[3] * values[0],
        ]
    )


def sweep_weights():
    return [
        1.0 / (1.15 - 0.85 * math.cos(math.pi * (2 * sweep + 1) / (2 * SWEEPS)))
        for sweep in range(SWEEPS)
    ]


def slot_factors(slot_index, total_steps):
    decay_base = circulant_alpha ** (1.0 / total_steps)
    angles = 2.0 * math.pi / total_steps * slot_index.astype(jnp.float32)
    real_eigen = 1.0 - decay_base * jnp.cos(angles)
    imaginary_eigen = decay_base * jnp.sin(angles)
    real_shift = real_eigen + 4.0 * viscous
    modulus = real_shift * real_shift + imaginary_eigen * imaginary_eigen
    eigen = jnp.stack([real_eigen, imaginary_eigen, real_eigen, imaginary_eigen])
    jacobi = jnp.stack(
        [
            real_shift / modulus,
            -imaginary_eigen / modulus,
            real_shift / modulus,
            -imaginary_eigen / modulus,
        ]
    )
    leading = (slot_index == 0)[None, :]
    zero_part = jnp.zeros_like(real_eigen)
    packed_eigen = jnp.stack(
        [zero_part + (1.0 - decay_base), zero_part, zero_part + (1.0 + decay_base), zero_part]
    )
    packed_jacobi = jnp.stack(
        [
            zero_part + 1.0 / (1.0 - decay_base + 4.0 * viscous),
            zero_part,
            zero_part + 1.0 / (1.0 + decay_base + 4.0 * viscous),
            zero_part,
        ]
    )
    eigen = jnp.where(leading, packed_eigen, eigen)
    jacobi = jnp.where(leading, packed_jacobi, jacobi)
    return (eigen, jacobi)


def time_tables(total_steps):
    slot_total = total_steps // 2
    step_ids = jnp.arange(total_steps, dtype=jnp.int32)
    slot_ids = jnp.arange(slot_total, dtype=jnp.int32)
    phase = slot_ids[:, None] * step_ids[None, :] % total_steps
    angles = 2.0 * math.pi / total_steps * phase.astype(jnp.float32)
    decay_base = circulant_alpha ** (1.0 / total_steps)
    growth = decay_base ** step_ids.astype(jnp.float32)
    cosine = jnp.cos(angles)
    sines = jnp.sin(angles)
    forward_real = cosine * growth[None, :]
    forward_imaginary = -sines * growth[None, :]
    inverse_imaginary = -sines
    alternate = 1.0 - 2.0 * (step_ids % 2).astype(jnp.float32)
    leading = (slot_ids == 0)[:, None]
    forward_imaginary = jnp.where(leading, (alternate * growth)[None, :], forward_imaginary)
    inverse_real = jnp.where(leading, 1.0, 2.0 * cosine)
    inverse_imaginary = jnp.where(leading, alternate[None, :], -2.0 * sines)
    forward = jnp.concatenate([forward_real, forward_imaginary], axis=0)
    inverse = jnp.concatenate([inverse_real, inverse_imaginary], axis=0).T
    inverse = inverse * (1.0 / (total_steps * growth))[:, None]
    return (forward, inverse)


def on_device(state, initial):
    steps_dev, fields, band_rows, columns = state.shape
    width_tm = lax.axis_size("tm")
    total_steps = steps_dev * width_tm
    previous = from_behind(state[-1], "tm", 1)
    previous = jnp.where(lax.axis_index("tm") == 0, initial, previous)
    before = jnp.concatenate([previous[None], state[:-1]], axis=0)
    padded = extended(state, (("space", 2),), 1)
    residual = state - before + tendency(padded)
    forward, inverse = time_tables(total_steps)
    slot_total = forward.shape[0] // 2
    per_device = slot_total // width_tm
    spectrum = jnp.einsum(
        "rj,jnc->rnc",
        forward,
        lax.all_to_all(
            residual.reshape(steps_dev, fields, band_rows * columns),
            "tm",
            split_axis=2,
            concat_axis=0,
            tiled=True,
        ),
        precision=highest,
    )
    spectrum = spectrum.reshape(2, slot_total, fields, spectrum.shape[-1])
    banded = lax.all_to_all(spectrum, "tm", split_axis=1, concat_axis=3, tiled=True).reshape(
        2, per_device, fields, band_rows, columns
    )
    slot_index = lax.axis_index("tm") * per_device + jnp.arange(per_device, dtype=jnp.int32)
    eigen, jacobi = slot_factors(slot_index, total_steps)
    weights = sweep_weights()
    iterate = weights[0] * pair_apply(jacobi, banded)
    for sweep in range(1, SWEEPS):
        border = extended(iterate, (("space", 3),), 1)
        applied = pair_apply(eigen, iterate) + linear_part(border)
        iterate = iterate + weights[sweep] * pair_apply(jacobi, banded - applied)
    flat_solution = iterate.reshape(2, per_device, fields, band_rows * columns)
    blocks = lax.all_to_all(flat_solution, "tm", split_axis=3, concat_axis=1, tiled=True)
    merged = blocks.reshape(2 * blocks.shape[1], blocks.shape[2], blocks.shape[3])
    all_steps = jnp.einsum("jr,rnc->jnc", inverse, merged, precision=highest)
    correction = lax.all_to_all(all_steps, "tm", split_axis=0, concat_axis=2, tiled=True)
    return state - correction.reshape(state.shape)


LANES = 128
HALO = SWEEPS
GROUP = 2 * HALO
ROW0 = 8
MAIN = ROW0 + HALO
SHIFT = 1.0 + 4.0 * viscous
RATE = 1.0 / SHIFT
VMEM_BYTES = 48 * 1024 * 1024
SLABS = 2
FIELDS = 3
EACH = [(f, c) for f in range(FIELDS) for c in range(SLABS)]


def fits_fast_plan(state, width_tm):
    steps_dev, fields, band_rows, columns = state.shape
    half = width_tm // 2
    steps = steps_dev * half
    return (
        width_tm > 1
        and width_tm & (width_tm - 1) == 0
        and columns == SLABS * LANES * half
        and SWEEPS * GROUP <= GROUP * steps <= LANES
        and LANES % (GROUP * steps_dev) == 0
        and band_rows % 8 == 0
        and band_rows >= 16
        and fields == FIELDS
    )


def lanes(rows=8):
    return lax.broadcasted_iota(jnp.int32, (rows, LANES), 1)


def step_of_lane(lane):
    return ((lane + HALO) & (LANES - 1)) // GROUP


def turn(values, shift):
    return pltpu.roll(values, shift % LANES, 1)


def tile_at(index):
    return pl.ds(pl.multiple_of(index * LANES, LANES), LANES)


def binomial(top, bottom):
    return float(math.comb(top, bottom))


def side_places(tile, width_tm):
    last = width_tm // 2 * SLABS - 1
    return tile_at((SLABS * tile + SLABS) & last), tile_at((SLABS * tile + last) & last)


def pack_kernel(width_tm, state_ref, *outs):
    steps_dev, fields, rows, _ = state_ref.shape
    half = width_tm // 2
    me = lax.axis_index("tm")
    lane = lanes()
    step = step_of_lane(lane)
    blocks = rows // 8
    per_word = LANES // (GROUP * steps_dev)
    for b, out in enumerate(outs):
        tile = (me ^ b) & (half - 1)
        after, prior = side_places(tile, width_tm)
        at = 0
        for c in range(SLABS):
            for i in range(steps_dev):
                for f in range(fields):
                    out[at : at + rows, :] = state_ref[i, f, :, tile_at(SLABS * tile + c)]
                    at += rows
        for first in range(0, fields * blocks, per_word):
            packed = jnp.zeros((8, LANES), jnp.float32)
            for g in range(first, min(first + per_word, fields * blocks)):
                f, r = divmod(g, blocks)
                for i in range(steps_dev):
                    slot = steps_dev * (g - first) + i
                    sides = jnp.where(
                        lane < LANES // 2,
                        state_ref[i, f, 8 * r : 8 * r + 8, after],
                        state_ref[i, f, 8 * r : 8 * r + 8, prior],
                    )
                    packed = jnp.where(step == slot, turn(sides, GROUP * slot), packed)
            out[at : at + 8, :] = packed
            at += 8


def edge_kernel(width_tm, steps_dev, *refs):
    half = width_tm // 2
    pieces, initial_ref = refs[:half], refs[half]
    up, down, side, side_initial = refs[half + 1 :]
    fields, rows, _ = initial_ref.shape
    me = lax.axis_index("tm")
    mine = me & (half - 1)
    lane = lanes()
    owner = step_of_lane(lane) // steps_dev
    blocks = rows // 8
    per_word = LANES // (GROUP * steps_dev)
    main = SLABS * steps_dev * fields * rows
    after, prior = side_places(mine, width_tm)
    for g in range(fields * blocks):
        f, r = divmod(g, blocks)
        word, place = divmod(g, per_word)
        found = jnp.zeros((8, LANES), jnp.float32)
        for b in range(half):
            source = mine ^ b
            value = pieces[b][main + 8 * word : main + 8 * word + 8, :]
            shift = (GROUP * steps_dev * (source - place)) & (LANES - 1)
            found = jnp.where(owner == source, pltpu.roll(value, shift, 1), found)
        side[f, 8 * r : 8 * r + 8, :] = found
        side_initial[f, 8 * r : 8 * r + 8, :] = jnp.where(
            lane < LANES // 2,
            initial_ref[f, 8 * r : 8 * r + 8, after],
            initial_ref[f, 8 * r : 8 * r + 8, prior],
        )
    for out, part in ((up, slice(0, HALO)), (down, slice(rows - HALO, rows))):
        k = 0
        for b in range(half):
            for at in range(0, main, rows):
                out[k : k + HALO, :] = pieces[b][at + part.start : at + part.stop, :]
                k += HALO
        for c in range(SLABS):
            for f in range(fields):
                out[k : k + HALO, :] = initial_ref[f, part, tile_at(SLABS * mine + c)]
                k += HALO
        for held in (side, side_initial):
            for f in range(fields):
                out[k : k + HALO, :] = held[f, part, :]
                k += HALO


def full_tendency(own, east, west, north, south):
    e, u, v = own
    around = [east[f] + west[f] + (north[f] + south[f]) for f in range(FIELDS)]
    quarter = 0.5 * time_step
    flux = ((1.0 + east[0]) * east[1] - (1.0 + west[0]) * west[1]) + (
        (1.0 + south[0]) * south[2] - (1.0 + north[0]) * north[2]
    )
    carry1 = u * (east[1] - west[1]) + v * (south[1] - north[1]) + (east[0] - west[0])
    carry2 = u * (east[2] - west[2]) + v * (south[2] - north[2]) + (south[0] - north[0])
    diagonal = 1.0 + 4.0 * viscous
    return (
        diagonal * e + quarter * flux - viscous * around[0],
        diagonal * u + quarter * carry1 - coriolis * v - viscous * around[1],
        diagonal * v + quarter * carry2 + coriolis * u - viscous * around[2],
    )


def off_diagonal(own, east, west, north, south):
    _, u, v = own
    around = [east[f] + west[f] + (north[f] + south[f]) for f in range(FIELDS)]
    quarter = 0.5 * time_step
    return (
        viscous * around[0] - quarter * ((east[1] - west[1]) + (south[2] - north[2])),
        viscous * around[1] - quarter * (east[0] - west[0]) + coriolis * v,
        viscous * around[2] - quarter * (south[0] - north[0]) - coriolis * u,
    )


def chain_factors():
    gammas = []
    for weight in sweep_weights():
        shifted = [1.0] + gammas
        gammas = [weight * x for x in shifted]
        for i, x in enumerate(shifted[1:]):
            gammas[i] += (1.0 - weight) * x
    scale = RATE * gammas[-1]
    ratios = []
    for gamma in reversed(gammas[:-1]):
        ratios.append(gamma / scale)
        scale *= RATE
    return gammas, ratios, scale


def series_product(a, b):
    return [sum(a[i] * b[d - i] for i in range(d + 1)) for d in range(SWEEPS)]


def swap_factors(steps):
    hop = [RATE ** (steps + d) * binomial(steps - 1 + d, d) for d in range(SWEEPS)]
    lap = [circulant_alpha * x for x in series_product(hop, hop)]
    inverse = []
    for d in range(SWEEPS):
        value = (1.0 if d == 0 else 0.0) + sum(lap[i] * inverse[d - i] for i in range(1, d + 1))
        inverse.append(value / (1.0 - lap[0]))
    own = [circulant_alpha * x for x in series_product(inverse, hop)]
    return own, [circulant_alpha * x for x in inverse], inverse


class Side:
    def __init__(self, rows):
        self.tall = rows + 2 * HALO
        self.span = slice(ROW0, ROW0 + self.tall)
        lane = lanes(self.tall)
        self.step = step_of_lane(lane)
        self.after = (lane & (GROUP - 1)) == 0
        self.before = (lane & (GROUP - 1)) == GROUP - 1

    def parts(self, held, ends):
        own, north, south = (
            [held[f, ROW0 + d : ROW0 + d + self.tall, :] for f in range(FIELDS)] for d in (0, -1, 1)
        )
        last = [ends[f, self.span, :] for f in range(FIELDS)]
        east = [jnp.where(self.before, turn(last[f], -1), turn(own[f], -1)) for f in range(FIELDS)]
        west = [jnp.where(self.after, turn(last[f], 1), turn(own[f], 1)) for f in range(FIELDS)]
        return own, east, west, north, south

    def set_seams(self, seams, values):
        for f in range(FIELDS):
            seams[f, self.span, :] = jnp.where(self.after, turn(values[f], 1), turn(values[f], -1))

    def product(self, values, matrix):
        done = jnp.dot(
            jnp.concatenate(values, axis=0),
            matrix,
            precision=highest,
            preferred_element_type=jnp.float32,
        )
        return [done[self.tall * f : self.tall * (f + 1), :] for f in range(FIELDS)]


def lane_matrix(entry):
    source = lax.broadcasted_iota(jnp.int32, (LANES, LANES), 0)
    target = lax.broadcasted_iota(jnp.int32, (LANES, LANES), 1)
    same = ((source - target) & (GROUP - 1)) == 0
    return jnp.where(same, entry(step_of_lane(source), step_of_lane(target)), 0.0)


def step_parts(held, n, start, seam):
    lane = lanes()
    load = lambda d: {k: held[n, k[0], k[1], pl.ds(start + d, 8), :] for k in EACH}
    own, north, south = load(0), load(-1), load(1)
    east, west = {}, {}
    return own, east, west, north, south, lane


def neighbours(held, slot, start, seam, n):
    lane = lanes()
    is_first, is_last = lane == 0, lane == LANES - 1
    load = lambda d: {k: held[slot, k[0], k[1], pl.ds(start + d, 8), :] for k in EACH}
    own, north, south = load(0), load(-1), load(1)
    east, west = {}, {}
    for f in range(FIELDS):
        across = turn(seam[f], -GROUP * n)
        back = [turn(own[f, c], -1) for c in range(SLABS)] + [across]
        ahead = [across] + [turn(own[f, c], 1) for c in range(SLABS)]
        for c in range(SLABS):
            east[f, c] = jnp.where(is_last, back[c + 1], back[c])
            west[f, c] = jnp.where(is_first, ahead[c], ahead[c + 1])
    return own, east, west, north, south


def slab(parts, c):
    return [[part[f, c] for f in range(FIELDS)] for part in parts]


def add_ends(last, own, n):
    lane = lanes()
    step = step_of_lane(lane)
    for f in range(FIELDS):
        both = jnp.where(lane < LANES // 2, own[f, 0], own[f, SLABS - 1])
        last[f] = jnp.where(step == n, turn(both, GROUP * n), last[f])


def zeros(count):
    return [jnp.zeros((8, LANES), jnp.float32)] * count


def residual_tile(steps, first_half, start, state, rhs, seams, ends, send):
    seam = [seams[f, pl.ds(start, 8), :] for f in range(FIELDS)]
    last = zeros(FIELDS)
    sums = {k: zeros(SWEEPS) for k in EACH}
    for n in range(steps):
        parts = neighbours(state, n + 1, start, seam, n)
        add_ends(last, parts[0], n)
        for c in range(SLABS):
            value = full_tendency(*slab(parts, c))
            for f in range(FIELDS):
                carry = (value[f] - state[n, f, c, pl.ds(start, 8), :]) * SHIFT**n
                rhs[n, f, c, pl.ds(start, 8), :] = carry
                for j in range(SWEEPS):
                    carry = sums[f, c][j] + carry
                    sums[f, c][j] = carry
    for f in range(FIELDS):
        ends[f, pl.ds(start, 8), :] = last[f]
    for f, c in EACH:
        for j in range(SWEEPS):
            value = sums[f, c][j] * RATE ** (steps + j)
            if j == 0:
                value = value - jnp.where(first_half, state[steps, f, c, pl.ds(start, 8), :], 0.0)
            send(SWEEPS - 1 - j, f, c, value)


def inner_kernel(width_tm, steps_dev, *refs):
    half = width_tm // 2
    pieces, (initial_ref, side) = refs[:half], refs[half : half + 2]
    state, rhs, ends, sent, seams = refs[half + 2 :]
    fields, rows, _ = initial_ref.shape
    steps = half * steps_dev
    me = lax.axis_index("tm")
    mine = me & (half - 1)
    first_half = me < half
    body = slice(MAIN, MAIN + rows)
    for b in range(half):
        at = 0
        for c in range(SLABS):
            for i in range(steps_dev):
                n = steps_dev * (mine ^ b) + i
                for f in range(fields):
                    state[n + 1, f, c, body, :] = pieces[b][at : at + rows, :]
                    at += rows
    for f, c in EACH:
        state[0, f, c, body, :] = jnp.where(first_half, initial_ref[f, :, tile_at(SLABS * mine + c)], 0.0)
    lane = lanes(rows)
    after = (lane & (GROUP - 1)) == 0
    for f in range(fields):
        seams[f, body, :] = jnp.where(after, turn(side[f], 1), turn(side[f], -1))

    @pl.loop(1, rows // 8)
    def _(t):
        def send(p, f, c, value):
            sent[p, f, c, pl.ds(pl.multiple_of(8 * t - 8, 8), 8), :] = value

        residual_tile(steps, first_half, ROW0 + 8 * t, state, rhs, seams, ends, send)


def outer_kernel(width_tm, steps_dev, rows, *refs):
    half = width_tm // 2
    side, side_initial, above, below = refs[3:7]
    state, rhs, ends, hrhs, sent, hstate, hbefore, seams = refs[7:]
    steps = half * steps_dev
    me = lax.axis_index("tm")
    mine = me & (half - 1)
    first_half = me < half
    body = slice(MAIN, MAIN + rows)
    top, bottom = slice(ROW0, MAIN), slice(MAIN + rows, MAIN + rows + HALO)
    k = 0
    for b in range(half):
        for c in range(SLABS):
            for i in range(steps_dev):
                n = steps_dev * (mine ^ b) + i
                for f in range(FIELDS):
                    state[n + 1, f, c, top, :] = above[k : k + HALO, :]
                    state[n + 1, f, c, bottom, :] = below[k : k + HALO, :]
                    k += HALO
    for c in range(SLABS):
        for f in range(FIELDS):
            state[0, f, c, top, :] = jnp.where(first_half, above[k : k + HALO, :], 0.0)
            state[0, f, c, bottom, :] = jnp.where(first_half, below[k : k + HALO, :], 0.0)
            k += HALO
    for held, given in ((hstate, side), (hbefore, side_initial)):
        for f in range(FIELDS):
            held[f, body, :] = given[f, :, :]
            held[f, top, :] = above[k : k + HALO, :]
            held[f, bottom, :] = below[k : k + HALO, :]
            k += HALO
    sides = Side(rows)
    sides.set_seams(seams, [hstate[f, sides.span, :] for f in range(FIELDS)])
    main = SWEEPS * FIELDS * SLABS * 16
    for which, start in enumerate((ROW0, ROW0 + rows)):

        def send(p, f, c, value):
            at = ((p * FIELDS + f) * SLABS + c) * 16 + 8 * which
            sent[at : at + 8, :] = value

        residual_tile(steps, first_half, start, state, rhs, seams, ends, send)
    parts = sides.parts(hstate, ends)
    value = full_tendency(*parts)
    growth = jnp.where(
        sides.step < steps, jnp.exp(sides.step.astype(jnp.float32) * math.log(SHIFT)), 0.0
    )
    held = []
    for f in range(FIELDS):
        first = jnp.where(first_half, hbefore[f, sides.span, :], 0.0)
        before = jnp.where(sides.step == 0, first, turn(parts[0][f], GROUP))
        held.append((value[f] - before) * growth)
        hrhs[f, sides.span, :] = held[f]

    def entry(source, target):
        result = jnp.zeros((LANES, LANES), jnp.float32)
        for p in range(SWEEPS):
            j = SWEEPS - p
            for n in range(steps):
                weight = RATE ** (steps - 1 + j) * binomial(steps - 1 - n + j - 1, j - 1)
                result = jnp.where((target == p) & (source == n), weight, result)
        return result

    handed = sides.product(held, lane_matrix(entry))
    for f in range(FIELDS):
        last = turn(parts[0][f], GROUP * (SWEEPS - steps))
        last = jnp.where(first_half & (sides.step == SWEEPS - 1), last, 0.0)
        sent[main + sides.tall * f : main + sides.tall * (f + 1), :] = handed[f] - last


def chain_kernel(steps, rows, rhs, hrhs, result, ya, yb, hya, hyb, ends, seams):
    _, ratios, _ = chain_factors()
    sides = Side(rows)
    blocks = sides.tall // 8
    running = lane_matrix(
        lambda source, target: jnp.where((source <= target) & (target < steps), 1.0, 0.0)
    )
    side_new = sides.product([hrhs[f, sides.span, :] for f in range(FIELDS)], running)
    for f in range(FIELDS):
        hya[f, sides.span, :] = side_new[f]
    sides.set_seams(seams, side_new)

    @pl.loop(0, blocks)
    def _(t):
        start = ROW0 + 8 * t
        for f, c in EACH:
            total = jnp.zeros((8, LANES), jnp.float32)
            for n in range(steps):
                total = total + rhs[n, f, c, pl.ds(start, 8), :]
                ya[n, f, c, pl.ds(start, 8), :] = total

    def sweep(ratio, old, hold, new, hnew, final):
        first = MAIN if final else ROW0

        @pl.loop(0, rows // 8 if final else blocks)
        def _(t):
            start = first + 8 * t
            seam = [seams[f, pl.ds(start, 8), :] for f in range(FIELDS)]
            last = zeros(FIELDS)
            total = dict(zip(EACH, zeros(len(EACH))))
            for n in range(steps):
                parts = neighbours(old, n, start, seam, n)
                if not final:
                    add_ends(last, parts[0], n)
                for c in range(SLABS):
                    value = off_diagonal(*slab(parts, c))
                    for f in range(FIELDS):
                        carry = value[f] + ratio * rhs[n, f, c, pl.ds(start, 8), :]
                        total[f, c] = total[f, c] + carry
                        if final:
                            at = pl.ds(pl.multiple_of(8 * t, 8), 8)
                            new[n, f, c, at, :] = total[f, c]
                        else:
                            new[n, f, c, pl.ds(start, 8), :] = total[f, c]
            if not final:
                for f in range(FIELDS):
                    ends[f, pl.ds(start, 8), :] = last[f]

        if not final:
            value = off_diagonal(*sides.parts(hold, ends))
            side_next = sides.product(
                [value[f] + ratio * hrhs[f, sides.span, :] for f in range(FIELDS)], running
            )
            for f in range(FIELDS):
                hnew[f, sides.span, :] = side_next[f]
            sides.set_seams(seams, side_next)

    buffers = [(ya, hya), (yb, hyb)]
    for m in range(1, SWEEPS):
        old, new = buffers[(m + 1) % 2], buffers[m % 2]
        final = m == SWEEPS - 1
        sweep(ratios[m - 1], *old, result if final else new[0], new[1], final)


def join_kernel(width_tm, steps_dev, rows, *refs):
    half = width_tm // 2
    inner_own, outer_own, inner_other, outer_other, chained, state = refs[:6]
    outs = refs[6 : 6 + half]
    given, pa, pb, hgiven, hpa, hpb, ends, seams, result = refs[6 + half :]
    steps = half * steps_dev
    me = lax.axis_index("tm")
    mine = me & (half - 1)
    gammas, _, scale = chain_factors()
    own, first, second = swap_factors(steps)
    other = [jnp.where(me < half, a, b) for a, b in zip(first, second)]
    sides = Side(rows)
    blocks = sides.tall // 8
    middle = slice(ROW0 + 8, ROW0 + rows)
    main = SWEEPS * FIELDS * SLABS * 16

    def joined(pick_own, pick_other, p):
        total = None
        for d in range(SWEEPS - p):
            term = other[d] * pick_other(p + d) + own[d] * pick_own(p + d)
            total = term if total is None else total + term
        return total

    for f, c in EACH:
        for p in range(SWEEPS):
            value = joined(lambda k: inner_own[k, f, c], lambda k: inner_other[k, f, c], p)
            given[p, f, c, middle, :] = value
            pa[p, f, c, middle, :] = gammas[-1] * value
            for which, start in enumerate((ROW0, ROW0 + rows)):

                def pick(ref, k):
                    at = ((k * FIELDS + f) * SLABS + c) * 16 + 8 * which
                    return ref[at : at + 8, :]

                value = joined(lambda k: pick(outer_own, k), lambda k: pick(outer_other, k), p)
                given[p, f, c, start : start + 8, :] = value
                pa[p, f, c, start : start + 8, :] = gammas[-1] * value

    def from_later(value, d):
        return jnp.where(sides.step < SWEEPS - d, turn(value, -GROUP * d), 0.0)

    side_new = []
    for f in range(FIELDS):
        rows_f = slice(main + sides.tall * f, main + sides.tall * (f + 1))
        value = jnp.zeros((sides.tall, LANES), jnp.float32)
        for d in range(SWEEPS):
            value = value + from_later(
                other[d] * outer_other[rows_f, :] + own[d] * outer_own[rows_f, :], d
            )
        hgiven[f, sides.span, :] = value
        side_new.append(gammas[-1] * value)
        hpa[f, sides.span, :] = side_new[f]
    sides.set_seams(seams, side_new)

    buffers = [(pa, hpa), (pb, hpb)]
    for k in range(1, SWEEPS):
        (old, hold), (new, hnew) = buffers[(k + 1) % 2], buffers[k % 2]
        gamma = gammas[SWEEPS - 1 - k]
        final = k == SWEEPS - 1
        first_row = MAIN if final else ROW0

        @pl.loop(0, rows // 8 if final else blocks)
        def _(t):
            start = first_row + 8 * t
            here = pl.ds(start, 8)
            seam = [seams[f, here, :] for f in range(FIELDS)]
            last = zeros(FIELDS)
            found = {}
            for p in range(SWEEPS):
                parts = neighbours(old, p, start, seam, p)
                if not final:
                    add_ends(last, parts[0], p)
                for c in range(SLABS):
                    value = off_diagonal(*slab(parts, c))
                    for f in range(FIELDS):
                        total = value[f]
                        if p + k < SWEEPS:
                            total = total + gamma * given[p + k, f, c, here, :]
                        if final:
                            found[p, f, c] = total * RATE ** (p + 1)
                        else:
                            new[p, f, c, here, :] = total
            if not final:
                for f in range(FIELDS):
                    ends[f, here, :] = last[f]
            else:
                at = pl.ds(pl.multiple_of(8 * t, 8), 8)
                for f, c in EACH:
                    for n in range(steps):
                        total = scale * chained[n, f, c, at, :]
                        for p in range(SWEEPS):
                            total = total + binomial(n + p, p) * found[p, f, c]
                        result[n, f, c, at, :] = state[n + 1, f, c, here, :] - total * RATE**n

        if not final:
            value = off_diagonal(*sides.parts(hold, ends))
            side_next = [
                value[f] + gamma * from_later(hgiven[f, sides.span, :], k) for f in range(FIELDS)
            ]
            for f in range(FIELDS):
                hnew[f, sides.span, :] = side_next[f]
            sides.set_seams(seams, side_next)

    for b in range(half):
        at = 0
        for c in range(SLABS):
            for i in range(steps_dev):
                n = steps_dev * (mine ^ b) + i
                for f in range(FIELDS):
                    outs[b][at : at + rows, :] = result[n, f, c, :, :]
                    at += rows


def unpack_kernel(width_tm, *refs):
    half = width_tm // 2
    pieces, out = refs[:half], refs[half]
    steps_dev, fields, rows, _ = out.shape
    mine = lax.axis_index("tm") & (half - 1)
    for b in range(half):
        at = 0
        for c in range(SLABS):
            for i in range(steps_dev):
                for f in range(fields):
                    out[i, f, :, tile_at(SLABS * (mine ^ b) + c)] = pieces[b][at : at + rows, :]
                    at += rows


def call(kernel, out_shapes, operands, scratch=(), aliases=None):
    whole = pl.BlockSpec(memory_space=pltpu.VMEM)
    shapes = [jax.ShapeDtypeStruct(shape, jnp.float32) for shape in out_shapes]
    moved = 4 * sum(math.prod(x.shape) for x in list(shapes) + list(operands))
    return pl.pallas_call(
        kernel,
        out_shape=shapes,
        in_specs=[whole] * len(operands),
        out_specs=[whole] * len(shapes),
        scratch_shapes=[pltpu.VMEM(shape, jnp.float32) for shape in scratch],
        input_output_aliases=aliases or {},
        compiler_params=pltpu.CompilerParams(vmem_limit_bytes=VMEM_BYTES),
        cost_estimate=pl.CostEstimate(flops=moved, bytes_accessed=moved, transcendentals=0),
    )(*operands)


def swap(piece, b):
    count = lax.axis_size("tm")
    return lax.ppermute(piece, "tm", [(k, k ^ b) for k in range(count)])


def fast_on_device(state, initial):
    steps_dev, fields, rows, columns = state.shape
    width_tm = lax.axis_size("tm")
    bands = lax.axis_size("space")
    half = width_tm // 2
    steps = steps_dev * half
    main = SLABS * steps_dev * fields * rows
    words = -(-fields * rows // 8 // (LANES // (GROUP * steps_dev)))
    tall = rows + 2 * HALO + 2 * ROW0
    sized = (width_tm, steps_dev)
    pieces = call(
        functools.partial(pack_kernel, width_tm), [(main + 8 * words, LANES)] * half, [state]
    )
    pieces = [pieces[0]] + [swap(pieces[b], b) for b in range(1, half)]
    edge_rows = -(-HALO * fields * (SLABS * (steps + 1) + 2) // 8) * 8
    up, down, side, side_initial = call(
        functools.partial(edge_kernel, *sized),
        [(edge_rows, LANES)] * 2 + [(fields, rows, LANES)] * 2,
        pieces + [initial],
    )
    above = lax.ppermute(down, "space", [(i, (i + 1) % bands) for i in range(bands)])
    below = lax.ppermute(up, "space", [((i + 1) % bands, i) for i in range(bands)])
    flat = (fields, tall, LANES)
    held = [(steps + 1, fields, SLABS, tall, LANES), (steps, fields, SLABS, tall, LANES), flat]
    held_shapes = held
    *held, inner = call(
        functools.partial(inner_kernel, *sized),
        held_shapes + [(SWEEPS, fields, SLABS, rows - 8, LANES)],
        pieces + [initial, side],
        [flat],
    )
    inner_other = swap(inner, half)
    tall_rows = rows + 2 * HALO
    solved, rhs, _, hrhs, outer = call(
        functools.partial(outer_kernel, *sized, rows),
        held_shapes + [flat, (SWEEPS * fields * SLABS * 16 + fields * tall_rows, LANES)],
        held + [side, side_initial, above, below],
        [flat] * 3,
        aliases={0: 0, 1: 1, 2: 2},
    )
    outer_other = swap(outer, half)
    (chained,) = call(
        functools.partial(chain_kernel, steps, rows),
        [(steps, fields, SLABS, rows, LANES)],
        [rhs, hrhs],
        [held_shapes[1]] * 2 + [flat] * 4,
    )
    four = (SWEEPS, fields, SLABS, tall, LANES)
    results = call(
        functools.partial(join_kernel, *sized, rows),
        [(main, LANES)] * half,
        [inner, outer, inner_other, outer_other, chained, solved],
        [four] * 3 + [flat] * 5 + [(steps, fields, SLABS, rows, LANES)],
    )
    results = [results[0]] + [swap(results[b], b) for b in range(1, half)]
    (updated,) = call(functools.partial(unpack_kernel, width_tm), [state.shape], results)
    return updated


def choose(state, initial):
    if fits_fast_plan(state, lax.axis_size("tm")):
        return fast_on_device(state, initial)
    return on_device(state, initial)


def solution(mesh):
    in_specs = (P("tm", None, "space", None), P(None, "space", None))
    out_specs = P("tm", None, "space", None)
    return jax.shard_map(
        choose, mesh=mesh, in_specs=in_specs, out_specs=out_specs, check_vma=False
    )
```

```python
import functools
import math

import jax
import jax.numpy as jnp
from jax import lax
from jax.experimental import pallas as pl
from jax.experimental.pallas import tpu as pltpu
from jax.sharding import PartitionSpec as P

SWEEPS = 4


circulant_alpha = 0.1
time_step = 0.5
coriolis = 0.3
viscous = 0.2
highest = lax.Precision.HIGHEST


def from_behind(block, axis, distance):
    devices = range(lax.axis_size(axis))
    route = [(i - distance, i) for i in devices if i - distance in devices]
    return lax.ppermute(block, axis, route)


def extended(cells, sides, width):
    for axis, dim in sides:
        count = lax.axis_size(axis)
        head = lax.slice_in_dim(cells, 0, width, axis=dim)
        tail = lax.slice_in_dim(cells, cells.shape[dim] - width, cells.shape[dim], axis=dim)
        cells = jnp.concatenate(
            [
                lax.ppermute(tail, axis, [(i, (i + 1) % count) for i in range(count)]),
                cells,
                lax.ppermute(head, axis, [((i + 1) % count, i) for i in range(count)]),
            ],
            axis=dim,
        )
    return cells


def interior(values):
    return values[..., 1:-1, :]


def column_diff(values):
    return 0.5 * (jnp.roll(values, -1, axis=-1) - jnp.roll(values, 1, axis=-1))[..., 1:-1, :]


def row_diff(values):
    return 0.5 * (values[..., 2:, :] - values[..., :-2, :])


def laplace(values):
    return (
        values[..., 2:, :]
        + values[..., :-2, :]
        + jnp.roll(values, -1, axis=-1)[..., 1:-1, :]
        + jnp.roll(values, 1, axis=-1)[..., 1:-1, :]
        - 4.0 * values[..., 1:-1, :]
    )


def tendency(padded):
    surface = padded[..., 0, :, :]
    eastward = padded[..., 1, :, :]
    northward = padded[..., 2, :, :]
    column_depth = 1.0 + surface
    east_inner = interior(eastward)
    north_inner = interior(northward)
    mass_change = time_step * (
        column_diff(column_depth * eastward) + row_diff(column_depth * northward)
    ) - viscous * laplace(surface)
    east_change = (
        time_step
        * (
            east_inner * column_diff(eastward)
            + north_inner * row_diff(eastward)
            + column_diff(surface)
        )
        - coriolis * north_inner
        - viscous * laplace(eastward)
    )
    north_change = (
        time_step
        * (
            east_inner * column_diff(northward)
            + north_inner * row_diff(northward)
            + row_diff(surface)
        )
        + coriolis * east_inner
        - viscous * laplace(northward)
    )
    return jnp.stack([mass_change, east_change, north_change], axis=-3)


def linear_part(padded):
    surface = padded[..., 0, :, :]
    eastward = padded[..., 1, :, :]
    northward = padded[..., 2, :, :]
    mass_change = time_step * (column_diff(eastward) + row_diff(northward)) - viscous * laplace(
        surface
    )
    east_change = (
        time_step * column_diff(surface)
        - coriolis * interior(northward)
        - viscous * laplace(eastward)
    )
    north_change = (
        time_step * row_diff(surface) + coriolis * interior(eastward) - viscous * laplace(northward)
    )
    return jnp.stack([mass_change, east_change, north_change], axis=-3)


def pair_apply(factors, values):
    factor = factors[:, :, None, None, None]
    return jnp.stack(
        [
            factor[0] * values[0] - factor[1] * values[1],
            factor[2] * values[1] + factor[3] * values[0],
        ]
    )


def sweep_weights():
    return [
        1.0 / (1.15 - 0.85 * math.cos(math.pi * (2 * sweep + 1) / (2 * SWEEPS)))
        for sweep in range(SWEEPS)
    ]


def slot_factors(slot_index, total_steps):
    decay_base = circulant_alpha ** (1.0 / total_steps)
    angles = 2.0 * math.pi / total_steps * slot_index.astype(jnp.float32)
    real_eigen = 1.0 - decay_base * jnp.cos(angles)
    imaginary_eigen = decay_base * jnp.sin(angles)
    real_shift = real_eigen + 4.0 * viscous
    modulus = real_shift * real_shift + imaginary_eigen * imaginary_eigen
    eigen = jnp.stack([real_eigen, imaginary_eigen, real_eigen, imaginary_eigen])
    jacobi = jnp.stack(
        [
            real_shift / modulus,
            -imaginary_eigen / modulus,
            real_shift / modulus,
            -imaginary_eigen / modulus,
        ]
    )
    leading = (slot_index == 0)[None, :]
    zero_part = jnp.zeros_like(real_eigen)
    packed_eigen = jnp.stack(
        [zero_part + (1.0 - decay_base), zero_part, zero_part + (1.0 + decay_base), zero_part]
    )
    packed_jacobi = jnp.stack(
        [
            zero_part + 1.0 / (1.0 - decay_base + 4.0 * viscous),
            zero_part,
            zero_part + 1.0 / (1.0 + decay_base + 4.0 * viscous),
            zero_part,
        ]
    )
    eigen = jnp.where(leading, packed_eigen, eigen)
    jacobi = jnp.where(leading, packed_jacobi, jacobi)
    return (eigen, jacobi)


def time_tables(total_steps):
    slot_total = total_steps // 2
    step_ids = jnp.arange(total_steps, dtype=jnp.int32)
    slot_ids = jnp.arange(slot_total, dtype=jnp.int32)
    phase = slot_ids[:, None] * step_ids[None, :] % total_steps
    angles = 2.0 * math.pi / total_steps * phase.astype(jnp.float32)
    decay_base = circulant_alpha ** (1.0 / total_steps)
    growth = decay_base ** step_ids.astype(jnp.float32)
    cosine = jnp.cos(angles)
    sines = jnp.sin(angles)
    forward_real = cosine * growth[None, :]
    forward_imaginary = -sines * growth[None, :]
    inverse_imaginary = -sines
    alternate = 1.0 - 2.0 * (step_ids % 2).astype(jnp.float32)
    leading = (slot_ids == 0)[:, None]
    forward_imaginary = jnp.where(leading, (alternate * growth)[None, :], forward_imaginary)
    inverse_real = jnp.where(leading, 1.0, 2.0 * cosine)
    inverse_imaginary = jnp.where(leading, alternate[None, :], -2.0 * sines)
    forward = jnp.concatenate([forward_real, forward_imaginary], axis=0)
    inverse = jnp.concatenate([inverse_real, inverse_imaginary], axis=0).T
    inverse = inverse * (1.0 / (total_steps * growth))[:, None]
    return (forward, inverse)


def on_device(state, initial):
    steps_dev, fields, band_rows, columns = state.shape
    width_tm = lax.axis_size("tm")
    total_steps = steps_dev * width_tm
    previous = from_behind(state[-1], "tm", 1)
    previous = jnp.where(lax.axis_index("tm") == 0, initial, previous)
    before = jnp.concatenate([previous[None], state[:-1]], axis=0)
    padded = extended(state, (("space", 2),), 1)
    residual = state - before + tendency(padded)
    forward, inverse = time_tables(total_steps)
    slot_total = forward.shape[0] // 2
    per_device = slot_total // width_tm
    spectrum = jnp.einsum(
        "rj,jnc->rnc",
        forward,
        lax.all_to_all(
            residual.reshape(steps_dev, fields, band_rows * columns),
            "tm",
            split_axis=2,
            concat_axis=0,
            tiled=True,
        ),
        precision=highest,
    )
    spectrum = spectrum.reshape(2, slot_total, fields, spectrum.shape[-1])
    banded = lax.all_to_all(spectrum, "tm", split_axis=1, concat_axis=3, tiled=True).reshape(
        2, per_device, fields, band_rows, columns
    )
    slot_index = lax.axis_index("tm") * per_device + jnp.arange(per_device, dtype=jnp.int32)
    eigen, jacobi = slot_factors(slot_index, total_steps)
    weights = sweep_weights()
    iterate = weights[0] * pair_apply(jacobi, banded)
    for sweep in range(1, SWEEPS):
        border = extended(iterate, (("space", 3),), 1)
        applied = pair_apply(eigen, iterate) + linear_part(border)
        iterate = iterate + weights[sweep] * pair_apply(jacobi, banded - applied)
    flat_solution = iterate.reshape(2, per_device, fields, band_rows * columns)
    blocks = lax.all_to_all(flat_solution, "tm", split_axis=3, concat_axis=1, tiled=True)
    merged = blocks.reshape(2 * blocks.shape[1], blocks.shape[2], blocks.shape[3])
    all_steps = jnp.einsum("jr,rnc->jnc", inverse, merged, precision=highest)
    correction = lax.all_to_all(all_steps, "tm", split_axis=0, concat_axis=2, tiled=True)
    return state - correction.reshape(state.shape)


LANES = 128
HALO = SWEEPS
GROUP = 2 * HALO
ROW0 = 8
MAIN = ROW0 + HALO
SHIFT = 1.0 + 4.0 * viscous
RATE = 1.0 / SHIFT
VMEM_BYTES = 48 * 1024 * 1024
SLABS = 2
FIELDS = 3
EACH = [(f, c) for f in range(FIELDS) for c in range(SLABS)]


def fits_fast_plan(state, width_tm):
    steps_dev, fields, band_rows, columns = state.shape
    half = width_tm // 2
    steps = steps_dev * half
    return (
        width_tm > 1
        and width_tm & (width_tm - 1) == 0
        and columns == SLABS * LANES * half
        and SWEEPS * GROUP <= GROUP * steps <= LANES
        and LANES % (GROUP * steps_dev) == 0
        and band_rows % 8 == 0
        and band_rows >= 24
        and fields == FIELDS
    )


def lanes(rows=8):
    return lax.broadcasted_iota(jnp.int32, (rows, LANES), 1)


def step_of_lane(lane):
    return ((lane + HALO) & (LANES - 1)) // GROUP


def turn(values, shift):
    return pltpu.roll(values, shift % LANES, 1)


def tile_at(index):
    return pl.ds(pl.multiple_of(index * LANES, LANES), LANES)


def binomial(top, bottom):
    return float(math.comb(top, bottom))


def side_places(tile, width_tm):
    last = width_tm // 2 * SLABS - 1
    return tile_at((SLABS * tile + SLABS) & last), tile_at((SLABS * tile + last) & last)


def pack_kernel(width_tm, state_ref, *outs):
    steps_dev, fields, rows, _ = state_ref.shape
    half = width_tm // 2
    me = lax.axis_index("tm")
    lane = lanes()
    step = step_of_lane(lane)
    blocks = rows // 8
    per_word = LANES // (GROUP * steps_dev)
    for b, out in enumerate(outs):
        tile = (me ^ b) & (half - 1)
        after, prior = side_places(tile, width_tm)
        at = 0
        for c in range(SLABS):
            for i in range(steps_dev):
                for f in range(fields):
                    out[at : at + rows, :] = state_ref[i, f, :, tile_at(SLABS * tile + c)]
                    at += rows
        for first in range(0, fields * blocks, per_word):
            packed = jnp.zeros((8, LANES), jnp.float32)
            for g in range(first, min(first + per_word, fields * blocks)):
                f, r = divmod(g, blocks)
                for i in range(steps_dev):
                    slot = steps_dev * (g - first) + i
                    sides = jnp.where(
                        lane < LANES // 2,
                        state_ref[i, f, 8 * r : 8 * r + 8, after],
                        state_ref[i, f, 8 * r : 8 * r + 8, prior],
                    )
                    packed = jnp.where(step == slot, turn(sides, GROUP * slot), packed)
            out[at : at + 8, :] = packed
            at += 8


def place_initial(width_tm, initial_ref, _, tiles, side_initial):
    fields, rows, _ = initial_ref.shape
    mine = lax.axis_index("tm") & (width_tm // 2 - 1)
    after, prior = side_places(mine, width_tm)
    for f, c in EACH:
        tiles[f, c] = initial_ref[f, :, tile_at(SLABS * mine + c)]
    lane = lanes(rows)
    for f in range(fields):
        side_initial[f] = jnp.where(
            lane < LANES // 2, initial_ref[f, :, after], initial_ref[f, :, prior]
        )


def edge_kernel(width_tm, *refs):
    half = width_tm // 2
    pieces, (tiles, side, side_initial, up, down) = refs[:half], refs[half:]
    fields, rows, _ = side.shape
    main = pieces[0].shape[0] // rows * rows
    for out, part in ((up, slice(0, HALO)), (down, slice(rows - HALO, rows))):
        k = 0
        for b in range(half):
            for at in range(0, main, rows):
                out[k : k + HALO, :] = pieces[b][at + part.start : at + part.stop, :]
                k += HALO
        for c in range(SLABS):
            for f in range(fields):
                out[k : k + HALO, :] = tiles[f, c, part, :]
                k += HALO
        for held in (side, side_initial):
            for f in range(fields):
                out[k : k + HALO, :] = held[f, part, :]
                k += HALO


def full_tendency(own, east, west, north, south):
    e, u, v = own
    around = [east[f] + west[f] + (north[f] + south[f]) for f in range(FIELDS)]
    quarter = 0.5 * time_step
    flux = ((1.0 + east[0]) * east[1] - (1.0 + west[0]) * west[1]) + (
        (1.0 + south[0]) * south[2] - (1.0 + north[0]) * north[2]
    )
    carry1 = u * (east[1] - west[1]) + v * (south[1] - north[1]) + (east[0] - west[0])
    carry2 = u * (east[2] - west[2]) + v * (south[2] - north[2]) + (south[0] - north[0])
    diagonal = 1.0 + 4.0 * viscous
    return (
        diagonal * e + quarter * flux - viscous * around[0],
        diagonal * u + quarter * carry1 - coriolis * v - viscous * around[1],
        diagonal * v + quarter * carry2 + coriolis * u - viscous * around[2],
    )


def off_diagonal(own, east, west, north, south):
    _, u, v = own
    around = [east[f] + west[f] + (north[f] + south[f]) for f in range(FIELDS)]
    quarter = 0.5 * time_step
    return (
        viscous * around[0] - quarter * ((east[1] - west[1]) + (south[2] - north[2])),
        viscous * around[1] - quarter * (east[0] - west[0]) + coriolis * v,
        viscous * around[2] - quarter * (south[0] - north[0]) - coriolis * u,
    )


def chain_factors():
    gammas = []
    for weight in sweep_weights():
        shifted = [1.0] + gammas
        gammas = [weight * x for x in shifted]
        for i, x in enumerate(shifted[1:]):
            gammas[i] += (1.0 - weight) * x
    scale = RATE * gammas[-1]
    ratios = []
    for gamma in reversed(gammas[:-1]):
        ratios.append(gamma / scale)
        scale *= RATE
    return gammas, ratios, scale


def series_product(a, b):
    return [sum(a[i] * b[d - i] for i in range(d + 1)) for d in range(SWEEPS)]


def swap_factors(steps):
    hop = [RATE ** (steps + d) * binomial(steps - 1 + d, d) for d in range(SWEEPS)]
    lap = [circulant_alpha * x for x in series_product(hop, hop)]
    inverse = []
    for d in range(SWEEPS):
        value = (1.0 if d == 0 else 0.0) + sum(lap[i] * inverse[d - i] for i in range(1, d + 1))
        inverse.append(value / (1.0 - lap[0]))
    own = [circulant_alpha * x for x in series_product(inverse, hop)]
    return own, [circulant_alpha * x for x in inverse], inverse


class Side:
    def __init__(self, first, tall):
        self.first, self.tall = first, tall
        self.span = slice(first, first + tall)
        lane = lanes(self.tall)
        self.step = step_of_lane(lane)
        self.after = (lane & (GROUP - 1)) == 0
        self.before = (lane & (GROUP - 1)) == GROUP - 1

    def parts(self, held, ends):
        own, north, south = (
            [held[f, self.first + d : self.first + d + self.tall, :] for f in range(FIELDS)] for d in (0, -1, 1)
        )
        last = [ends[f, self.span, :] for f in range(FIELDS)]
        east = [jnp.where(self.before, turn(last[f], -1), turn(own[f], -1)) for f in range(FIELDS)]
        west = [jnp.where(self.after, turn(last[f], 1), turn(own[f], 1)) for f in range(FIELDS)]
        return own, east, west, north, south

    def set_seams(self, seams, values):
        for f in range(FIELDS):
            seams[f, self.span, :] = jnp.where(self.after, turn(values[f], 1), turn(values[f], -1))

    def product(self, values, matrix):
        done = jnp.dot(
            jnp.concatenate(values, axis=0),
            matrix,
            precision=highest,
            preferred_element_type=jnp.float32,
        )
        return [done[self.tall * f : self.tall * (f + 1), :] for f in range(FIELDS)]


def lane_matrix(entry):
    source = lax.broadcasted_iota(jnp.int32, (LANES, LANES), 0)
    target = lax.broadcasted_iota(jnp.int32, (LANES, LANES), 1)
    same = ((source - target) & (GROUP - 1)) == 0
    return jnp.where(same, entry(step_of_lane(source), step_of_lane(target)), 0.0)


def neighbours(held, slot, start, seam, n):
    lane = lanes()
    is_first, is_last = lane == 0, lane == LANES - 1
    load = lambda d: {k: held[slot, k[0], k[1], pl.ds(start + d, 8), :] for k in EACH}
    own, north, south = load(0), load(-1), load(1)
    east, west = {}, {}
    for f in range(FIELDS):
        across = turn(seam[f], -GROUP * n)
        back = [turn(own[f, c], -1) for c in range(SLABS)] + [across]
        ahead = [across] + [turn(own[f, c], 1) for c in range(SLABS)]
        for c in range(SLABS):
            east[f, c] = jnp.where(is_last, back[c + 1], back[c])
            west[f, c] = jnp.where(is_first, ahead[c], ahead[c + 1])
    return own, east, west, north, south


def slab(parts, c):
    return [[part[f, c] for f in range(FIELDS)] for part in parts]


def add_ends(last, own, n):
    lane = lanes()
    step = step_of_lane(lane)
    for f in range(FIELDS):
        both = jnp.where(lane < LANES // 2, own[f, 0], own[f, SLABS - 1])
        last[f] = jnp.where(step == n, turn(both, GROUP * n), last[f])


def zeros(count):
    return [jnp.zeros((8, LANES), jnp.float32)] * count


def residual_tile(steps, first_half, start, state, rhs, seams, ends, send):
    seam = [seams[f, pl.ds(start, 8), :] for f in range(FIELDS)]
    last = zeros(FIELDS)
    sums = {k: zeros(SWEEPS) for k in EACH}
    for n in range(steps):
        parts = neighbours(state, n + 1, start, seam, n)
        add_ends(last, parts[0], n)
        for c in range(SLABS):
            value = full_tendency(*slab(parts, c))
            for f in range(FIELDS):
                carry = (value[f] - state[n, f, c, pl.ds(start, 8), :]) * SHIFT**n
                rhs[n, f, c, pl.ds(start, 8), :] = carry
                for j in range(SWEEPS):
                    carry = sums[f, c][j] + carry
                    sums[f, c][j] = carry
    for f in range(FIELDS):
        ends[f, pl.ds(start, 8), :] = last[f]
    for f, c in EACH:
        for j in range(SWEEPS):
            value = sums[f, c][j] * RATE ** (steps + j)
            if j == 0:
                value = value - jnp.where(first_half, state[steps, f, c, pl.ds(start, 8), :], 0.0)
            send(SWEEPS - 1 - j, f, c, value)


PER_WORD = LANES // (SWEEPS * GROUP)


def pack_sides(blocks, sent, at):
    kind = step_of_lane(lanes()) // SWEEPS
    for first in range(0, len(blocks), PER_WORD):
        word = jnp.zeros((8, LANES), jnp.float32)
        for k, block in enumerate(blocks[first : first + PER_WORD]):
            word = jnp.where(kind == k, turn(block, SWEEPS * GROUP * k), word)
        sent[at : at + 8, :] = word
        at += 8


def unpack_side(sent, at, index):
    word, k = divmod(index, PER_WORD)
    value = turn(sent[at + 8 * word : at + 8 * word + 8, :], -SWEEPS * GROUP * k)
    return jnp.where(step_of_lane(lanes()) < SWEEPS, value, 0.0)


def side_residual(sides, steps, first_half, hstate, ends, before_first, hrhs):
    parts = sides.parts(hstate, ends)
    value = full_tendency(*parts)
    growth = jnp.where(
        sides.step < steps, jnp.exp(sides.step.astype(jnp.float32) * math.log(SHIFT)), 0.0
    )
    held = []
    for f in range(FIELDS):
        first = jnp.where(first_half, before_first(f), 0.0)
        before = jnp.where(sides.step == 0, first, turn(parts[0][f], GROUP))
        held.append((value[f] - before) * growth)
        hrhs[f, sides.span, :] = held[f]

    def entry(source, target):
        result = jnp.zeros((LANES, LANES), jnp.float32)
        for p in range(SWEEPS):
            j = SWEEPS - p
            for n in range(steps):
                weight = RATE ** (steps - 1 + j) * binomial(steps - 1 - n + j - 1, j - 1)
                result = jnp.where((target == p) & (source == n), weight, result)
        return result

    handed = sides.product(held, lane_matrix(entry))
    for f in range(FIELDS):
        last = turn(parts[0][f], GROUP * (SWEEPS - steps))
        handed[f] = handed[f] - jnp.where(first_half & (sides.step == SWEEPS - 1), last, 0.0)
    return handed


def inner_kernel(width_tm, steps_dev, *refs):
    half = width_tm // 2
    pieces, (tiles, side_initial) = refs[:half], refs[half : half + 2]
    state, rhs, ends, hrhs, side, sent, seams, hstate = refs[half + 2 :]
    fields, rows, _ = side.shape
    steps = half * steps_dev
    me = lax.axis_index("tm")
    mine = me & (half - 1)
    first_half = me < half
    body = slice(MAIN, MAIN + rows)
    for b in range(half):
        at = 0
        for c in range(SLABS):
            for i in range(steps_dev):
                n = steps_dev * (mine ^ b) + i
                for f in range(fields):
                    state[n + 1, f, c, body, :] = pieces[b][at : at + rows, :]
                    at += rows
    for f, c in EACH:
        state[0, f, c, body, :] = jnp.where(first_half, tiles[f, c], 0.0)
    owner = step_of_lane(lanes()) // steps_dev
    blocks = rows // 8
    per_word = LANES // (GROUP * steps_dev)
    main = SLABS * steps_dev * fields * rows
    for g in range(fields * blocks):
        f, r = divmod(g, blocks)
        word, place = divmod(g, per_word)
        found = jnp.zeros((8, LANES), jnp.float32)
        for b in range(half):
            source = mine ^ b
            value = pieces[b][main + 8 * word : main + 8 * word + 8, :]
            shift = (GROUP * steps_dev * (source - place)) & (LANES - 1)
            found = jnp.where(owner == source, pltpu.roll(value, shift, 1), found)
        side[f, 8 * r : 8 * r + 8, :] = found
        hstate[f, MAIN + 8 * r : MAIN + 8 * r + 8, :] = found
    Side(MAIN, rows).set_seams(seams, [side[f] for f in range(fields)])

    @pl.loop(1, blocks)
    def _(t):
        def send(p, f, c, value):
            at = ((p * FIELDS + f) * SLABS + c) * (rows - 8) + 8 * t - 8
            sent[pl.ds(pl.multiple_of(at, 8), 8), :] = value

        residual_tile(steps, first_half, ROW0 + 8 * t, state, rhs, seams, ends, send)

    sides = Side(ROW0 + 8, rows - 8)
    before_first = lambda f: side_initial[f, HALO : rows - HALO, :]
    handed = side_residual(sides, steps, first_half, hstate, ends, before_first, hrhs)
    flat = [handed[f][at : at + 8, :] for f in range(FIELDS) for at in range(0, rows - 8, 8)]
    pack_sides(flat, sent, SWEEPS * FIELDS * SLABS * (rows - 8))


def outer_kernel(width_tm, steps_dev, rows, *refs):
    half = width_tm // 2
    side, side_initial, above, below = refs[4:8]
    state, rhs, ends, hrhs, sent, hstate, hbefore, seams = refs[8:]
    steps = half * steps_dev
    me = lax.axis_index("tm")
    mine = me & (half - 1)
    first_half = me < half
    body = slice(MAIN, MAIN + rows)
    top, bottom = slice(ROW0, MAIN), slice(MAIN + rows, MAIN + rows + HALO)
    k = 0
    for b in range(half):
        for c in range(SLABS):
            for i in range(steps_dev):
                n = steps_dev * (mine ^ b) + i
                for f in range(FIELDS):
                    state[n + 1, f, c, top, :] = above[k : k + HALO, :]
                    state[n + 1, f, c, bottom, :] = below[k : k + HALO, :]
                    k += HALO
    for c in range(SLABS):
        for f in range(FIELDS):
            state[0, f, c, top, :] = jnp.where(first_half, above[k : k + HALO, :], 0.0)
            state[0, f, c, bottom, :] = jnp.where(first_half, below[k : k + HALO, :], 0.0)
            k += HALO
    for held, given in ((hstate, side), (hbefore, side_initial)):
        for f in range(FIELDS):
            held[f, body, :] = given[f, :, :]
            held[f, top, :] = above[k : k + HALO, :]
            held[f, bottom, :] = below[k : k + HALO, :]
            k += HALO
    whole = Side(ROW0, rows + 2 * HALO)
    whole.set_seams(seams, [hstate[f, whole.span, :] for f in range(FIELDS)])
    flat = []
    for which, start in enumerate((ROW0, ROW0 + rows)):

        def send(p, f, c, value):
            at = (((p * FIELDS + f) * SLABS + c) * 2 + which) * 7
            sent[at : at + 7, :] = value[1 - which : 8 - which, :]

        residual_tile(steps, first_half, start, state, rhs, seams, ends, send)
        sides = Side(start, 8)
        before_first = lambda f: hbefore[f, start : start + 8, :]
        flat += side_residual(sides, steps, first_half, hstate, ends, before_first, hrhs)
    pack_sides(flat, sent, SWEEPS * FIELDS * SLABS * 14)


def chain_kernel(steps, rows, rhs, hrhs, result, ya, yb, hya, hyb, ends, seams):
    _, ratios, _ = chain_factors()
    sides = Side(ROW0, rows + 2 * HALO)
    blocks = sides.tall // 8
    running = lane_matrix(
        lambda source, target: jnp.where((source <= target) & (target < steps), 1.0, 0.0)
    )
    side_new = sides.product([hrhs[f, sides.span, :] for f in range(FIELDS)], running)
    for f in range(FIELDS):
        hya[f, sides.span, :] = side_new[f]
    sides.set_seams(seams, side_new)

    @pl.loop(0, blocks)
    def _(t):
        start = ROW0 + 8 * t
        for f, c in EACH:
            total = jnp.zeros((8, LANES), jnp.float32)
            for n in range(steps):
                total = total + rhs[n, f, c, pl.ds(start, 8), :]
                ya[n, f, c, pl.ds(start, 8), :] = total

    def sweep(ratio, old, hold, new, hnew, final):
        first = MAIN if final else ROW0

        @pl.loop(0, rows // 8 if final else blocks)
        def _(t):
            start = first + 8 * t
            seam = [seams[f, pl.ds(start, 8), :] for f in range(FIELDS)]
            last = zeros(FIELDS)
            total = dict(zip(EACH, zeros(len(EACH))))
            for n in range(steps):
                parts = neighbours(old, n, start, seam, n)
                if not final:
                    add_ends(last, parts[0], n)
                for c in range(SLABS):
                    value = off_diagonal(*slab(parts, c))
                    for f in range(FIELDS):
                        carry = value[f] + ratio * rhs[n, f, c, pl.ds(start, 8), :]
                        total[f, c] = total[f, c] + carry
                        if final:
                            at = pl.ds(pl.multiple_of(8 * t, 8), 8)
                            new[n, f, c, at, :] = total[f, c]
                        else:
                            new[n, f, c, pl.ds(start, 8), :] = total[f, c]
            if not final:
                for f in range(FIELDS):
                    ends[f, pl.ds(start, 8), :] = last[f]

        if not final:
            value = off_diagonal(*sides.parts(hold, ends))
            side_next = sides.product(
                [value[f] + ratio * hrhs[f, sides.span, :] for f in range(FIELDS)], running
            )
            for f in range(FIELDS):
                hnew[f, sides.span, :] = side_next[f]
            sides.set_seams(seams, side_next)

    buffers = [(ya, hya), (yb, hyb)]
    for m in range(1, SWEEPS):
        old, new = buffers[(m + 1) % 2], buffers[m % 2]
        final = m == SWEEPS - 1
        sweep(ratios[m - 1], *old, result if final else new[0], new[1], final)


def join_kernel(width_tm, steps_dev, rows, inner_rows, *refs):
    half = width_tm // 2
    count = 2 if inner_rows else 4
    given_refs, (chained, state) = refs[:count], refs[count : count + 2]
    outs = refs[-9 - half : -9]
    given, pa, pb, hgiven, hpa, hpb, ends, seams, result = refs[-9:]
    inner_own, inner_other = given_refs[:2]
    steps = half * steps_dev
    me = lax.axis_index("tm")
    mine = me & (half - 1)
    gammas, _, scale = chain_factors()
    own, first, second = swap_factors(steps)
    other = [jnp.where(me < half, a, b) for a, b in zip(first, second)]
    tiles = rows // 8
    if inner_rows:
        sides = Side(ROW0 + 8, rows - 8)
        places = (tiles - 1, lambda t: ROW0 + 8 + 8 * t)
        finals = (tiles - 2, lambda t: MAIN + 8 + 8 * t)
    else:
        sides = Side(ROW0, rows + 2 * HALO)
        places = (4, lambda t: ROW0 + 8 * (t + (tiles - 3) * (t // 2)))
        finals = (2, lambda t: MAIN + (rows - 8) * t)
    cells = SWEEPS * FIELDS * SLABS

    def joined(ref_own, ref_other, at, size, step, p):
        total = None
        for d in range(SWEEPS - p):
            rows_d = slice(at + step * d, at + step * d + size)
            term = other[d] * ref_other[rows_d, :] + own[d] * ref_own[rows_d, :]
            total = term if total is None else total + term
        return total

    for p in range(SWEEPS):
        for f, c in EACH:
            cell = (p * FIELDS + f) * SLABS + c
            found = [(ROW0 + 8, joined(inner_own, inner_other, cell * (rows - 8), rows - 8, FIELDS * SLABS * (rows - 8), p))]
            if not inner_rows:
                for which, start in ((0, ROW0 + 1), (1, ROW0 + rows)):
                    at = (cell * 2 + which) * 7
                    found.append((start, joined(*given_refs[2:], at, 7, FIELDS * SLABS * 14, p)))
            for start, value in found:
                given[p, f, c, start : start + value.shape[0], :] = value
                pa[p, f, c, start : start + value.shape[0], :] = gammas[-1] * value

    step8 = step_of_lane(lanes())

    def from_later(value, d, step):
        return jnp.where(step < SWEEPS - d, turn(value, -GROUP * d), 0.0)

    def set_side(refs_side, at, index, f, start):
        ours, theirs = (unpack_side(ref, at, index) for ref in refs_side)
        value = jnp.zeros((8, LANES), jnp.float32)
        for d in range(SWEEPS):
            value = value + from_later(other[d] * theirs + own[d] * ours, d, step8)
        hgiven[f, start : start + 8, :] = value
        hpa[f, start : start + 8, :] = gammas[-1] * value

    for f in range(FIELDS):
        for r in range(tiles - 1):
            set_side(given_refs[:2], cells * (rows - 8), f * (tiles - 1) + r, f, ROW0 + 8 + 8 * r)
        if not inner_rows:
            for which, start in ((0, ROW0), (1, ROW0 + rows)):
                set_side(given_refs[2:], cells * 14, which * FIELDS + f, f, start)
    sides.set_seams(seams, [hpa[f, sides.span, :] for f in range(FIELDS)])

    buffers = [(pa, hpa), (pb, hpb)]
    for k in range(1, SWEEPS):
        (old, hold), (new, hnew) = buffers[(k + 1) % 2], buffers[k % 2]
        gamma = gammas[SWEEPS - 1 - k]
        final = k == SWEEPS - 1
        turns, place = finals if final else places

        @pl.loop(0, turns)
        def _(t):
            start = place(t)
            here = pl.ds(start, 8)
            seam = [seams[f, here, :] for f in range(FIELDS)]
            last = zeros(FIELDS)
            found = {}
            for p in range(SWEEPS):
                parts = neighbours(old, p, start, seam, p)
                if not final:
                    add_ends(last, parts[0], p)
                for c in range(SLABS):
                    value = off_diagonal(*slab(parts, c))
                    for f in range(FIELDS):
                        total = value[f]
                        if p + k < SWEEPS:
                            total = total + gamma * given[p + k, f, c, here, :]
                        if final:
                            found[p, f, c] = total * RATE ** (p + 1)
                        else:
                            new[p, f, c, here, :] = total
            if not final:
                for f in range(FIELDS):
                    ends[f, here, :] = last[f]
            else:
                at = pl.ds(pl.multiple_of(8 * t, 8), 8)
                from_chain = pl.ds(pl.multiple_of(start - MAIN, 8), 8)
                for f, c in EACH:
                    for n in range(steps):
                        total = scale * chained[n, f, c, from_chain, :]
                        for p in range(SWEEPS):
                            total = total + binomial(n + p, p) * found[p, f, c]
                        result[n, f, c, at, :] = state[n + 1, f, c, here, :] - total * RATE**n

        if not final:
            value = off_diagonal(*sides.parts(hold, ends))
            side_next = [
                value[f] + gamma * from_later(hgiven[f, sides.span, :], k, sides.step)
                for f in range(FIELDS)
            ]
            for f in range(FIELDS):
                hnew[f, sides.span, :] = side_next[f]
            sides.set_seams(seams, side_next)

    size = 8 * finals[0]
    for b in range(half):
        at = 0
        for c in range(SLABS):
            for i in range(steps_dev):
                n = steps_dev * (mine ^ b) + i
                for f in range(FIELDS):
                    outs[b][at : at + size, :] = result[n, f, c, :, :]
                    at += size


def unpack_kernel(width_tm, *refs):
    half = width_tm // 2
    inner, outer, out = refs[:half], refs[half : 2 * half], refs[2 * half]
    steps_dev, fields, rows, _ = out.shape
    mine = lax.axis_index("tm") & (half - 1)
    size = rows - 16
    for b in range(half):
        k = 0
        for c in range(SLABS):
            here = tile_at(SLABS * (mine ^ b) + c)
            for i in range(steps_dev):
                for f in range(fields):
                    out[i, f, 8 : rows - 8, here] = inner[b][size * k : size * (k + 1), :]
                    out[i, f, 0:8, here] = outer[b][16 * k : 16 * k + 8, :]
                    out[i, f, rows - 8 : rows, here] = outer[b][16 * k + 8 : 16 * k + 16, :]
                    k += 1


def call(kernel, out_shapes, operands, scratch=(), aliases=None, after=()):
    whole = pl.BlockSpec(memory_space=pltpu.VMEM)
    shapes = [jax.ShapeDtypeStruct(shape, jnp.float32) for shape in out_shapes]
    moved = 4 * sum(math.prod(x.shape) for x in list(shapes) + list(operands))
    in_specs = [whole] * len(operands) + [pl.BlockSpec(memory_space=pl.ANY)] * len(after)
    operands = list(operands) + list(after)
    return pl.pallas_call(
        kernel,
        out_shape=shapes,
        in_specs=in_specs,
        out_specs=[whole] * len(shapes),
        scratch_shapes=[pltpu.VMEM(shape, jnp.float32) for shape in scratch],
        input_output_aliases=aliases or {},
        compiler_params=pltpu.CompilerParams(vmem_limit_bytes=VMEM_BYTES),
        cost_estimate=pl.CostEstimate(flops=moved, bytes_accessed=moved, transcendentals=0),
    )(*operands)


def swap(piece, b):
    count = lax.axis_size("tm")
    return lax.ppermute(piece, "tm", [(k, k ^ b) for k in range(count)])


def fast_on_device(state, initial):
    steps_dev, fields, rows, columns = state.shape
    width_tm = lax.axis_size("tm")
    bands = lax.axis_size("space")
    half = width_tm // 2
    steps = steps_dev * half
    main = SLABS * steps_dev * fields * rows
    words = -(-fields * rows // 8 // (LANES // (GROUP * steps_dev)))
    tall = rows + 2 * HALO + 2 * ROW0
    sized = (width_tm, steps_dev)
    pieces = call(
        functools.partial(pack_kernel, width_tm), [(main + 8 * words, LANES)] * half, [state]
    )
    pieces = [pieces[0]] + [swap(pieces[b], b) for b in range(1, half)]
    tiles, side_initial = call(
        functools.partial(place_initial, width_tm),
        [(fields, SLABS, rows, LANES), (fields, rows, LANES)],
        [initial],
        after=pieces[:1],
    )
    flat = (fields, tall, LANES)
    held_shapes = [
        (steps + 1, fields, SLABS, tall, LANES),
        (steps, fields, SLABS, tall, LANES),
        flat,
        flat,
    ]
    cells = SWEEPS * fields * SLABS
    inner_words = -(-fields * (rows - 8) // 8 // PER_WORD)
    outer_words = -(-2 * fields // PER_WORD)
    *held, side, inner = call(
        functools.partial(inner_kernel, *sized),
        held_shapes
        + [(fields, rows, LANES), (cells * (rows - 8) + 8 * inner_words, LANES)],
        pieces + [tiles, side_initial],
        [flat] * 2,
    )
    inner_other = swap(inner, half)
    edge_rows = -(-HALO * fields * (SLABS * (steps + 1) + 2) // 8) * 8
    up, down = call(
        functools.partial(edge_kernel, width_tm),
        [(edge_rows, LANES)] * 2,
        pieces + [tiles, side, side_initial],
    )
    above = lax.ppermute(down, "space", [(i, (i + 1) % bands) for i in range(bands)])
    below = lax.ppermute(up, "space", [((i + 1) % bands, i) for i in range(bands)])
    solved, rhs, _, hrhs, outer = call(
        functools.partial(outer_kernel, *sized, rows),
        held_shapes + [(cells * 14 + 8 * outer_words, LANES)],
        held + [side, side_initial, above, below],
        [flat] * 3,
        aliases={0: 0, 1: 1, 2: 2, 3: 3},
    )
    outer_other = swap(outer, half)
    (chained,) = call(
        functools.partial(chain_kernel, steps, rows),
        [(steps, fields, SLABS, rows, LANES)],
        [rhs, hrhs],
        [held_shapes[1]] * 2 + [flat] * 4,
    )
    four = (SWEEPS, fields, SLABS, tall, LANES)
    results = []
    for given, size in (
        ([inner, inner_other], rows - 16),
        ([inner, inner_other, outer, outer_other], 16),
    ):
        parts = call(
            functools.partial(join_kernel, *sized, rows, len(given) == 2),
            [(SLABS * steps_dev * fields * size, LANES)] * half,
            given + [chained, solved],
            [four] * 3 + [flat] * 5 + [(steps, fields, SLABS, size, LANES)],
            after=results[:1],
        )
        results += [parts[0]] + [swap(parts[b], b) for b in range(1, half)]
    (updated,) = call(functools.partial(unpack_kernel, width_tm), [state.shape], results)
    return updated


def choose(state, initial):
    if fits_fast_plan(state, lax.axis_size("tm")):
        return fast_on_device(state, initial)
    return on_device(state, initial)


def solution(mesh):
    in_specs = (P("tm", None, "space", None), P(None, "space", None))
    out_specs = P("tm", None, "space", None)
    return jax.shard_map(
        choose, mesh=mesh, in_specs=in_specs, out_specs=out_specs, check_vma=False
    )
```

```python
import functools
import math

import jax
import jax.numpy as jnp
from jax import lax
from jax.experimental import pallas as pl
from jax.experimental.pallas import tpu as pltpu
from jax.sharding import PartitionSpec as P

SWEEPS = 4


circulant_alpha = 0.1
time_step = 0.5
coriolis = 0.3
viscous = 0.2
highest = lax.Precision.HIGHEST


def from_behind(block, axis, distance):
    devices = range(lax.axis_size(axis))
    route = [(i - distance, i) for i in devices if i - distance in devices]
    return lax.ppermute(block, axis, route)


def extended(cells, sides, width):
    for axis, dim in sides:
        count = lax.axis_size(axis)
        head = lax.slice_in_dim(cells, 0, width, axis=dim)
        tail = lax.slice_in_dim(cells, cells.shape[dim] - width, cells.shape[dim], axis=dim)
        cells = jnp.concatenate(
            [
                lax.ppermute(tail, axis, [(i, (i + 1) % count) for i in range(count)]),
                cells,
                lax.ppermute(head, axis, [((i + 1) % count, i) for i in range(count)]),
            ],
            axis=dim,
        )
    return cells


def interior(values):
    return values[..., 1:-1, :]


def column_diff(values):
    return 0.5 * (jnp.roll(values, -1, axis=-1) - jnp.roll(values, 1, axis=-1))[..., 1:-1, :]


def row_diff(values):
    return 0.5 * (values[..., 2:, :] - values[..., :-2, :])


def laplace(values):
    return (
        values[..., 2:, :]
        + values[..., :-2, :]
        + jnp.roll(values, -1, axis=-1)[..., 1:-1, :]
        + jnp.roll(values, 1, axis=-1)[..., 1:-1, :]
        - 4.0 * values[..., 1:-1, :]
    )


def tendency(padded):
    surface = padded[..., 0, :, :]
    eastward = padded[..., 1, :, :]
    northward = padded[..., 2, :, :]
    column_depth = 1.0 + surface
    east_inner = interior(eastward)
    north_inner = interior(northward)
    mass_change = time_step * (
        column_diff(column_depth * eastward) + row_diff(column_depth * northward)
    ) - viscous * laplace(surface)
    east_change = (
        time_step
        * (
            east_inner * column_diff(eastward)
            + north_inner * row_diff(eastward)
            + column_diff(surface)
        )
        - coriolis * north_inner
        - viscous * laplace(eastward)
    )
    north_change = (
        time_step
        * (
            east_inner * column_diff(northward)
            + north_inner * row_diff(northward)
            + row_diff(surface)
        )
        + coriolis * east_inner
        - viscous * laplace(northward)
    )
    return jnp.stack([mass_change, east_change, north_change], axis=-3)


def linear_part(padded):
    surface = padded[..., 0, :, :]
    eastward = padded[..., 1, :, :]
    northward = padded[..., 2, :, :]
    mass_change = time_step * (column_diff(eastward) + row_diff(northward)) - viscous * laplace(
        surface
    )
    east_change = (
        time_step * column_diff(surface)
        - coriolis * interior(northward)
        - viscous * laplace(eastward)
    )
    north_change = (
        time_step * row_diff(surface) + coriolis * interior(eastward) - viscous * laplace(northward)
    )
    return jnp.stack([mass_change, east_change, north_change], axis=-3)


def pair_apply(factors, values):
    factor = factors[:, :, None, None, None]
    return jnp.stack(
        [
            factor[0] * values[0] - factor[1] * values[1],
            factor[2] * values[1] + factor[3] * values[0],
        ]
    )


def sweep_weights():
    return [
        1.0 / (1.15 - 0.85 * math.cos(math.pi * (2 * sweep + 1) / (2 * SWEEPS)))
        for sweep in range(SWEEPS)
    ]


def slot_factors(slot_index, total_steps):
    decay_base = circulant_alpha ** (1.0 / total_steps)
    angles = 2.0 * math.pi / total_steps * slot_index.astype(jnp.float32)
    real_eigen = 1.0 - decay_base * jnp.cos(angles)
    imaginary_eigen = decay_base * jnp.sin(angles)
    real_shift = real_eigen + 4.0 * viscous
    modulus = real_shift * real_shift + imaginary_eigen * imaginary_eigen
    eigen = jnp.stack([real_eigen, imaginary_eigen, real_eigen, imaginary_eigen])
    jacobi = jnp.stack(
        [
            real_shift / modulus,
            -imaginary_eigen / modulus,
            real_shift / modulus,
            -imaginary_eigen / modulus,
        ]
    )
    leading = (slot_index == 0)[None, :]
    zero_part = jnp.zeros_like(real_eigen)
    packed_eigen = jnp.stack(
        [zero_part + (1.0 - decay_base), zero_part, zero_part + (1.0 + decay_base), zero_part]
    )
    packed_jacobi = jnp.stack(
        [
            zero_part + 1.0 / (1.0 - decay_base + 4.0 * viscous),
            zero_part,
            zero_part + 1.0 / (1.0 + decay_base + 4.0 * viscous),
            zero_part,
        ]
    )
    eigen = jnp.where(leading, packed_eigen, eigen)
    jacobi = jnp.where(leading, packed_jacobi, jacobi)
    return (eigen, jacobi)


def time_tables(total_steps):
    slot_total = total_steps // 2
    step_ids = jnp.arange(total_steps, dtype=jnp.int32)
    slot_ids = jnp.arange(slot_total, dtype=jnp.int32)
    phase = slot_ids[:, None] * step_ids[None, :] % total_steps
    angles = 2.0 * math.pi / total_steps * phase.astype(jnp.float32)
    decay_base = circulant_alpha ** (1.0 / total_steps)
    growth = decay_base ** step_ids.astype(jnp.float32)
    cosine = jnp.cos(angles)
    sines = jnp.sin(angles)
    forward_real = cosine * growth[None, :]
    forward_imaginary = -sines * growth[None, :]
    inverse_imaginary = -sines
    alternate = 1.0 - 2.0 * (step_ids % 2).astype(jnp.float32)
    leading = (slot_ids == 0)[:, None]
    forward_imaginary = jnp.where(leading, (alternate * growth)[None, :], forward_imaginary)
    inverse_real = jnp.where(leading, 1.0, 2.0 * cosine)
    inverse_imaginary = jnp.where(leading, alternate[None, :], -2.0 * sines)
    forward = jnp.concatenate([forward_real, forward_imaginary], axis=0)
    inverse = jnp.concatenate([inverse_real, inverse_imaginary], axis=0).T
    inverse = inverse * (1.0 / (total_steps * growth))[:, None]
    return (forward, inverse)


def on_device(state, initial):
    steps_dev, fields, band_rows, columns = state.shape
    width_tm = lax.axis_size("tm")
    total_steps = steps_dev * width_tm
    previous = from_behind(state[-1], "tm", 1)
    previous = jnp.where(lax.axis_index("tm") == 0, initial, previous)
    before = jnp.concatenate([previous[None], state[:-1]], axis=0)
    padded = extended(state, (("space", 2),), 1)
    residual = state - before + tendency(padded)
    forward, inverse = time_tables(total_steps)
    slot_total = forward.shape[0] // 2
    per_device = slot_total // width_tm
    spectrum = jnp.einsum(
        "rj,jnc->rnc",
        forward,
        lax.all_to_all(
            residual.reshape(steps_dev, fields, band_rows * columns),
            "tm",
            split_axis=2,
            concat_axis=0,
            tiled=True,
        ),
        precision=highest,
    )
    spectrum = spectrum.reshape(2, slot_total, fields, spectrum.shape[-1])
    banded = lax.all_to_all(spectrum, "tm", split_axis=1, concat_axis=3, tiled=True).reshape(
        2, per_device, fields, band_rows, columns
    )
    slot_index = lax.axis_index("tm") * per_device + jnp.arange(per_device, dtype=jnp.int32)
    eigen, jacobi = slot_factors(slot_index, total_steps)
    weights = sweep_weights()
    iterate = weights[0] * pair_apply(jacobi, banded)
    for sweep in range(1, SWEEPS):
        border = extended(iterate, (("space", 3),), 1)
        applied = pair_apply(eigen, iterate) + linear_part(border)
        iterate = iterate + weights[sweep] * pair_apply(jacobi, banded - applied)
    flat_solution = iterate.reshape(2, per_device, fields, band_rows * columns)
    blocks = lax.all_to_all(flat_solution, "tm", split_axis=3, concat_axis=1, tiled=True)
    merged = blocks.reshape(2 * blocks.shape[1], blocks.shape[2], blocks.shape[3])
    all_steps = jnp.einsum("jr,rnc->jnc", inverse, merged, precision=highest)
    correction = lax.all_to_all(all_steps, "tm", split_axis=0, concat_axis=2, tiled=True)
    return state - correction.reshape(state.shape)


LANES = 128
HALO = SWEEPS
GROUP = 2 * HALO
ROW0 = 8
MAIN = ROW0 + HALO
SHIFT = 1.0 + 4.0 * viscous
RATE = 1.0 / SHIFT
VMEM_BYTES = 48 * 1024 * 1024
SLABS = 2
FIELDS = 3
EACH = [(f, c) for f in range(FIELDS) for c in range(SLABS)]


def fits_fast_plan(state, width_tm):
    steps_dev, fields, band_rows, columns = state.shape
    half = width_tm // 2
    steps = steps_dev * half
    return (
        width_tm > 1
        and width_tm & (width_tm - 1) == 0
        and columns == SLABS * LANES * half
        and SWEEPS * GROUP <= GROUP * steps <= LANES
        and LANES % (GROUP * steps_dev) == 0
        and band_rows % 8 == 0
        and band_rows >= 24
        and fields == FIELDS
    )


def lanes(rows=8):
    return lax.broadcasted_iota(jnp.int32, (rows, LANES), 1)


def step_of_lane(lane):
    return ((lane + HALO) & (LANES - 1)) // GROUP


def turn(values, shift):
    return pltpu.roll(values, shift % LANES, 1)


def tile_at(index):
    return pl.ds(pl.multiple_of(index * LANES, LANES), LANES)


def binomial(top, bottom):
    return float(math.comb(top, bottom))


def side_places(tile, width_tm):
    last = width_tm // 2 * SLABS - 1
    return tile_at((SLABS * tile + SLABS) & last), tile_at((SLABS * tile + last) & last)


def pack_kernel(width_tm, state_ref, *outs):
    steps_dev, fields, rows, _ = state_ref.shape
    half = width_tm // 2
    me = lax.axis_index("tm")
    lane = lanes()
    step = step_of_lane(lane)
    blocks = rows // 8
    per_word = LANES // (GROUP * steps_dev)
    for b, out in enumerate(outs):
        tile = (me ^ b) & (half - 1)
        after, prior = side_places(tile, width_tm)
        at = 0
        for c in range(SLABS):
            for i in range(steps_dev):
                for f in range(fields):
                    out[at : at + rows, :] = state_ref[i, f, :, tile_at(SLABS * tile + c)]
                    at += rows
        for first in range(0, fields * blocks, per_word):
            packed = jnp.zeros((8, LANES), jnp.float32)
            for g in range(first, min(first + per_word, fields * blocks)):
                f, r = divmod(g, blocks)
                for i in range(steps_dev):
                    slot = steps_dev * (g - first) + i
                    sides = jnp.where(
                        lane < LANES // 2,
                        state_ref[i, f, 8 * r : 8 * r + 8, after],
                        state_ref[i, f, 8 * r : 8 * r + 8, prior],
                    )
                    packed = jnp.where(step == slot, turn(sides, GROUP * slot), packed)
            out[at : at + 8, :] = packed
            at += 8


def place_initial(width_tm, initial_ref, _, tiles, side_initial):
    fields, rows, _ = initial_ref.shape
    mine = lax.axis_index("tm") & (width_tm // 2 - 1)
    after, prior = side_places(mine, width_tm)
    for f, c in EACH:
        tiles[f, c] = initial_ref[f, :, tile_at(SLABS * mine + c)]
    lane = lanes(rows)
    for f in range(fields):
        side_initial[f] = jnp.where(
            lane < LANES // 2, initial_ref[f, :, after], initial_ref[f, :, prior]
        )


def edge_kernel(width_tm, *refs):
    half = width_tm // 2
    pieces, (tiles, side, side_initial, up, down) = refs[:half], refs[half:]
    fields, rows, _ = side.shape
    main = pieces[0].shape[0] // rows * rows
    for out, part in ((up, slice(0, HALO)), (down, slice(rows - HALO, rows))):
        k = 0
        for b in range(half):
            for at in range(0, main, rows):
                out[k : k + HALO, :] = pieces[b][at + part.start : at + part.stop, :]
                k += HALO
        for c in range(SLABS):
            for f in range(fields):
                out[k : k + HALO, :] = tiles[f, c, part, :]
                k += HALO
        for held in (side, side_initial):
            for f in range(fields):
                out[k : k + HALO, :] = held[f, part, :]
                k += HALO


def full_tendency(own, east, west, north, south):
    e, u, v = own
    around = [east[f] + west[f] + (north[f] + south[f]) for f in range(FIELDS)]
    quarter = 0.5 * time_step
    flux = ((1.0 + east[0]) * east[1] - (1.0 + west[0]) * west[1]) + (
        (1.0 + south[0]) * south[2] - (1.0 + north[0]) * north[2]
    )
    carry1 = u * (east[1] - west[1]) + v * (south[1] - north[1]) + (east[0] - west[0])
    carry2 = u * (east[2] - west[2]) + v * (south[2] - north[2]) + (south[0] - north[0])
    diagonal = 1.0 + 4.0 * viscous
    return (
        diagonal * e + quarter * flux - viscous * around[0],
        diagonal * u + quarter * carry1 - coriolis * v - viscous * around[1],
        diagonal * v + quarter * carry2 + coriolis * u - viscous * around[2],
    )


def off_diagonal(own, east, west, north, south):
    _, u, v = own
    around = [east[f] + west[f] + (north[f] + south[f]) for f in range(FIELDS)]
    quarter = 0.5 * time_step
    return (
        viscous * around[0] - quarter * ((east[1] - west[1]) + (south[2] - north[2])),
        viscous * around[1] - quarter * (east[0] - west[0]) + coriolis * v,
        viscous * around[2] - quarter * (south[0] - north[0]) - coriolis * u,
    )


def chain_factors():
    gammas = []
    for weight in sweep_weights():
        shifted = [1.0] + gammas
        gammas = [weight * x for x in shifted]
        for i, x in enumerate(shifted[1:]):
            gammas[i] += (1.0 - weight) * x
    scale = RATE * gammas[-1]
    ratios = []
    for gamma in reversed(gammas[:-1]):
        ratios.append(gamma / scale)
        scale *= RATE
    return gammas, ratios, scale


def series_product(a, b):
    return [sum(a[i] * b[d - i] for i in range(d + 1)) for d in range(SWEEPS)]


def swap_factors(steps):
    hop = [RATE ** (steps + d) * binomial(steps - 1 + d, d) for d in range(SWEEPS)]
    lap = [circulant_alpha * x for x in series_product(hop, hop)]
    inverse = []
    for d in range(SWEEPS):
        value = (1.0 if d == 0 else 0.0) + sum(lap[i] * inverse[d - i] for i in range(1, d + 1))
        inverse.append(value / (1.0 - lap[0]))
    own = [circulant_alpha * x for x in series_product(inverse, hop)]
    return own, [circulant_alpha * x for x in inverse], inverse


class Side:
    def __init__(self, first, tall):
        self.first, self.tall = first, tall
        self.span = slice(first, first + tall)
        lane = lanes(self.tall)
        self.step = step_of_lane(lane)
        self.after = (lane & (GROUP - 1)) == 0
        self.before = (lane & (GROUP - 1)) == GROUP - 1

    def parts(self, held, ends):
        own, north, south = (
            [held[f, self.first + d : self.first + d + self.tall, :] for f in range(FIELDS)] for d in (0, -1, 1)
        )
        last = [ends[f, self.span, :] for f in range(FIELDS)]
        east = [jnp.where(self.before, turn(last[f], -1), turn(own[f], -1)) for f in range(FIELDS)]
        west = [jnp.where(self.after, turn(last[f], 1), turn(own[f], 1)) for f in range(FIELDS)]
        return own, east, west, north, south

    def set_seams(self, seams, values):
        for f in range(FIELDS):
            seams[f, self.span, :] = jnp.where(self.after, turn(values[f], 1), turn(values[f], -1))

    def product(self, values, matrix):
        done = jnp.dot(
            jnp.concatenate(values, axis=0),
            matrix,
            precision=highest,
            preferred_element_type=jnp.float32,
        )
        return [done[self.tall * f : self.tall * (f + 1), :] for f in range(FIELDS)]


def lane_matrix(entry):
    source = lax.broadcasted_iota(jnp.int32, (LANES, LANES), 0)
    target = lax.broadcasted_iota(jnp.int32, (LANES, LANES), 1)
    same = ((source - target) & (GROUP - 1)) == 0
    return jnp.where(same, entry(step_of_lane(source), step_of_lane(target)), 0.0)


def neighbours(held, slot, start, seam, n):
    lane = lanes()
    is_first, is_last = lane == 0, lane == LANES - 1
    load = lambda d: {k: held[slot, k[0], k[1], pl.ds(start + d, 8), :] for k in EACH}
    own, north, south = load(0), load(-1), load(1)
    east, west = {}, {}
    for f in range(FIELDS):
        across = turn(seam[f], -GROUP * n)
        back = [turn(own[f, c], -1) for c in range(SLABS)] + [across]
        ahead = [across] + [turn(own[f, c], 1) for c in range(SLABS)]
        for c in range(SLABS):
            east[f, c] = jnp.where(is_last, back[c + 1], back[c])
            west[f, c] = jnp.where(is_first, ahead[c], ahead[c + 1])
    return own, east, west, north, south


def slab(parts, c):
    return [[part[f, c] for f in range(FIELDS)] for part in parts]


def add_ends(last, own, n):
    lane = lanes()
    step = step_of_lane(lane)
    for f in range(FIELDS):
        both = jnp.where(lane < LANES // 2, own[f, 0], own[f, SLABS - 1])
        last[f] = jnp.where(step == n, turn(both, GROUP * n), last[f])


def zeros(count):
    return [jnp.zeros((8, LANES), jnp.float32)] * count


def residual_tile(steps, first_half, start, state, rhs, seams, ends, send):
    seam = [seams[f, pl.ds(start, 8), :] for f in range(FIELDS)]
    last = zeros(FIELDS)
    sums = {k: zeros(SWEEPS) for k in EACH}
    for n in range(steps):
        parts = neighbours(state, n + 1, start, seam, n)
        add_ends(last, parts[0], n)
        for c in range(SLABS):
            value = full_tendency(*slab(parts, c))
            for f in range(FIELDS):
                carry = (value[f] - state[n, f, c, pl.ds(start, 8), :]) * SHIFT**n
                rhs[n, f, c, pl.ds(start, 8), :] = carry
                for j in range(SWEEPS):
                    carry = sums[f, c][j] + carry
                    sums[f, c][j] = carry
    for f in range(FIELDS):
        ends[f, pl.ds(start, 8), :] = last[f]
    for f, c in EACH:
        for j in range(SWEEPS):
            value = sums[f, c][j] * RATE ** (steps + j)
            if j == 0:
                value = value - jnp.where(first_half, state[steps, f, c, pl.ds(start, 8), :], 0.0)
            send(SWEEPS - 1 - j, f, c, value)


PER_WORD = LANES // (SWEEPS * GROUP)


def pack_sides(blocks, sent, at):
    kind = step_of_lane(lanes()) // SWEEPS
    for first in range(0, len(blocks), PER_WORD):
        word = jnp.zeros((8, LANES), jnp.float32)
        for k, block in enumerate(blocks[first : first + PER_WORD]):
            word = jnp.where(kind == k, turn(block, SWEEPS * GROUP * k), word)
        sent[at : at + 8, :] = word
        at += 8


def unpack_side(sent, at, index):
    word, k = divmod(index, PER_WORD)
    value = turn(sent[at + 8 * word : at + 8 * word + 8, :], -SWEEPS * GROUP * k)
    return jnp.where(step_of_lane(lanes()) < SWEEPS, value, 0.0)


def side_residual(sides, steps, first_half, hstate, ends, before_first, hrhs):
    parts = sides.parts(hstate, ends)
    value = full_tendency(*parts)
    growth = jnp.where(
        sides.step < steps, jnp.exp(sides.step.astype(jnp.float32) * math.log(SHIFT)), 0.0
    )
    held = []
    for f in range(FIELDS):
        first = jnp.where(first_half, before_first(f), 0.0)
        before = jnp.where(sides.step == 0, first, turn(parts[0][f], GROUP))
        held.append((value[f] - before) * growth)
        hrhs[f, sides.span, :] = held[f]

    def entry(source, target):
        after = (steps - 1 - source).astype(jnp.float32)
        weight = jnp.full((LANES, LANES), RATE**steps, jnp.float32)
        result = jnp.zeros((LANES, LANES), jnp.float32)
        for j in range(1, SWEEPS + 1):
            result = jnp.where(target == SWEEPS - j, weight, result)
            weight = weight * (after + float(j)) * (RATE / j)
        return jnp.where(source < steps, result, 0.0)

    handed = sides.product(held, lane_matrix(entry))
    for f in range(FIELDS):
        last = turn(parts[0][f], GROUP * (SWEEPS - steps))
        handed[f] = handed[f] - jnp.where(first_half & (sides.step == SWEEPS - 1), last, 0.0)
    return handed


def inner_kernel(width_tm, steps_dev, *refs):
    half = width_tm // 2
    pieces, (tiles, side_initial) = refs[:half], refs[half : half + 2]
    state, rhs, ends, hrhs, side, sent, seams, hstate = refs[half + 2 :]
    fields, rows, _ = side.shape
    steps = half * steps_dev
    me = lax.axis_index("tm")
    mine = me & (half - 1)
    first_half = me < half
    body = slice(MAIN, MAIN + rows)
    for b in range(half):
        at = 0
        for c in range(SLABS):
            for i in range(steps_dev):
                n = steps_dev * (mine ^ b) + i
                for f in range(fields):
                    state[n + 1, f, c, body, :] = pieces[b][at : at + rows, :]
                    at += rows
    for f, c in EACH:
        state[0, f, c, body, :] = jnp.where(first_half, tiles[f, c], 0.0)
    owner = step_of_lane(lanes()) // steps_dev
    blocks = rows // 8
    per_word = LANES // (GROUP * steps_dev)
    main = SLABS * steps_dev * fields * rows
    for g in range(fields * blocks):
        f, r = divmod(g, blocks)
        word, place = divmod(g, per_word)
        found = jnp.zeros((8, LANES), jnp.float32)
        for b in range(half):
            source = mine ^ b
            value = pieces[b][main + 8 * word : main + 8 * word + 8, :]
            shift = (GROUP * steps_dev * (source - place)) & (LANES - 1)
            found = jnp.where(owner == source, pltpu.roll(value, shift, 1), found)
        side[f, 8 * r : 8 * r + 8, :] = found
        hstate[f, MAIN + 8 * r : MAIN + 8 * r + 8, :] = found
    Side(MAIN, rows).set_seams(seams, [side[f] for f in range(fields)])

    for t in range(1, blocks):

        def send(p, f, c, value):
            at = ((p * FIELDS + f) * SLABS + c) * (rows - 8) + 8 * t - 8
            sent[at : at + 8, :] = value

        residual_tile(steps, first_half, ROW0 + 8 * t, state, rhs, seams, ends, send)

    sides = Side(ROW0 + 8, rows - 8)
    before_first = lambda f: side_initial[f, HALO : rows - HALO, :]
    handed = side_residual(sides, steps, first_half, hstate, ends, before_first, hrhs)
    flat = [handed[f][at : at + 8, :] for f in range(FIELDS) for at in range(0, rows - 8, 8)]
    pack_sides(flat, sent, SWEEPS * FIELDS * SLABS * (rows - 8))


def outer_kernel(width_tm, steps_dev, rows, *refs):
    half = width_tm // 2
    side, side_initial, above, below = refs[4:8]
    state, rhs, ends, hrhs, sent, hstate, hbefore, seams = refs[8:]
    steps = half * steps_dev
    me = lax.axis_index("tm")
    mine = me & (half - 1)
    first_half = me < half
    body = slice(MAIN, MAIN + rows)
    top, bottom = slice(ROW0, MAIN), slice(MAIN + rows, MAIN + rows + HALO)
    k = 0
    for b in range(half):
        for c in range(SLABS):
            for i in range(steps_dev):
                n = steps_dev * (mine ^ b) + i
                for f in range(FIELDS):
                    state[n + 1, f, c, top, :] = above[k : k + HALO, :]
                    state[n + 1, f, c, bottom, :] = below[k : k + HALO, :]
                    k += HALO
    for c in range(SLABS):
        for f in range(FIELDS):
            state[0, f, c, top, :] = jnp.where(first_half, above[k : k + HALO, :], 0.0)
            state[0, f, c, bottom, :] = jnp.where(first_half, below[k : k + HALO, :], 0.0)
            k += HALO
    for held, given in ((hstate, side), (hbefore, side_initial)):
        for f in range(FIELDS):
            held[f, body, :] = given[f, :, :]
            held[f, top, :] = above[k : k + HALO, :]
            held[f, bottom, :] = below[k : k + HALO, :]
            k += HALO
    whole = Side(ROW0, rows + 2 * HALO)
    whole.set_seams(seams, [hstate[f, whole.span, :] for f in range(FIELDS)])
    flat = []
    for which, start in enumerate((ROW0, ROW0 + rows)):

        def send(p, f, c, value):
            at = (((p * FIELDS + f) * SLABS + c) * 2 + which) * 7
            sent[at : at + 7, :] = value[1 - which : 8 - which, :]

        residual_tile(steps, first_half, start, state, rhs, seams, ends, send)
        sides = Side(start, 8)
        before_first = lambda f: hbefore[f, start : start + 8, :]
        flat += side_residual(sides, steps, first_half, hstate, ends, before_first, hrhs)
    pack_sides(flat, sent, SWEEPS * FIELDS * SLABS * 14)


def chain_kernel(steps, rows, rhs, hrhs, result, ya, yb, hya, hyb, ends, seams):
    _, ratios, _ = chain_factors()
    sides = Side(ROW0, rows + 2 * HALO)
    blocks = sides.tall // 8
    running = lane_matrix(
        lambda source, target: jnp.where((source <= target) & (target < steps), 1.0, 0.0)
    )
    side_new = sides.product([hrhs[f, sides.span, :] for f in range(FIELDS)], running)
    for f in range(FIELDS):
        hya[f, sides.span, :] = side_new[f]
    sides.set_seams(seams, side_new)

    @pl.loop(0, blocks)
    def _(t):
        start = ROW0 + 8 * t
        for f, c in EACH:
            total = jnp.zeros((8, LANES), jnp.float32)
            for n in range(steps):
                total = total + rhs[n, f, c, pl.ds(start, 8), :]
                ya[n, f, c, pl.ds(start, 8), :] = total

    def sweep(ratio, old, hold, new, hnew, final):
        first = MAIN if final else ROW0

        @pl.loop(0, rows // 8 if final else blocks)
        def _(t):
            start = first + 8 * t
            seam = [seams[f, pl.ds(start, 8), :] for f in range(FIELDS)]
            last = zeros(FIELDS)
            total = dict(zip(EACH, zeros(len(EACH))))
            for n in range(steps):
                parts = neighbours(old, n, start, seam, n)
                if not final:
                    add_ends(last, parts[0], n)
                for c in range(SLABS):
                    value = off_diagonal(*slab(parts, c))
                    for f in range(FIELDS):
                        carry = value[f] + ratio * rhs[n, f, c, pl.ds(start, 8), :]
                        total[f, c] = total[f, c] + carry
                        if final:
                            at = pl.ds(pl.multiple_of(8 * t, 8), 8)
                            new[n, f, c, at, :] = total[f, c]
                        else:
                            new[n, f, c, pl.ds(start, 8), :] = total[f, c]
            if not final:
                for f in range(FIELDS):
                    ends[f, pl.ds(start, 8), :] = last[f]

        if not final:
            value = off_diagonal(*sides.parts(hold, ends))
            side_next = sides.product(
                [value[f] + ratio * hrhs[f, sides.span, :] for f in range(FIELDS)], running
            )
            for f in range(FIELDS):
                hnew[f, sides.span, :] = side_next[f]
            sides.set_seams(seams, side_next)

    buffers = [(ya, hya), (yb, hyb)]
    for m in range(1, SWEEPS):
        old, new = buffers[(m + 1) % 2], buffers[m % 2]
        final = m == SWEEPS - 1
        sweep(ratios[m - 1], *old, result if final else new[0], new[1], final)


def join_kernel(width_tm, steps_dev, rows, inner_rows, *refs):
    half = width_tm // 2
    count = 2 if inner_rows else 4
    given_refs, (chained, state) = refs[:count], refs[count : count + 2]
    outs = refs[-9 - half : -9]
    given, pa, pb, hgiven, hpa, hpb, ends, seams, result = refs[-9:]
    inner_own, inner_other = given_refs[:2]
    steps = half * steps_dev
    me = lax.axis_index("tm")
    mine = me & (half - 1)
    gammas, _, scale = chain_factors()
    own, first, second = swap_factors(steps)
    other = [jnp.where(me < half, a, b) for a, b in zip(first, second)]
    tiles = rows // 8
    if inner_rows:
        sides = Side(ROW0 + 8, rows - 8)
        places = (tiles - 1, lambda t: ROW0 + 8 + 8 * t)
        finals = (tiles - 2, lambda t: MAIN + 8 + 8 * t)
    else:
        sides = Side(ROW0, rows + 2 * HALO)
        places = (4, lambda t: ROW0 + 8 * (t + (tiles - 3) * (t // 2)))
        finals = (2, lambda t: MAIN + (rows - 8) * t)
    cells = SWEEPS * FIELDS * SLABS

    def joined(ref_own, ref_other, at, size, step, p):
        total = None
        for d in range(SWEEPS - p):
            rows_d = slice(at + step * d, at + step * d + size)
            term = other[d] * ref_other[rows_d, :] + own[d] * ref_own[rows_d, :]
            total = term if total is None else total + term
        return total

    for p in range(SWEEPS):
        for f, c in EACH:
            cell = (p * FIELDS + f) * SLABS + c
            found = [(ROW0 + 8, joined(inner_own, inner_other, cell * (rows - 8), rows - 8, FIELDS * SLABS * (rows - 8), p))]
            if not inner_rows:
                for which, start in ((0, ROW0 + 1), (1, ROW0 + rows)):
                    at = (cell * 2 + which) * 7
                    found.append((start, joined(*given_refs[2:], at, 7, FIELDS * SLABS * 14, p)))
            for start, value in found:
                given[p, f, c, start : start + value.shape[0], :] = value
                pa[p, f, c, start : start + value.shape[0], :] = gammas[-1] * value

    step8 = step_of_lane(lanes())

    def from_later(value, d, step):
        return jnp.where(step < SWEEPS - d, turn(value, -GROUP * d), 0.0)

    def set_side(refs_side, at, index, f, start):
        ours, theirs = (unpack_side(ref, at, index) for ref in refs_side)
        value = jnp.zeros((8, LANES), jnp.float32)
        for d in range(SWEEPS):
            value = value + from_later(other[d] * theirs + own[d] * ours, d, step8)
        hgiven[f, start : start + 8, :] = value
        hpa[f, start : start + 8, :] = gammas[-1] * value

    for f in range(FIELDS):
        for r in range(tiles - 1):
            set_side(given_refs[:2], cells * (rows - 8), f * (tiles - 1) + r, f, ROW0 + 8 + 8 * r)
        if not inner_rows:
            for which, start in ((0, ROW0), (1, ROW0 + rows)):
                set_side(given_refs[2:], cells * 14, which * FIELDS + f, f, start)
    sides.set_seams(seams, [hpa[f, sides.span, :] for f in range(FIELDS)])

    buffers = [(pa, hpa), (pb, hpb)]
    for k in range(1, SWEEPS):
        (old, hold), (new, hnew) = buffers[(k + 1) % 2], buffers[k % 2]
        gamma = gammas[SWEEPS - 1 - k]
        final = k == SWEEPS - 1
        turns, place = finals if final else places

        for t in range(turns):
            start = place(t)
            here = pl.ds(start, 8)
            seam = [seams[f, here, :] for f in range(FIELDS)]
            last = zeros(FIELDS)
            found = {}
            for p in range(SWEEPS):
                parts = neighbours(old, p, start, seam, p)
                if not final:
                    add_ends(last, parts[0], p)
                for c in range(SLABS):
                    value = off_diagonal(*slab(parts, c))
                    for f in range(FIELDS):
                        total = value[f]
                        if p + k < SWEEPS:
                            total = total + gamma * given[p + k, f, c, here, :]
                        if final:
                            found[p, f, c] = total * RATE ** (p + 1)
                        else:
                            new[p, f, c, here, :] = total
            if not final:
                for f in range(FIELDS):
                    ends[f, here, :] = last[f]
            else:
                at = pl.ds(8 * t, 8)
                from_chain = pl.ds(start - MAIN, 8)
                for f, c in EACH:
                    for n in range(steps):
                        total = scale * chained[n, f, c, from_chain, :]
                        for p in range(SWEEPS):
                            total = total + binomial(n + p, p) * found[p, f, c]
                        result[n, f, c, at, :] = state[n + 1, f, c, here, :] - total * RATE**n

        if not final:
            value = off_diagonal(*sides.parts(hold, ends))
            side_next = [
                value[f] + gamma * from_later(hgiven[f, sides.span, :], k, sides.step)
                for f in range(FIELDS)
            ]
            for f in range(FIELDS):
                hnew[f, sides.span, :] = side_next[f]
            sides.set_seams(seams, side_next)

    size = 8 * finals[0]
    for b in range(half):
        at = 0
        for c in range(SLABS):
            for i in range(steps_dev):
                n = steps_dev * (mine ^ b) + i
                for f in range(FIELDS):
                    outs[b][at : at + size, :] = result[n, f, c, :, :]
                    at += size


def unpack_kernel(width_tm, *refs):
    half = width_tm // 2
    inner, outer, out = refs[:half], refs[half : 2 * half], refs[2 * half]
    steps_dev, fields, rows, _ = out.shape
    mine = lax.axis_index("tm") & (half - 1)
    size = rows - 16
    for b in range(half):
        k = 0
        for c in range(SLABS):
            here = tile_at(SLABS * (mine ^ b) + c)
            for i in range(steps_dev):
                for f in range(fields):
                    out[i, f, 8 : rows - 8, here] = inner[b][size * k : size * (k + 1), :]
                    out[i, f, 0:8, here] = outer[b][16 * k : 16 * k + 8, :]
                    out[i, f, rows - 8 : rows, here] = outer[b][16 * k + 8 : 16 * k + 16, :]
                    k += 1


def call(kernel, out_shapes, operands, scratch=(), aliases=None, after=()):
    whole = pl.BlockSpec(memory_space=pltpu.VMEM)
    shapes = [jax.ShapeDtypeStruct(shape, jnp.float32) for shape in out_shapes]
    moved = 4 * sum(math.prod(x.shape) for x in list(shapes) + list(operands))
    in_specs = [whole] * len(operands) + [pl.BlockSpec(memory_space=pl.ANY)] * len(after)
    operands = list(operands) + list(after)
    return pl.pallas_call(
        kernel,
        out_shape=shapes,
        in_specs=in_specs,
        out_specs=[whole] * len(shapes),
        scratch_shapes=[pltpu.VMEM(shape, jnp.float32) for shape in scratch],
        input_output_aliases=aliases or {},
        compiler_params=pltpu.CompilerParams(vmem_limit_bytes=VMEM_BYTES),
        cost_estimate=pl.CostEstimate(flops=moved, bytes_accessed=moved, transcendentals=0),
    )(*operands)


def swap(piece, b):
    count = lax.axis_size("tm")
    return lax.ppermute(piece, "tm", [(k, k ^ b) for k in range(count)])


def fast_on_device(state, initial):
    steps_dev, fields, rows, columns = state.shape
    width_tm = lax.axis_size("tm")
    bands = lax.axis_size("space")
    half = width_tm // 2
    steps = steps_dev * half
    main = SLABS * steps_dev * fields * rows
    words = -(-fields * rows // 8 // (LANES // (GROUP * steps_dev)))
    tall = rows + 2 * HALO + 2 * ROW0
    sized = (width_tm, steps_dev)
    pieces = call(
        functools.partial(pack_kernel, width_tm), [(main + 8 * words, LANES)] * half, [state]
    )
    pieces = [pieces[0]] + [swap(pieces[b], b) for b in range(1, half)]
    tiles, side_initial = call(
        functools.partial(place_initial, width_tm),
        [(fields, SLABS, rows, LANES), (fields, rows, LANES)],
        [initial],
        after=pieces[:1],
    )
    flat = (fields, tall, LANES)
    held_shapes = [
        (steps + 1, fields, SLABS, tall, LANES),
        (steps, fields, SLABS, tall, LANES),
        flat,
        flat,
    ]
    cells = SWEEPS * fields * SLABS
    inner_words = -(-fields * (rows - 8) // 8 // PER_WORD)
    outer_words = -(-2 * fields // PER_WORD)
    *held, side, inner = call(
        functools.partial(inner_kernel, *sized),
        held_shapes
        + [(fields, rows, LANES), (cells * (rows - 8) + 8 * inner_words, LANES)],
        pieces + [tiles, side_initial],
        [flat] * 2,
    )
    inner_other = swap(inner, half)
    edge_rows = -(-HALO * fields * (SLABS * (steps + 1) + 2) // 8) * 8
    up, down = call(
        functools.partial(edge_kernel, width_tm),
        [(edge_rows, LANES)] * 2,
        pieces + [tiles, side, side_initial],
    )
    above = lax.ppermute(down, "space", [(i, (i + 1) % bands) for i in range(bands)])
    below = lax.ppermute(up, "space", [((i + 1) % bands, i) for i in range(bands)])
    solved, rhs, _, hrhs, outer = call(
        functools.partial(outer_kernel, *sized, rows),
        held_shapes + [(cells * 14 + 8 * outer_words, LANES)],
        held + [side, side_initial, above, below],
        [flat] * 3,
        aliases={0: 0, 1: 1, 2: 2, 3: 3},
    )
    outer_other = swap(outer, half)
    (chained,) = call(
        functools.partial(chain_kernel, steps, rows),
        [(steps, fields, SLABS, rows, LANES)],
        [rhs, hrhs],
        [held_shapes[1]] * 2 + [flat] * 4,
    )
    four = (SWEEPS, fields, SLABS, tall, LANES)
    results = []
    for given, size in (
        ([inner, inner_other], rows - 16),
        ([inner, inner_other, outer, outer_other], 16),
    ):
        parts = call(
            functools.partial(join_kernel, *sized, rows, len(given) == 2),
            [(SLABS * steps_dev * fields * size, LANES)] * half,
            given + [chained, solved],
            [four] * 3 + [flat] * 5 + [(steps, fields, SLABS, size, LANES)],
            after=results[:1],
        )
        results += [parts[0]] + [swap(parts[b], b) for b in range(1, half)]
    (updated,) = call(functools.partial(unpack_kernel, width_tm), [state.shape], results)
    return updated


def choose(state, initial):
    if fits_fast_plan(state, lax.axis_size("tm")):
        return fast_on_device(state, initial)
    return on_device(state, initial)


def solution(mesh):
    in_specs = (P("tm", None, "space", None), P(None, "space", None))
    out_specs = P("tm", None, "space", None)
    return jax.shard_map(
        choose, mesh=mesh, in_specs=in_specs, out_specs=out_specs, check_vma=False
    )
```

```python
import functools
import math

import jax
import jax.numpy as jnp
from jax import lax
from jax.experimental import pallas as pl
from jax.experimental.pallas import tpu as pltpu
from jax.sharding import PartitionSpec as P

SWEEPS = 4


circulant_alpha = 0.1
time_step = 0.5
coriolis = 0.3
viscous = 0.2
highest = lax.Precision.HIGHEST


def from_behind(block, axis, distance):
    devices = range(lax.axis_size(axis))
    route = [(i - distance, i) for i in devices if i - distance in devices]
    return lax.ppermute(block, axis, route)


def extended(cells, sides, width):
    for axis, dim in sides:
        count = lax.axis_size(axis)
        head = lax.slice_in_dim(cells, 0, width, axis=dim)
        tail = lax.slice_in_dim(cells, cells.shape[dim] - width, cells.shape[dim], axis=dim)
        cells = jnp.concatenate(
            [
                lax.ppermute(tail, axis, [(i, (i + 1) % count) for i in range(count)]),
                cells,
                lax.ppermute(head, axis, [((i + 1) % count, i) for i in range(count)]),
            ],
            axis=dim,
        )
    return cells


def interior(values):
    return values[..., 1:-1, :]


def column_diff(values):
    return 0.5 * (jnp.roll(values, -1, axis=-1) - jnp.roll(values, 1, axis=-1))[..., 1:-1, :]


def row_diff(values):
    return 0.5 * (values[..., 2:, :] - values[..., :-2, :])


def laplace(values):
    return (
        values[..., 2:, :]
        + values[..., :-2, :]
        + jnp.roll(values, -1, axis=-1)[..., 1:-1, :]
        + jnp.roll(values, 1, axis=-1)[..., 1:-1, :]
        - 4.0 * values[..., 1:-1, :]
    )


def tendency(padded):
    surface = padded[..., 0, :, :]
    eastward = padded[..., 1, :, :]
    northward = padded[..., 2, :, :]
    column_depth = 1.0 + surface
    east_inner = interior(eastward)
    north_inner = interior(northward)
    mass_change = time_step * (
        column_diff(column_depth * eastward) + row_diff(column_depth * northward)
    ) - viscous * laplace(surface)
    east_change = (
        time_step
        * (
            east_inner * column_diff(eastward)
            + north_inner * row_diff(eastward)
            + column_diff(surface)
        )
        - coriolis * north_inner
        - viscous * laplace(eastward)
    )
    north_change = (
        time_step
        * (
            east_inner * column_diff(northward)
            + north_inner * row_diff(northward)
            + row_diff(surface)
        )
        + coriolis * east_inner
        - viscous * laplace(northward)
    )
    return jnp.stack([mass_change, east_change, north_change], axis=-3)


def linear_part(padded):
    surface = padded[..., 0, :, :]
    eastward = padded[..., 1, :, :]
    northward = padded[..., 2, :, :]
    mass_change = time_step * (column_diff(eastward) + row_diff(northward)) - viscous * laplace(
        surface
    )
    east_change = (
        time_step * column_diff(surface)
        - coriolis * interior(northward)
        - viscous * laplace(eastward)
    )
    north_change = (
        time_step * row_diff(surface) + coriolis * interior(eastward) - viscous * laplace(northward)
    )
    return jnp.stack([mass_change, east_change, north_change], axis=-3)


def pair_apply(factors, values):
    factor = factors[:, :, None, None, None]
    return jnp.stack(
        [
            factor[0] * values[0] - factor[1] * values[1],
            factor[2] * values[1] + factor[3] * values[0],
        ]
    )


def sweep_weights():
    return [
        1.0 / (1.15 - 0.85 * math.cos(math.pi * (2 * sweep + 1) / (2 * SWEEPS)))
        for sweep in range(SWEEPS)
    ]


def slot_factors(slot_index, total_steps):
    decay_base = circulant_alpha ** (1.0 / total_steps)
    angles = 2.0 * math.pi / total_steps * slot_index.astype(jnp.float32)
    real_eigen = 1.0 - decay_base * jnp.cos(angles)
    imaginary_eigen = decay_base * jnp.sin(angles)
    real_shift = real_eigen + 4.0 * viscous
    modulus = real_shift * real_shift + imaginary_eigen * imaginary_eigen
    eigen = jnp.stack([real_eigen, imaginary_eigen, real_eigen, imaginary_eigen])
    jacobi = jnp.stack(
        [
            real_shift / modulus,
            -imaginary_eigen / modulus,
            real_shift / modulus,
            -imaginary_eigen / modulus,
        ]
    )
    leading = (slot_index == 0)[None, :]
    zero_part = jnp.zeros_like(real_eigen)
    packed_eigen = jnp.stack(
        [zero_part + (1.0 - decay_base), zero_part, zero_part + (1.0 + decay_base), zero_part]
    )
    packed_jacobi = jnp.stack(
        [
            zero_part + 1.0 / (1.0 - decay_base + 4.0 * viscous),
            zero_part,
            zero_part + 1.0 / (1.0 + decay_base + 4.0 * viscous),
            zero_part,
        ]
    )
    eigen = jnp.where(leading, packed_eigen, eigen)
    jacobi = jnp.where(leading, packed_jacobi, jacobi)
    return (eigen, jacobi)


def time_tables(total_steps):
    slot_total = total_steps // 2
    step_ids = jnp.arange(total_steps, dtype=jnp.int32)
    slot_ids = jnp.arange(slot_total, dtype=jnp.int32)
    phase = slot_ids[:, None] * step_ids[None, :] % total_steps
    angles = 2.0 * math.pi / total_steps * phase.astype(jnp.float32)
    decay_base = circulant_alpha ** (1.0 / total_steps)
    growth = decay_base ** step_ids.astype(jnp.float32)
    cosine = jnp.cos(angles)
    sines = jnp.sin(angles)
    forward_real = cosine * growth[None, :]
    forward_imaginary = -sines * growth[None, :]
    inverse_imaginary = -sines
    alternate = 1.0 - 2.0 * (step_ids % 2).astype(jnp.float32)
    leading = (slot_ids == 0)[:, None]
    forward_imaginary = jnp.where(leading, (alternate * growth)[None, :], forward_imaginary)
    inverse_real = jnp.where(leading, 1.0, 2.0 * cosine)
    inverse_imaginary = jnp.where(leading, alternate[None, :], -2.0 * sines)
    forward = jnp.concatenate([forward_real, forward_imaginary], axis=0)
    inverse = jnp.concatenate([inverse_real, inverse_imaginary], axis=0).T
    inverse = inverse * (1.0 / (total_steps * growth))[:, None]
    return (forward, inverse)


def on_device(state, initial):
    steps_dev, fields, band_rows, columns = state.shape
    width_tm = lax.axis_size("tm")
    total_steps = steps_dev * width_tm
    previous = from_behind(state[-1], "tm", 1)
    previous = jnp.where(lax.axis_index("tm") == 0, initial, previous)
    before = jnp.concatenate([previous[None], state[:-1]], axis=0)
    padded = extended(state, (("space", 2),), 1)
    residual = state - before + tendency(padded)
    forward, inverse = time_tables(total_steps)
    slot_total = forward.shape[0] // 2
    per_device = slot_total // width_tm
    spectrum = jnp.einsum(
        "rj,jnc->rnc",
        forward,
        lax.all_to_all(
            residual.reshape(steps_dev, fields, band_rows * columns),
            "tm",
            split_axis=2,
            concat_axis=0,
            tiled=True,
        ),
        precision=highest,
    )
    spectrum = spectrum.reshape(2, slot_total, fields, spectrum.shape[-1])
    banded = lax.all_to_all(spectrum, "tm", split_axis=1, concat_axis=3, tiled=True).reshape(
        2, per_device, fields, band_rows, columns
    )
    slot_index = lax.axis_index("tm") * per_device + jnp.arange(per_device, dtype=jnp.int32)
    eigen, jacobi = slot_factors(slot_index, total_steps)
    weights = sweep_weights()
    iterate = weights[0] * pair_apply(jacobi, banded)
    for sweep in range(1, SWEEPS):
        border = extended(iterate, (("space", 3),), 1)
        applied = pair_apply(eigen, iterate) + linear_part(border)
        iterate = iterate + weights[sweep] * pair_apply(jacobi, banded - applied)
    flat_solution = iterate.reshape(2, per_device, fields, band_rows * columns)
    blocks = lax.all_to_all(flat_solution, "tm", split_axis=3, concat_axis=1, tiled=True)
    merged = blocks.reshape(2 * blocks.shape[1], blocks.shape[2], blocks.shape[3])
    all_steps = jnp.einsum("jr,rnc->jnc", inverse, merged, precision=highest)
    correction = lax.all_to_all(all_steps, "tm", split_axis=0, concat_axis=2, tiled=True)
    return state - correction.reshape(state.shape)


LANES = 128
HALO = SWEEPS
GROUP = 2 * HALO
ROW0 = 8
MAIN = ROW0 + HALO
SHIFT = 1.0 + 4.0 * viscous
RATE = 1.0 / SHIFT
VMEM_BYTES = 48 * 1024 * 1024
SLABS = 2
FIELDS = 3
EACH = [(f, c) for f in range(FIELDS) for c in range(SLABS)]


def fits_fast_plan(state, width_tm):
    steps_dev, fields, band_rows, columns = state.shape
    half = width_tm // 2
    steps = steps_dev * half
    return (
        width_tm > 1
        and width_tm & (width_tm - 1) == 0
        and columns == SLABS * LANES * half
        and SWEEPS * GROUP <= GROUP * steps <= LANES
        and LANES % (GROUP * steps_dev) == 0
        and band_rows % 8 == 0
        and band_rows >= 24
        and fields == FIELDS
    )


def lanes(rows=8):
    return lax.broadcasted_iota(jnp.int32, (rows, LANES), 1)


def step_of_lane(lane):
    return ((lane + HALO) & (LANES - 1)) // GROUP


def turn(values, shift):
    return pltpu.roll(values, shift % LANES, 1)


def tile_at(index):
    return pl.ds(pl.multiple_of(index * LANES, LANES), LANES)


def binomial(top, bottom):
    return float(math.comb(top, bottom))


def side_places(tile, width_tm):
    last = width_tm // 2 * SLABS - 1
    return tile_at((SLABS * tile + SLABS) & last), tile_at((SLABS * tile + last) & last)


def pack_kernel(width_tm, state_ref, *outs):
    steps_dev, fields, rows, _ = state_ref.shape
    half = width_tm // 2
    me = lax.axis_index("tm")
    lane = lanes()
    step = step_of_lane(lane)
    blocks = rows // 8
    per_word = LANES // (GROUP * steps_dev)
    for b, out in enumerate(outs):
        tile = (me ^ b) & (half - 1)
        after, prior = side_places(tile, width_tm)
        at = 0
        for c in range(SLABS):
            for i in range(steps_dev):
                for f in range(fields):
                    out[at : at + rows, :] = state_ref[i, f, :, tile_at(SLABS * tile + c)]
                    at += rows
        for first in range(0, fields * blocks, per_word):
            packed = jnp.zeros((8, LANES), jnp.float32)
            for g in range(first, min(first + per_word, fields * blocks)):
                f, r = divmod(g, blocks)
                for i in range(steps_dev):
                    slot = steps_dev * (g - first) + i
                    sides = jnp.where(
                        lane < LANES // 2,
                        state_ref[i, f, 8 * r : 8 * r + 8, after],
                        state_ref[i, f, 8 * r : 8 * r + 8, prior],
                    )
                    packed = jnp.where(step == slot, turn(sides, GROUP * slot), packed)
            out[at : at + 8, :] = packed
            at += 8


def place_initial(width_tm, initial_ref, _, tiles, side_initial):
    fields, rows, _ = initial_ref.shape
    mine = lax.axis_index("tm") & (width_tm // 2 - 1)
    after, prior = side_places(mine, width_tm)
    for f, c in EACH:
        tiles[f, c] = initial_ref[f, :, tile_at(SLABS * mine + c)]
    lane = lanes(rows)
    for f in range(fields):
        side_initial[f] = jnp.where(
            lane < LANES // 2, initial_ref[f, :, after], initial_ref[f, :, prior]
        )


def edge_kernel(width_tm, *refs):
    half = width_tm // 2
    pieces, (tiles, side, side_initial, up, down) = refs[:half], refs[half:]
    fields, rows, _ = side.shape
    main = pieces[0].shape[0] // rows * rows
    for out, part in ((up, slice(0, HALO)), (down, slice(rows - HALO, rows))):
        k = 0
        for b in range(half):
            for at in range(0, main, rows):
                out[k : k + HALO, :] = pieces[b][at + part.start : at + part.stop, :]
                k += HALO
        for c in range(SLABS):
            for f in range(fields):
                out[k : k + HALO, :] = tiles[f, c, part, :]
                k += HALO
        for held in (side, side_initial):
            for f in range(fields):
                out[k : k + HALO, :] = held[f, part, :]
                k += HALO


def full_tendency(own, east, west, north, south):
    e, u, v = own
    around = [east[f] + west[f] + (north[f] + south[f]) for f in range(FIELDS)]
    quarter = 0.5 * time_step
    flux = ((1.0 + east[0]) * east[1] - (1.0 + west[0]) * west[1]) + (
        (1.0 + south[0]) * south[2] - (1.0 + north[0]) * north[2]
    )
    carry1 = u * (east[1] - west[1]) + v * (south[1] - north[1]) + (east[0] - west[0])
    carry2 = u * (east[2] - west[2]) + v * (south[2] - north[2]) + (south[0] - north[0])
    diagonal = 1.0 + 4.0 * viscous
    return (
        diagonal * e + quarter * flux - viscous * around[0],
        diagonal * u + quarter * carry1 - coriolis * v - viscous * around[1],
        diagonal * v + quarter * carry2 + coriolis * u - viscous * around[2],
    )


def off_diagonal(own, east, west, north, south):
    _, u, v = own
    around = [east[f] + west[f] + (north[f] + south[f]) for f in range(FIELDS)]
    quarter = 0.5 * time_step
    return (
        viscous * around[0] - quarter * ((east[1] - west[1]) + (south[2] - north[2])),
        viscous * around[1] - quarter * (east[0] - west[0]) + coriolis * v,
        viscous * around[2] - quarter * (south[0] - north[0]) - coriolis * u,
    )


def chain_factors():
    gammas = []
    for weight in sweep_weights():
        shifted = [1.0] + gammas
        gammas = [weight * x for x in shifted]
        for i, x in enumerate(shifted[1:]):
            gammas[i] += (1.0 - weight) * x
    scale = RATE * gammas[-1]
    ratios = []
    for gamma in reversed(gammas[:-1]):
        ratios.append(gamma / scale)
        scale *= RATE
    return gammas, ratios, scale


def series_product(a, b):
    return [sum(a[i] * b[d - i] for i in range(d + 1)) for d in range(SWEEPS)]


def swap_factors(steps):
    hop = [RATE ** (steps + d) * binomial(steps - 1 + d, d) for d in range(SWEEPS)]
    lap = [circulant_alpha * x for x in series_product(hop, hop)]
    inverse = []
    for d in range(SWEEPS):
        value = (1.0 if d == 0 else 0.0) + sum(lap[i] * inverse[d - i] for i in range(1, d + 1))
        inverse.append(value / (1.0 - lap[0]))
    own = [circulant_alpha * x for x in series_product(inverse, hop)]
    return own, [circulant_alpha * x for x in inverse], inverse


class Side:
    def __init__(self, first, tall):
        self.first, self.tall = first, tall
        self.span = slice(first, first + tall)
        lane = lanes(self.tall)
        self.step = step_of_lane(lane)
        self.after = (lane & (GROUP - 1)) == 0
        self.before = (lane & (GROUP - 1)) == GROUP - 1

    def parts(self, held, ends):
        own, north, south = (
            [held[f, self.first + d : self.first + d + self.tall, :] for f in range(FIELDS)] for d in (0, -1, 1)
        )
        last = [ends[f, self.span, :] for f in range(FIELDS)]
        east = [jnp.where(self.before, turn(last[f], -1), turn(own[f], -1)) for f in range(FIELDS)]
        west = [jnp.where(self.after, turn(last[f], 1), turn(own[f], 1)) for f in range(FIELDS)]
        return own, east, west, north, south

    def set_seams(self, seams, values):
        for f in range(FIELDS):
            seams[f, self.span, :] = jnp.where(self.after, turn(values[f], 1), turn(values[f], -1))

    def product(self, values, matrix):
        done = jnp.dot(
            jnp.concatenate(values, axis=0),
            matrix,
            precision=highest,
            preferred_element_type=jnp.float32,
        )
        return [done[self.tall * f : self.tall * (f + 1), :] for f in range(FIELDS)]


def lane_matrix(entry):
    source = lax.broadcasted_iota(jnp.int32, (LANES, LANES), 0)
    target = lax.broadcasted_iota(jnp.int32, (LANES, LANES), 1)
    same = ((source - target) & (GROUP - 1)) == 0
    return jnp.where(same, entry(step_of_lane(source), step_of_lane(target)), 0.0)


def neighbours(held, slot, start, seam, n):
    lane = lanes()
    is_first, is_last = lane == 0, lane == LANES - 1
    load = lambda d: {k: held[slot, k[0], k[1], pl.ds(start + d, 8), :] for k in EACH}
    own, north, south = load(0), load(-1), load(1)
    east, west = {}, {}
    for f in range(FIELDS):
        across = turn(seam[f], -GROUP * n)
        back = [turn(own[f, c], -1) for c in range(SLABS)] + [across]
        ahead = [across] + [turn(own[f, c], 1) for c in range(SLABS)]
        for c in range(SLABS):
            east[f, c] = jnp.where(is_last, back[c + 1], back[c])
            west[f, c] = jnp.where(is_first, ahead[c], ahead[c + 1])
    return own, east, west, north, south


def slab(parts, c):
    return [[part[f, c] for f in range(FIELDS)] for part in parts]


def add_ends(last, own, n):
    lane = lanes()
    step = step_of_lane(lane)
    for f in range(FIELDS):
        both = jnp.where(lane < LANES // 2, own[f, 0], own[f, SLABS - 1])
        last[f] = jnp.where(step == n, turn(both, GROUP * n), last[f])


def zeros(count):
    return [jnp.zeros((8, LANES), jnp.float32)] * count


def residual_tile(steps, first_half, start, state, rhs, seams, ends, send):
    seam = [seams[f, pl.ds(start, 8), :] for f in range(FIELDS)]
    last = zeros(FIELDS)
    sums = {k: zeros(SWEEPS) for k in EACH}
    for n in range(steps):
        parts = neighbours(state, n + 1, start, seam, n)
        add_ends(last, parts[0], n)
        for c in range(SLABS):
            value = full_tendency(*slab(parts, c))
            for f in range(FIELDS):
                carry = (value[f] - state[n, f, c, pl.ds(start, 8), :]) * SHIFT**n
                rhs[n, f, c, pl.ds(start, 8), :] = carry
                for j in range(SWEEPS):
                    carry = sums[f, c][j] + carry
                    sums[f, c][j] = carry
    for f in range(FIELDS):
        ends[f, pl.ds(start, 8), :] = last[f]
    for f, c in EACH:
        for j in range(SWEEPS):
            value = sums[f, c][j] * RATE ** (steps + j)
            if j == 0:
                value = value - jnp.where(first_half, state[steps, f, c, pl.ds(start, 8), :], 0.0)
            send(SWEEPS - 1 - j, f, c, value)


PER_WORD = LANES // (SWEEPS * GROUP)


def pack_sides(blocks, sent, at):
    kind = step_of_lane(lanes()) // SWEEPS
    for first in range(0, len(blocks), PER_WORD):
        word = jnp.zeros((8, LANES), jnp.float32)
        for k, block in enumerate(blocks[first : first + PER_WORD]):
            word = jnp.where(kind == k, turn(block, SWEEPS * GROUP * k), word)
        sent[at : at + 8, :] = word
        at += 8


def unpack_side(sent, at, index):
    word, k = divmod(index, PER_WORD)
    value = turn(sent[at + 8 * word : at + 8 * word + 8, :], -SWEEPS * GROUP * k)
    return jnp.where(step_of_lane(lanes()) < SWEEPS, value, 0.0)


def side_residual(sides, steps, first_half, hstate, ends, before_first, hrhs):
    parts = sides.parts(hstate, ends)
    value = full_tendency(*parts)
    growth = jnp.where(
        sides.step < steps, jnp.exp(sides.step.astype(jnp.float32) * math.log(SHIFT)), 0.0
    )
    held = []
    for f in range(FIELDS):
        first = jnp.where(first_half, before_first(f), 0.0)
        before = jnp.where(sides.step == 0, first, turn(parts[0][f], GROUP))
        held.append((value[f] - before) * growth)
        hrhs[f, sides.span, :] = held[f]

    def entry(source, target):
        after = (steps - 1 - source).astype(jnp.float32)
        weight = jnp.full((LANES, LANES), RATE**steps, jnp.float32)
        result = jnp.zeros((LANES, LANES), jnp.float32)
        for j in range(1, SWEEPS + 1):
            result = jnp.where(target == SWEEPS - j, weight, result)
            weight = weight * (after + float(j)) * (RATE / j)
        return jnp.where(source < steps, result, 0.0)

    handed = sides.product(held, lane_matrix(entry))
    for f in range(FIELDS):
        last = turn(parts[0][f], GROUP * (SWEEPS - steps))
        handed[f] = handed[f] - jnp.where(first_half & (sides.step == SWEEPS - 1), last, 0.0)
    return handed


def inner_kernel(width_tm, steps_dev, *refs):
    half = width_tm // 2
    pieces, (tiles, side_initial) = refs[:half], refs[half : half + 2]
    state, rhs, ends, hrhs, side, sent, seams, hstate = refs[half + 2 :]
    fields, rows, _ = side.shape
    steps = half * steps_dev
    me = lax.axis_index("tm")
    mine = me & (half - 1)
    first_half = me < half
    body = slice(MAIN, MAIN + rows)
    for b in range(half):
        at = 0
        for c in range(SLABS):
            for i in range(steps_dev):
                n = steps_dev * (mine ^ b) + i
                for f in range(fields):
                    state[n + 1, f, c, body, :] = pieces[b][at : at + rows, :]
                    at += rows
    for f, c in EACH:
        state[0, f, c, body, :] = jnp.where(first_half, tiles[f, c], 0.0)
    owner = step_of_lane(lanes()) // steps_dev
    blocks = rows // 8
    per_word = LANES // (GROUP * steps_dev)
    main = SLABS * steps_dev * fields * rows
    for g in range(fields * blocks):
        f, r = divmod(g, blocks)
        word, place = divmod(g, per_word)
        found = jnp.zeros((8, LANES), jnp.float32)
        for b in range(half):
            source = mine ^ b
            value = pieces[b][main + 8 * word : main + 8 * word + 8, :]
            shift = (GROUP * steps_dev * (source - place)) & (LANES - 1)
            found = jnp.where(owner == source, pltpu.roll(value, shift, 1), found)
        side[f, 8 * r : 8 * r + 8, :] = found
        hstate[f, MAIN + 8 * r : MAIN + 8 * r + 8, :] = found
    Side(MAIN, rows).set_seams(seams, [side[f] for f in range(fields)])

    for t in range(1, blocks):

        def send(p, f, c, value):
            at = ((p * FIELDS + f) * SLABS + c) * (rows - 8) + 8 * t - 8
            sent[at : at + 8, :] = value

        residual_tile(steps, first_half, ROW0 + 8 * t, state, rhs, seams, ends, send)

    sides = Side(ROW0 + 8, rows - 8)
    before_first = lambda f: side_initial[f, HALO : rows - HALO, :]
    handed = side_residual(sides, steps, first_half, hstate, ends, before_first, hrhs)
    flat = [handed[f][at : at + 8, :] for f in range(FIELDS) for at in range(0, rows - 8, 8)]
    pack_sides(flat, sent, SWEEPS * FIELDS * SLABS * (rows - 8))


def outer_kernel(width_tm, steps_dev, rows, *refs):
    half = width_tm // 2
    side, side_initial, above, below = refs[4:8]
    state, rhs, ends, hrhs, sent, hstate, hbefore, seams = refs[8:]
    steps = half * steps_dev
    me = lax.axis_index("tm")
    mine = me & (half - 1)
    first_half = me < half
    body = slice(MAIN, MAIN + rows)
    top, bottom = slice(ROW0, MAIN), slice(MAIN + rows, MAIN + rows + HALO)
    k = 0
    for b in range(half):
        for c in range(SLABS):
            for i in range(steps_dev):
                n = steps_dev * (mine ^ b) + i
                for f in range(FIELDS):
                    state[n + 1, f, c, top, :] = above[k : k + HALO, :]
                    state[n + 1, f, c, bottom, :] = below[k : k + HALO, :]
                    k += HALO
    for c in range(SLABS):
        for f in range(FIELDS):
            state[0, f, c, top, :] = jnp.where(first_half, above[k : k + HALO, :], 0.0)
            state[0, f, c, bottom, :] = jnp.where(first_half, below[k : k + HALO, :], 0.0)
            k += HALO
    for held, given in ((hstate, side), (hbefore, side_initial)):
        for f in range(FIELDS):
            held[f, body, :] = given[f, :, :]
            held[f, top, :] = above[k : k + HALO, :]
            held[f, bottom, :] = below[k : k + HALO, :]
            k += HALO
    whole = Side(ROW0, rows + 2 * HALO)
    whole.set_seams(seams, [hstate[f, whole.span, :] for f in range(FIELDS)])
    flat = []
    for which, start in enumerate((ROW0, ROW0 + rows)):

        def send(p, f, c, value):
            at = (((p * FIELDS + f) * SLABS + c) * 2 + which) * 7
            sent[at : at + 7, :] = value[1 - which : 8 - which, :]

        residual_tile(steps, first_half, start, state, rhs, seams, ends, send)
        sides = Side(start, 8)
        before_first = lambda f: hbefore[f, start : start + 8, :]
        flat += side_residual(sides, steps, first_half, hstate, ends, before_first, hrhs)
    pack_sides(flat, sent, SWEEPS * FIELDS * SLABS * 14)


def chain_kernel(steps, rows, rhs, hrhs, result, ya, yb, hya, hyb, ends, seams):
    _, ratios, _ = chain_factors()
    sides = Side(ROW0, rows + 2 * HALO)
    blocks = sides.tall // 8
    running = lane_matrix(
        lambda source, target: jnp.where((source <= target) & (target < steps), 1.0, 0.0)
    )
    side_new = sides.product([hrhs[f, sides.span, :] for f in range(FIELDS)], running)
    for f in range(FIELDS):
        hya[f, sides.span, :] = side_new[f]
    sides.set_seams(seams, side_new)

    @pl.loop(0, blocks)
    def _(t):
        start = ROW0 + 8 * t
        for f, c in EACH:
            total = jnp.zeros((8, LANES), jnp.float32)
            for n in range(steps):
                total = total + rhs[n, f, c, pl.ds(start, 8), :]
                ya[n, f, c, pl.ds(start, 8), :] = total

    def sweep(ratio, old, hold, new, hnew, final):
        first = MAIN if final else ROW0

        @pl.loop(0, rows // 8 if final else blocks)
        def _(t):
            start = first + 8 * t
            seam = [seams[f, pl.ds(start, 8), :] for f in range(FIELDS)]
            last = zeros(FIELDS)
            total = dict(zip(EACH, zeros(len(EACH))))
            for n in range(steps):
                parts = neighbours(old, n, start, seam, n)
                if not final:
                    add_ends(last, parts[0], n)
                for c in range(SLABS):
                    value = off_diagonal(*slab(parts, c))
                    for f in range(FIELDS):
                        carry = value[f] + ratio * rhs[n, f, c, pl.ds(start, 8), :]
                        total[f, c] = total[f, c] + carry
                        if final:
                            at = pl.ds(pl.multiple_of(8 * t, 8), 8)
                            new[n, f, c, at, :] = total[f, c]
                        else:
                            new[n, f, c, pl.ds(start, 8), :] = total[f, c]
            if not final:
                for f in range(FIELDS):
                    ends[f, pl.ds(start, 8), :] = last[f]

        if not final:
            value = off_diagonal(*sides.parts(hold, ends))
            side_next = sides.product(
                [value[f] + ratio * hrhs[f, sides.span, :] for f in range(FIELDS)], running
            )
            for f in range(FIELDS):
                hnew[f, sides.span, :] = side_next[f]
            sides.set_seams(seams, side_next)

    buffers = [(ya, hya), (yb, hyb)]
    for m in range(1, SWEEPS):
        old, new = buffers[(m + 1) % 2], buffers[m % 2]
        final = m == SWEEPS - 1
        sweep(ratios[m - 1], *old, result if final else new[0], new[1], final)


def join_kernel(width_tm, steps_dev, rows, inner_rows, *refs):
    half = width_tm // 2
    count = 2 if inner_rows else 4
    given_refs, (chained, state) = refs[:count], refs[count : count + 2]
    outs = refs[-9 - half : -9]
    given, pa, pb, hgiven, hpa, hpb, ends, seams, result = refs[-9:]
    inner_own, inner_other = given_refs[:2]
    steps = half * steps_dev
    me = lax.axis_index("tm")
    mine = me & (half - 1)
    gammas, _, scale = chain_factors()
    own, first, second = swap_factors(steps)
    other = [jnp.where(me < half, a, b) for a, b in zip(first, second)]
    tiles = rows // 8
    if inner_rows:
        sides = Side(ROW0 + 8, rows - 8)
        places = (tiles - 1, lambda t: ROW0 + 8 + 8 * t)
        finals = (tiles - 2, lambda t: MAIN + 8 + 8 * t)
    else:
        sides = Side(ROW0, rows + 2 * HALO)
        places = (4, lambda t: ROW0 + 8 * (t + (tiles - 3) * (t // 2)))
        finals = (2, lambda t: MAIN + (rows - 8) * t)
    cells = SWEEPS * FIELDS * SLABS

    def joined(ref_own, ref_other, at, size, step, p):
        total = None
        for d in range(SWEEPS - p):
            rows_d = slice(at + step * d, at + step * d + size)
            term = other[d] * ref_other[rows_d, :] + own[d] * ref_own[rows_d, :]
            total = term if total is None else total + term
        return total

    for p in range(SWEEPS):
        for f, c in EACH:
            cell = (p * FIELDS + f) * SLABS + c
            found = [(ROW0 + 8, joined(inner_own, inner_other, cell * (rows - 8), rows - 8, FIELDS * SLABS * (rows - 8), p))]
            if not inner_rows:
                for which, start in ((0, ROW0 + 1), (1, ROW0 + rows)):
                    at = (cell * 2 + which) * 7
                    found.append((start, joined(*given_refs[2:], at, 7, FIELDS * SLABS * 14, p)))
            for start, value in found:
                given[p, f, c, start : start + value.shape[0], :] = value
                pa[p, f, c, start : start + value.shape[0], :] = gammas[-1] * value

    step8 = step_of_lane(lanes())

    def from_later(value, d, step):
        return jnp.where(step < SWEEPS - d, turn(value, -GROUP * d), 0.0)

    def set_side(refs_side, at, index, f, start):
        ours, theirs = (unpack_side(ref, at, index) for ref in refs_side)
        value = jnp.zeros((8, LANES), jnp.float32)
        for d in range(SWEEPS):
            value = value + from_later(other[d] * theirs + own[d] * ours, d, step8)
        hgiven[f, start : start + 8, :] = value
        hpa[f, start : start + 8, :] = gammas[-1] * value

    for f in range(FIELDS):
        for r in range(tiles - 1):
            set_side(given_refs[:2], cells * (rows - 8), f * (tiles - 1) + r, f, ROW0 + 8 + 8 * r)
        if not inner_rows:
            for which, start in ((0, ROW0), (1, ROW0 + rows)):
                set_side(given_refs[2:], cells * 14, which * FIELDS + f, f, start)
    sides.set_seams(seams, [hpa[f, sides.span, :] for f in range(FIELDS)])

    buffers = [(pa, hpa), (pb, hpb)]
    for k in range(1, SWEEPS):
        (old, hold), (new, hnew) = buffers[(k + 1) % 2], buffers[k % 2]
        gamma = gammas[SWEEPS - 1 - k]
        final = k == SWEEPS - 1
        turns, place = finals if final else places

        for t in range(turns):
            start = place(t)
            here = pl.ds(start, 8)
            seam = [seams[f, here, :] for f in range(FIELDS)]
            last = zeros(FIELDS)
            found = {}
            for p in range(SWEEPS):
                parts = neighbours(old, p, start, seam, p)
                if not final:
                    add_ends(last, parts[0], p)
                for c in range(SLABS):
                    value = off_diagonal(*slab(parts, c))
                    for f in range(FIELDS):
                        total = value[f]
                        if p + k < SWEEPS:
                            total = total + gamma * given[p + k, f, c, here, :]
                        if final:
                            found[p, f, c] = total * RATE ** (p + 1)
                        else:
                            new[p, f, c, here, :] = total
            if not final:
                for f in range(FIELDS):
                    ends[f, here, :] = last[f]
            else:
                at = pl.ds(8 * t, 8)
                from_chain = pl.ds(start - MAIN, 8)
                for f, c in EACH:
                    for n in range(steps):
                        total = scale * chained[n, f, c, from_chain, :]
                        for p in range(SWEEPS):
                            total = total + binomial(n + p, p) * found[p, f, c]
                        result[n, f, c, at, :] = state[n + 1, f, c, here, :] - total * RATE**n

        if not final:
            value = off_diagonal(*sides.parts(hold, ends))
            side_next = [
                value[f] + gamma * from_later(hgiven[f, sides.span, :], k, sides.step)
                for f in range(FIELDS)
            ]
            for f in range(FIELDS):
                hnew[f, sides.span, :] = side_next[f]
            sides.set_seams(seams, side_next)

    size = 8 * finals[0]
    for b in range(half):
        at = 0
        for c in range(SLABS):
            for i in range(steps_dev):
                n = steps_dev * (mine ^ b) + i
                for f in range(FIELDS):
                    outs[b][at : at + size, :] = result[n, f, c, :, :]
                    at += size


def unpack_kernel(width_tm, size, *refs):
    half = width_tm // 2
    out = refs[-1]
    steps_dev, fields, _, _ = out.shape
    mine = lax.axis_index("tm") & (half - 1)
    t = pl.program_id(0)
    for b in range(half):
        at = 0
        for c in range(SLABS):
            here = tile_at(SLABS * (mine ^ b) + c)
            for i in range(steps_dev):
                for f in range(fields):
                    out[i, f, :, here] = refs[b][pl.ds(pl.multiple_of(at + 8 * t, 8), 8), :]
                    at += size


def unpack(width_tm, shape, pieces, size, place, held=()):
    steps_dev, fields, _, columns = shape
    return pl.pallas_call(
        functools.partial(unpack_kernel, width_tm, size),
        grid=(size // 8,),
        out_shape=jax.ShapeDtypeStruct(shape, jnp.float32),
        in_specs=[pl.BlockSpec(memory_space=pltpu.VMEM)] * len(pieces)
        + [pl.BlockSpec(memory_space=pl.ANY)] * len(held),
        out_specs=pl.BlockSpec((steps_dev, fields, 8, columns), lambda t: (0, 0, place(t), 0)),
        input_output_aliases={len(pieces): 0} if held else {},
        compiler_params=pltpu.CompilerParams(vmem_limit_bytes=VMEM_BYTES),
    )(*pieces, *held)


def call(kernel, out_shapes, operands, scratch=(), aliases=None, after=()):
    whole = pl.BlockSpec(memory_space=pltpu.VMEM)
    shapes = [jax.ShapeDtypeStruct(shape, jnp.float32) for shape in out_shapes]
    moved = 4 * sum(math.prod(x.shape) for x in list(shapes) + list(operands))
    in_specs = [whole] * len(operands) + [pl.BlockSpec(memory_space=pl.ANY)] * len(after)
    operands = list(operands) + list(after)
    return pl.pallas_call(
        kernel,
        out_shape=shapes,
        in_specs=in_specs,
        out_specs=[whole] * len(shapes),
        scratch_shapes=[pltpu.VMEM(shape, jnp.float32) for shape in scratch],
        input_output_aliases=aliases or {},
        compiler_params=pltpu.CompilerParams(vmem_limit_bytes=VMEM_BYTES),
        cost_estimate=pl.CostEstimate(flops=moved, bytes_accessed=moved, transcendentals=0),
    )(*operands)


def swap(piece, b):
    count = lax.axis_size("tm")
    return lax.ppermute(piece, "tm", [(k, k ^ b) for k in range(count)])


def fast_on_device(state, initial):
    steps_dev, fields, rows, columns = state.shape
    width_tm = lax.axis_size("tm")
    bands = lax.axis_size("space")
    half = width_tm // 2
    steps = steps_dev * half
    main = SLABS * steps_dev * fields * rows
    words = -(-fields * rows // 8 // (LANES // (GROUP * steps_dev)))
    tall = rows + 2 * HALO + 2 * ROW0
    sized = (width_tm, steps_dev)
    pieces = call(
        functools.partial(pack_kernel, width_tm), [(main + 8 * words, LANES)] * half, [state]
    )
    pieces = [pieces[0]] + [swap(pieces[b], b) for b in range(1, half)]
    tiles, side_initial = call(
        functools.partial(place_initial, width_tm),
        [(fields, SLABS, rows, LANES), (fields, rows, LANES)],
        [initial],
        after=pieces[:1],
    )
    flat = (fields, tall, LANES)
    held_shapes = [
        (steps + 1, fields, SLABS, tall, LANES),
        (steps, fields, SLABS, tall, LANES),
        flat,
        flat,
    ]
    cells = SWEEPS * fields * SLABS
    inner_words = -(-fields * (rows - 8) // 8 // PER_WORD)
    outer_words = -(-2 * fields // PER_WORD)
    *held, side, inner = call(
        functools.partial(inner_kernel, *sized),
        held_shapes
        + [(fields, rows, LANES), (cells * (rows - 8) + 8 * inner_words, LANES)],
        pieces + [tiles, side_initial],
        [flat] * 2,
    )
    inner_other = swap(inner, half)
    edge_rows = -(-HALO * fields * (SLABS * (steps + 1) + 2) // 8) * 8
    up, down = call(
        functools.partial(edge_kernel, width_tm),
        [(edge_rows, LANES)] * 2,
        pieces + [tiles, side, side_initial],
    )
    above = lax.ppermute(down, "space", [(i, (i + 1) % bands) for i in range(bands)])
    below = lax.ppermute(up, "space", [((i + 1) % bands, i) for i in range(bands)])
    solved, rhs, _, hrhs, outer = call(
        functools.partial(outer_kernel, *sized, rows),
        held_shapes + [(cells * 14 + 8 * outer_words, LANES)],
        held + [side, side_initial, above, below],
        [flat] * 3,
        aliases={0: 0, 1: 1, 2: 2, 3: 3},
    )
    outer_other = swap(outer, half)
    (chained,) = call(
        functools.partial(chain_kernel, steps, rows),
        [(steps, fields, SLABS, rows, LANES)],
        [rhs, hrhs],
        [held_shapes[1]] * 2 + [flat] * 4,
    )
    four = (SWEEPS, fields, SLABS, tall, LANES)
    results = []
    for given, size in (
        ([inner, inner_other], rows - 16),
        ([inner, inner_other, outer, outer_other], 16),
    ):
        parts = call(
            functools.partial(join_kernel, *sized, rows, len(given) == 2),
            [(SLABS * steps_dev * fields * size, LANES)] * half,
            given + [chained, solved],
            [four] * 3 + [flat] * 5 + [(steps, fields, SLABS, size, LANES)],
            after=results[:1],
        )
        results += [parts[0]] + [swap(parts[b], b) for b in range(1, half)]
    updated = unpack(width_tm, state.shape, results[:half], rows - 16, lambda t: t + 1)
    updated = unpack(
        width_tm, state.shape, results[half:], 16, lambda t: t * (rows // 8 - 1), (updated,)
    )
    return updated


def choose(state, initial):
    if fits_fast_plan(state, lax.axis_size("tm")):
        return fast_on_device(state, initial)
    return on_device(state, initial)


def solution(mesh):
    in_specs = (P("tm", None, "space", None), P(None, "space", None))
    out_specs = P("tm", None, "space", None)
    return jax.shard_map(
        choose, mesh=mesh, in_specs=in_specs, out_specs=out_specs, check_vma=False
    )
```

```python
import functools
import math

import jax
import jax.numpy as jnp
from jax import lax
from jax.experimental import pallas as pl
from jax.experimental.pallas import tpu as pltpu
from jax.sharding import PartitionSpec as P

SWEEPS = 4


circulant_alpha = 0.1
time_step = 0.5
coriolis = 0.3
viscous = 0.2
highest = lax.Precision.HIGHEST


def from_behind(block, axis, distance):
    devices = range(lax.axis_size(axis))
    route = [(i - distance, i) for i in devices if i - distance in devices]
    return lax.ppermute(block, axis, route)


def extended(cells, sides, width):
    for axis, dim in sides:
        count = lax.axis_size(axis)
        head = lax.slice_in_dim(cells, 0, width, axis=dim)
        tail = lax.slice_in_dim(cells, cells.shape[dim] - width, cells.shape[dim], axis=dim)
        cells = jnp.concatenate(
            [
                lax.ppermute(tail, axis, [(i, (i + 1) % count) for i in range(count)]),
                cells,
                lax.ppermute(head, axis, [((i + 1) % count, i) for i in range(count)]),
            ],
            axis=dim,
        )
    return cells


def interior(values):
    return values[..., 1:-1, :]


def column_diff(values):
    return 0.5 * (jnp.roll(values, -1, axis=-1) - jnp.roll(values, 1, axis=-1))[..., 1:-1, :]


def row_diff(values):
    return 0.5 * (values[..., 2:, :] - values[..., :-2, :])


def laplace(values):
    return (
        values[..., 2:, :]
        + values[..., :-2, :]
        + jnp.roll(values, -1, axis=-1)[..., 1:-1, :]
        + jnp.roll(values, 1, axis=-1)[..., 1:-1, :]
        - 4.0 * values[..., 1:-1, :]
    )


def tendency(padded):
    surface = padded[..., 0, :, :]
    eastward = padded[..., 1, :, :]
    northward = padded[..., 2, :, :]
    column_depth = 1.0 + surface
    east_inner = interior(eastward)
    north_inner = interior(northward)
    mass_change = time_step * (
        column_diff(column_depth * eastward) + row_diff(column_depth * northward)
    ) - viscous * laplace(surface)
    east_change = (
        time_step
        * (
            east_inner * column_diff(eastward)
            + north_inner * row_diff(eastward)
            + column_diff(surface)
        )
        - coriolis * north_inner
        - viscous * laplace(eastward)
    )
    north_change = (
        time_step
        * (
            east_inner * column_diff(northward)
            + north_inner * row_diff(northward)
            + row_diff(surface)
        )
        + coriolis * east_inner
        - viscous * laplace(northward)
    )
    return jnp.stack([mass_change, east_change, north_change], axis=-3)


def linear_part(padded):
    surface = padded[..., 0, :, :]
    eastward = padded[..., 1, :, :]
    northward = padded[..., 2, :, :]
    mass_change = time_step * (column_diff(eastward) + row_diff(northward)) - viscous * laplace(
        surface
    )
    east_change = (
        time_step * column_diff(surface)
        - coriolis * interior(northward)
        - viscous * laplace(eastward)
    )
    north_change = (
        time_step * row_diff(surface) + coriolis * interior(eastward) - viscous * laplace(northward)
    )
    return jnp.stack([mass_change, east_change, north_change], axis=-3)


def pair_apply(factors, values):
    factor = factors[:, :, None, None, None]
    return jnp.stack(
        [
            factor[0] * values[0] - factor[1] * values[1],
            factor[2] * values[1] + factor[3] * values[0],
        ]
    )


def sweep_weights():
    return [
        1.0 / (1.15 - 0.85 * math.cos(math.pi * (2 * sweep + 1) / (2 * SWEEPS)))
        for sweep in range(SWEEPS)
    ]


def slot_factors(slot_index, total_steps):
    decay_base = circulant_alpha ** (1.0 / total_steps)
    angles = 2.0 * math.pi / total_steps * slot_index.astype(jnp.float32)
    real_eigen = 1.0 - decay_base * jnp.cos(angles)
    imaginary_eigen = decay_base * jnp.sin(angles)
    real_shift = real_eigen + 4.0 * viscous
    modulus = real_shift * real_shift + imaginary_eigen * imaginary_eigen
    eigen = jnp.stack([real_eigen, imaginary_eigen, real_eigen, imaginary_eigen])
    jacobi = jnp.stack(
        [
            real_shift / modulus,
            -imaginary_eigen / modulus,
            real_shift / modulus,
            -imaginary_eigen / modulus,
        ]
    )
    leading = (slot_index == 0)[None, :]
    zero_part = jnp.zeros_like(real_eigen)
    packed_eigen = jnp.stack(
        [zero_part + (1.0 - decay_base), zero_part, zero_part + (1.0 + decay_base), zero_part]
    )
    packed_jacobi = jnp.stack(
        [
            zero_part + 1.0 / (1.0 - decay_base + 4.0 * viscous),
            zero_part,
            zero_part + 1.0 / (1.0 + decay_base + 4.0 * viscous),
            zero_part,
        ]
    )
    eigen = jnp.where(leading, packed_eigen, eigen)
    jacobi = jnp.where(leading, packed_jacobi, jacobi)
    return (eigen, jacobi)


def time_tables(total_steps):
    slot_total = total_steps // 2
    step_ids = jnp.arange(total_steps, dtype=jnp.int32)
    slot_ids = jnp.arange(slot_total, dtype=jnp.int32)
    phase = slot_ids[:, None] * step_ids[None, :] % total_steps
    angles = 2.0 * math.pi / total_steps * phase.astype(jnp.float32)
    decay_base = circulant_alpha ** (1.0 / total_steps)
    growth = decay_base ** step_ids.astype(jnp.float32)
    cosine = jnp.cos(angles)
    sines = jnp.sin(angles)
    forward_real = cosine * growth[None, :]
    forward_imaginary = -sines * growth[None, :]
    inverse_imaginary = -sines
    alternate = 1.0 - 2.0 * (step_ids % 2).astype(jnp.float32)
    leading = (slot_ids == 0)[:, None]
    forward_imaginary = jnp.where(leading, (alternate * growth)[None, :], forward_imaginary)
    inverse_real = jnp.where(leading, 1.0, 2.0 * cosine)
    inverse_imaginary = jnp.where(leading, alternate[None, :], -2.0 * sines)
    forward = jnp.concatenate([forward_real, forward_imaginary], axis=0)
    inverse = jnp.concatenate([inverse_real, inverse_imaginary], axis=0).T
    inverse = inverse * (1.0 / (total_steps * growth))[:, None]
    return (forward, inverse)


def on_device(state, initial):
    steps_dev, fields, band_rows, columns = state.shape
    width_tm = lax.axis_size("tm")
    total_steps = steps_dev * width_tm
    previous = from_behind(state[-1], "tm", 1)
    previous = jnp.where(lax.axis_index("tm") == 0, initial, previous)
    before = jnp.concatenate([previous[None], state[:-1]], axis=0)
    padded = extended(state, (("space", 2),), 1)
    residual = state - before + tendency(padded)
    forward, inverse = time_tables(total_steps)
    slot_total = forward.shape[0] // 2
    per_device = slot_total // width_tm
    spectrum = jnp.einsum(
        "rj,jnc->rnc",
        forward,
        lax.all_to_all(
            residual.reshape(steps_dev, fields, band_rows * columns),
            "tm",
            split_axis=2,
            concat_axis=0,
            tiled=True,
        ),
        precision=highest,
    )
    spectrum = spectrum.reshape(2, slot_total, fields, spectrum.shape[-1])
    banded = lax.all_to_all(spectrum, "tm", split_axis=1, concat_axis=3, tiled=True).reshape(
        2, per_device, fields, band_rows, columns
    )
    slot_index = lax.axis_index("tm") * per_device + jnp.arange(per_device, dtype=jnp.int32)
    eigen, jacobi = slot_factors(slot_index, total_steps)
    weights = sweep_weights()
    iterate = weights[0] * pair_apply(jacobi, banded)
    for sweep in range(1, SWEEPS):
        border = extended(iterate, (("space", 3),), 1)
        applied = pair_apply(eigen, iterate) + linear_part(border)
        iterate = iterate + weights[sweep] * pair_apply(jacobi, banded - applied)
    flat_solution = iterate.reshape(2, per_device, fields, band_rows * columns)
    blocks = lax.all_to_all(flat_solution, "tm", split_axis=3, concat_axis=1, tiled=True)
    merged = blocks.reshape(2 * blocks.shape[1], blocks.shape[2], blocks.shape[3])
    all_steps = jnp.einsum("jr,rnc->jnc", inverse, merged, precision=highest)
    correction = lax.all_to_all(all_steps, "tm", split_axis=0, concat_axis=2, tiled=True)
    return state - correction.reshape(state.shape)


LANES = 128
HALO = SWEEPS
GROUP = 2 * HALO
ROW0 = 8
MAIN = ROW0 + HALO
SHIFT = 1.0 + 4.0 * viscous
RATE = 1.0 / SHIFT
VMEM_BYTES = 48 * 1024 * 1024
SLABS = 2
FIELDS = 3
EACH = [(f, c) for f in range(FIELDS) for c in range(SLABS)]


def fits_fast_plan(state, width_tm):
    steps_dev, fields, band_rows, columns = state.shape
    half = width_tm // 2
    steps = steps_dev * half
    return (
        width_tm > 1
        and width_tm & (width_tm - 1) == 0
        and columns == SLABS * LANES * half
        and SWEEPS * GROUP <= GROUP * steps <= LANES
        and LANES % (GROUP * steps_dev) == 0
        and band_rows % 8 == 0
        and band_rows >= 24
        and fields == FIELDS
    )


def lanes(rows=8):
    return lax.broadcasted_iota(jnp.int32, (rows, LANES), 1)


def step_of_lane(lane):
    return ((lane + HALO) & (LANES - 1)) // GROUP


def turn(values, shift):
    return pltpu.roll(values, shift % LANES, 1)


def tile_at(index):
    return pl.ds(pl.multiple_of(index * LANES, LANES), LANES)


def binomial(top, bottom):
    return float(math.comb(top, bottom))


def side_places(tile, width_tm):
    last = width_tm // 2 * SLABS - 1
    return tile_at((SLABS * tile + SLABS) & last), tile_at((SLABS * tile + last) & last)


def pack_kernel(width_tm, state_ref, *outs):
    steps_dev, fields, rows, _ = state_ref.shape
    half = width_tm // 2
    me = lax.axis_index("tm")
    lane = lanes()
    step = step_of_lane(lane)
    blocks = rows // 8
    per_word = LANES // (GROUP * steps_dev)
    for b, out in enumerate(outs):
        tile = (me ^ b) & (half - 1)
        after, prior = side_places(tile, width_tm)
        at = 0
        for c in range(SLABS):
            for i in range(steps_dev):
                for f in range(fields):
                    out[at : at + rows, :] = state_ref[i, f, :, tile_at(SLABS * tile + c)]
                    at += rows
        for first in range(0, fields * blocks, per_word):
            packed = jnp.zeros((8, LANES), jnp.float32)
            for g in range(first, min(first + per_word, fields * blocks)):
                f, r = divmod(g, blocks)
                for i in range(steps_dev):
                    slot = steps_dev * (g - first) + i
                    sides = jnp.where(
                        lane < LANES // 2,
                        state_ref[i, f, 8 * r : 8 * r + 8, after],
                        state_ref[i, f, 8 * r : 8 * r + 8, prior],
                    )
                    packed = jnp.where(step == slot, turn(sides, GROUP * slot), packed)
            out[at : at + 8, :] = packed
            at += 8


def place_initial(width_tm, initial_ref, _, tiles, side_initial):
    fields, rows, _ = initial_ref.shape
    mine = lax.axis_index("tm") & (width_tm // 2 - 1)
    after, prior = side_places(mine, width_tm)
    for f, c in EACH:
        tiles[f, c] = initial_ref[f, :, tile_at(SLABS * mine + c)]
    lane = lanes(rows)
    for f in range(fields):
        side_initial[f] = jnp.where(
            lane < LANES // 2, initial_ref[f, :, after], initial_ref[f, :, prior]
        )


def edge_kernel(width_tm, *refs):
    half = width_tm // 2
    pieces, (tiles, side, side_initial, up, down) = refs[:half], refs[half:]
    fields, rows, _ = side.shape
    main = pieces[0].shape[0] // rows * rows
    for out, part in ((up, slice(0, HALO)), (down, slice(rows - HALO, rows))):
        k = 0
        for b in range(half):
            for at in range(0, main, rows):
                out[k : k + HALO, :] = pieces[b][at + part.start : at + part.stop, :]
                k += HALO
        for c in range(SLABS):
            for f in range(fields):
                out[k : k + HALO, :] = tiles[f, c, part, :]
                k += HALO
        for held in (side, side_initial):
            for f in range(fields):
                out[k : k + HALO, :] = held[f, part, :]
                k += HALO


def full_tendency(own, east, west, north, south):
    e, u, v = own
    around = [east[f] + west[f] + (north[f] + south[f]) for f in range(FIELDS)]
    quarter = 0.5 * time_step
    flux = ((1.0 + east[0]) * east[1] - (1.0 + west[0]) * west[1]) + (
        (1.0 + south[0]) * south[2] - (1.0 + north[0]) * north[2]
    )
    carry1 = u * (east[1] - west[1]) + v * (south[1] - north[1]) + (east[0] - west[0])
    carry2 = u * (east[2] - west[2]) + v * (south[2] - north[2]) + (south[0] - north[0])
    diagonal = 1.0 + 4.0 * viscous
    return (
        diagonal * e + quarter * flux - viscous * around[0],
        diagonal * u + quarter * carry1 - coriolis * v - viscous * around[1],
        diagonal * v + quarter * carry2 + coriolis * u - viscous * around[2],
    )


def off_diagonal(own, east, west, north, south):
    _, u, v = own
    around = [east[f] + west[f] + (north[f] + south[f]) for f in range(FIELDS)]
    quarter = 0.5 * time_step
    return (
        viscous * around[0] - quarter * ((east[1] - west[1]) + (south[2] - north[2])),
        viscous * around[1] - quarter * (east[0] - west[0]) + coriolis * v,
        viscous * around[2] - quarter * (south[0] - north[0]) - coriolis * u,
    )


def chain_factors():
    gammas = []
    for weight in sweep_weights():
        shifted = [1.0] + gammas
        gammas = [weight * x for x in shifted]
        for i, x in enumerate(shifted[1:]):
            gammas[i] += (1.0 - weight) * x
    scale = RATE * gammas[-1]
    ratios = []
    for gamma in reversed(gammas[:-1]):
        ratios.append(gamma / scale)
        scale *= RATE
    return gammas, ratios, scale


def series_product(a, b):
    return [sum(a[i] * b[d - i] for i in range(d + 1)) for d in range(SWEEPS)]


def swap_factors(steps):
    hop = [RATE ** (steps + d) * binomial(steps - 1 + d, d) for d in range(SWEEPS)]
    lap = [circulant_alpha * x for x in series_product(hop, hop)]
    inverse = []
    for d in range(SWEEPS):
        value = (1.0 if d == 0 else 0.0) + sum(lap[i] * inverse[d - i] for i in range(1, d + 1))
        inverse.append(value / (1.0 - lap[0]))
    own = [circulant_alpha * x for x in series_product(inverse, hop)]
    return own, [circulant_alpha * x for x in inverse], inverse


class Side:
    def __init__(self, first, tall):
        self.first, self.tall = first, tall
        self.span = slice(first, first + tall)
        lane = lanes(self.tall)
        self.step = step_of_lane(lane)
        self.after = (lane & (GROUP - 1)) == 0
        self.before = (lane & (GROUP - 1)) == GROUP - 1

    def parts(self, held, ends):
        own, north, south = (
            [held[f, self.first + d : self.first + d + self.tall, :] for f in range(FIELDS)] for d in (0, -1, 1)
        )
        last = [ends[f, self.span, :] for f in range(FIELDS)]
        east = [jnp.where(self.before, turn(last[f], -1), turn(own[f], -1)) for f in range(FIELDS)]
        west = [jnp.where(self.after, turn(last[f], 1), turn(own[f], 1)) for f in range(FIELDS)]
        return own, east, west, north, south

    def set_seams(self, seams, values):
        for f in range(FIELDS):
            seams[f, self.span, :] = jnp.where(self.after, turn(values[f], 1), turn(values[f], -1))

    def product(self, values, matrix):
        done = jnp.dot(
            jnp.concatenate(values, axis=0),
            matrix,
            precision=highest,
            preferred_element_type=jnp.float32,
        )
        return [done[self.tall * f : self.tall * (f + 1), :] for f in range(FIELDS)]


def lane_matrix(entry):
    source = lax.broadcasted_iota(jnp.int32, (LANES, LANES), 0)
    target = lax.broadcasted_iota(jnp.int32, (LANES, LANES), 1)
    same = ((source - target) & (GROUP - 1)) == 0
    return jnp.where(same, entry(step_of_lane(source), step_of_lane(target)), 0.0)


def neighbours(held, slot, start, seam, n):
    lane = lanes()
    is_first, is_last = lane == 0, lane == LANES - 1
    load = lambda d: {k: held[slot, k[0], k[1], pl.ds(start + d, 8), :] for k in EACH}
    own, north, south = load(0), load(-1), load(1)
    east, west = {}, {}
    for f in range(FIELDS):
        across = turn(seam[f], -GROUP * n)
        back = [turn(own[f, c], -1) for c in range(SLABS)] + [across]
        ahead = [across] + [turn(own[f, c], 1) for c in range(SLABS)]
        for c in range(SLABS):
            east[f, c] = jnp.where(is_last, back[c + 1], back[c])
            west[f, c] = jnp.where(is_first, ahead[c], ahead[c + 1])
    return own, east, west, north, south


def slab(parts, c):
    return [[part[f, c] for f in range(FIELDS)] for part in parts]


def add_ends(last, own, n):
    lane = lanes()
    step = step_of_lane(lane)
    for f in range(FIELDS):
        both = jnp.where(lane < LANES // 2, own[f, 0], own[f, SLABS - 1])
        last[f] = jnp.where(step == n, turn(both, GROUP * n), last[f])


def zeros(count):
    return [jnp.zeros((8, LANES), jnp.float32)] * count


def residual_tile(steps, first_half, start, state, rhs, seams, ends, send):
    seam = [seams[f, pl.ds(start, 8), :] for f in range(FIELDS)]
    last = zeros(FIELDS)
    sums = {k: zeros(SWEEPS) for k in EACH}
    for n in range(steps):
        parts = neighbours(state, n + 1, start, seam, n)
        add_ends(last, parts[0], n)
        for c in range(SLABS):
            value = full_tendency(*slab(parts, c))
            for f in range(FIELDS):
                carry = (value[f] - state[n, f, c, pl.ds(start, 8), :]) * SHIFT**n
                rhs[n, f, c, pl.ds(start, 8), :] = carry
                for j in range(SWEEPS):
                    carry = sums[f, c][j] + carry
                    sums[f, c][j] = carry
    for f in range(FIELDS):
        ends[f, pl.ds(start, 8), :] = last[f]
    for f, c in EACH:
        for j in range(SWEEPS):
            value = sums[f, c][j] * RATE ** (steps + j)
            if j == 0:
                value = value - jnp.where(first_half, state[steps, f, c, pl.ds(start, 8), :], 0.0)
            send(SWEEPS - 1 - j, f, c, value)


PER_WORD = LANES // (SWEEPS * GROUP)


def pack_sides(blocks, sent, at):
    kind = step_of_lane(lanes()) // SWEEPS
    for first in range(0, len(blocks), PER_WORD):
        word = jnp.zeros((8, LANES), jnp.float32)
        for k, block in enumerate(blocks[first : first + PER_WORD]):
            word = jnp.where(kind == k, turn(block, SWEEPS * GROUP * k), word)
        sent[at : at + 8, :] = word
        at += 8


def unpack_side(sent, at, index):
    word, k = divmod(index, PER_WORD)
    value = turn(sent[at + 8 * word : at + 8 * word + 8, :], -SWEEPS * GROUP * k)
    return jnp.where(step_of_lane(lanes()) < SWEEPS, value, 0.0)


def side_residual(sides, steps, first_half, hstate, ends, before_first, hrhs):
    parts = sides.parts(hstate, ends)
    value = full_tendency(*parts)
    growth = jnp.where(
        sides.step < steps, jnp.exp(sides.step.astype(jnp.float32) * math.log(SHIFT)), 0.0
    )
    held = []
    for f in range(FIELDS):
        first = jnp.where(first_half, before_first(f), 0.0)
        before = jnp.where(sides.step == 0, first, turn(parts[0][f], GROUP))
        held.append((value[f] - before) * growth)
        hrhs[f, sides.span, :] = held[f]

    def entry(source, target):
        after = (steps - 1 - source).astype(jnp.float32)
        weight = jnp.full((LANES, LANES), RATE**steps, jnp.float32)
        result = jnp.zeros((LANES, LANES), jnp.float32)
        for j in range(1, SWEEPS + 1):
            result = jnp.where(target == SWEEPS - j, weight, result)
            weight = weight * (after + float(j)) * (RATE / j)
        return jnp.where(source < steps, result, 0.0)

    handed = sides.product(held, lane_matrix(entry))
    for f in range(FIELDS):
        last = turn(parts[0][f], GROUP * (SWEEPS - steps))
        handed[f] = handed[f] - jnp.where(first_half & (sides.step == SWEEPS - 1), last, 0.0)
    return handed


def inner_kernel(width_tm, steps_dev, *refs):
    half = width_tm // 2
    pieces, (tiles, side_initial) = refs[:half], refs[half : half + 2]
    state, rhs, ends, hrhs, side, sent, seams, hstate = refs[half + 2 :]
    fields, rows, _ = side.shape
    steps = half * steps_dev
    me = lax.axis_index("tm")
    mine = me & (half - 1)
    first_half = me < half
    body = slice(MAIN, MAIN + rows)
    for b in range(half):
        at = 0
        for c in range(SLABS):
            for i in range(steps_dev):
                n = steps_dev * (mine ^ b) + i
                for f in range(fields):
                    state[n + 1, f, c, body, :] = pieces[b][at : at + rows, :]
                    at += rows
    for f, c in EACH:
        state[0, f, c, body, :] = jnp.where(first_half, tiles[f, c], 0.0)
    owner = step_of_lane(lanes()) // steps_dev
    blocks = rows // 8
    per_word = LANES // (GROUP * steps_dev)
    main = SLABS * steps_dev * fields * rows
    for g in range(fields * blocks):
        f, r = divmod(g, blocks)
        word, place = divmod(g, per_word)
        found = jnp.zeros((8, LANES), jnp.float32)
        for b in range(half):
            source = mine ^ b
            value = pieces[b][main + 8 * word : main + 8 * word + 8, :]
            shift = (GROUP * steps_dev * (source - place)) & (LANES - 1)
            found = jnp.where(owner == source, pltpu.roll(value, shift, 1), found)
        side[f, 8 * r : 8 * r + 8, :] = found
        hstate[f, MAIN + 8 * r : MAIN + 8 * r + 8, :] = found
    Side(MAIN, rows).set_seams(seams, [side[f] for f in range(fields)])

    for t in range(1, blocks):

        def send(p, f, c, value):
            at = ((p * FIELDS + f) * SLABS + c) * (rows - 8) + 8 * t - 8
            sent[at : at + 8, :] = value

        residual_tile(steps, first_half, ROW0 + 8 * t, state, rhs, seams, ends, send)

    sides = Side(ROW0 + 8, rows - 8)
    before_first = lambda f: side_initial[f, HALO : rows - HALO, :]
    handed = side_residual(sides, steps, first_half, hstate, ends, before_first, hrhs)
    flat = [handed[f][at : at + 8, :] for f in range(FIELDS) for at in range(0, rows - 8, 8)]
    pack_sides(flat, sent, SWEEPS * FIELDS * SLABS * (rows - 8))


def outer_kernel(width_tm, steps_dev, rows, *refs):
    half = width_tm // 2
    side, side_initial, above, below = refs[4:8]
    state, rhs, ends, hrhs, sent, hstate, hbefore, seams = refs[8:]
    steps = half * steps_dev
    me = lax.axis_index("tm")
    mine = me & (half - 1)
    first_half = me < half
    body = slice(MAIN, MAIN + rows)
    top, bottom = slice(ROW0, MAIN), slice(MAIN + rows, MAIN + rows + HALO)
    k = 0
    for b in range(half):
        for c in range(SLABS):
            for i in range(steps_dev):
                n = steps_dev * (mine ^ b) + i
                for f in range(FIELDS):
                    state[n + 1, f, c, top, :] = above[k : k + HALO, :]
                    state[n + 1, f, c, bottom, :] = below[k : k + HALO, :]
                    k += HALO
    for c in range(SLABS):
        for f in range(FIELDS):
            state[0, f, c, top, :] = jnp.where(first_half, above[k : k + HALO, :], 0.0)
            state[0, f, c, bottom, :] = jnp.where(first_half, below[k : k + HALO, :], 0.0)
            k += HALO
    for held, given in ((hstate, side), (hbefore, side_initial)):
        for f in range(FIELDS):
            held[f, body, :] = given[f, :, :]
            held[f, top, :] = above[k : k + HALO, :]
            held[f, bottom, :] = below[k : k + HALO, :]
            k += HALO
    whole = Side(ROW0, rows + 2 * HALO)
    whole.set_seams(seams, [hstate[f, whole.span, :] for f in range(FIELDS)])
    flat = []
    for which, start in enumerate((ROW0, ROW0 + rows)):

        def send(p, f, c, value):
            at = (((p * FIELDS + f) * SLABS + c) * 2 + which) * 7
            sent[at : at + 7, :] = value[1 - which : 8 - which, :]

        residual_tile(steps, first_half, start, state, rhs, seams, ends, send)
        sides = Side(start, 8)
        before_first = lambda f: hbefore[f, start : start + 8, :]
        flat += side_residual(sides, steps, first_half, hstate, ends, before_first, hrhs)
    pack_sides(flat, sent, SWEEPS * FIELDS * SLABS * 14)


def chain_kernel(steps, rows, rhs, hrhs, result, ya, yb, hya, hyb, ends, seams):
    _, ratios, _ = chain_factors()
    sides = Side(ROW0, rows + 2 * HALO)
    blocks = sides.tall // 8
    running = lane_matrix(
        lambda source, target: jnp.where((source <= target) & (target < steps), 1.0, 0.0)
    )
    side_new = sides.product([hrhs[f, sides.span, :] for f in range(FIELDS)], running)
    for f in range(FIELDS):
        hya[f, sides.span, :] = side_new[f]
    sides.set_seams(seams, side_new)

    @pl.loop(0, blocks)
    def _(t):
        start = ROW0 + 8 * t
        for f, c in EACH:
            total = jnp.zeros((8, LANES), jnp.float32)
            for n in range(steps):
                total = total + rhs[n, f, c, pl.ds(start, 8), :]
                ya[n, f, c, pl.ds(start, 8), :] = total

    def sweep(ratio, old, hold, new, hnew, final):
        first = MAIN if final else ROW0

        @pl.loop(0, rows // 8 if final else blocks)
        def _(t):
            start = first + 8 * t
            seam = [seams[f, pl.ds(start, 8), :] for f in range(FIELDS)]
            last = zeros(FIELDS)
            total = dict(zip(EACH, zeros(len(EACH))))
            for n in range(steps):
                parts = neighbours(old, n, start, seam, n)
                if not final:
                    add_ends(last, parts[0], n)
                for c in range(SLABS):
                    value = off_diagonal(*slab(parts, c))
                    for f in range(FIELDS):
                        carry = value[f] + ratio * rhs[n, f, c, pl.ds(start, 8), :]
                        total[f, c] = total[f, c] + carry
                        if final:
                            at = pl.ds(pl.multiple_of(8 * t, 8), 8)
                            new[n, f, c, at, :] = total[f, c]
                        else:
                            new[n, f, c, pl.ds(start, 8), :] = total[f, c]
            if not final:
                for f in range(FIELDS):
                    ends[f, pl.ds(start, 8), :] = last[f]

        if not final:
            value = off_diagonal(*sides.parts(hold, ends))
            side_next = sides.product(
                [value[f] + ratio * hrhs[f, sides.span, :] for f in range(FIELDS)], running
            )
            for f in range(FIELDS):
                hnew[f, sides.span, :] = side_next[f]
            sides.set_seams(seams, side_next)

    buffers = [(ya, hya), (yb, hyb)]
    for m in range(1, SWEEPS):
        old, new = buffers[(m + 1) % 2], buffers[m % 2]
        final = m == SWEEPS - 1
        sweep(ratios[m - 1], *old, result if final else new[0], new[1], final)


def join_kernel(width_tm, steps_dev, rows, inner_rows, *refs):
    half = width_tm // 2
    count = 2 if inner_rows else 4
    given_refs, (chained, state) = refs[:count], refs[count : count + 2]
    outs = refs[-9 - half : -9]
    given, pa, pb, hgiven, hpa, hpb, ends, seams, result = refs[-9:]
    inner_own, inner_other = given_refs[:2]
    steps = half * steps_dev
    me = lax.axis_index("tm")
    mine = me & (half - 1)
    gammas, _, scale = chain_factors()
    own, first, second = swap_factors(steps)
    other = [jnp.where(me < half, a, b) for a, b in zip(first, second)]
    tiles = rows // 8
    if inner_rows:
        sides = Side(ROW0 + 8, rows - 8)
        places = (tiles - 1, lambda t: ROW0 + 8 + 8 * t)
        finals = (tiles - 2, lambda t: MAIN + 8 + 8 * t)
    else:
        sides = Side(ROW0, rows + 2 * HALO)
        places = (4, lambda t: ROW0 + 8 * (t + (tiles - 3) * (t // 2)))
        finals = (2, lambda t: MAIN + (rows - 8) * t)
    cells = SWEEPS * FIELDS * SLABS

    def joined(ref_own, ref_other, at, size, step, p):
        total = None
        for d in range(SWEEPS - p):
            rows_d = slice(at + step * d, at + step * d + size)
            term = other[d] * ref_other[rows_d, :] + own[d] * ref_own[rows_d, :]
            total = term if total is None else total + term
        return total

    for p in range(SWEEPS):
        for f, c in EACH:
            cell = (p * FIELDS + f) * SLABS + c
            found = [(ROW0 + 8, joined(inner_own, inner_other, cell * (rows - 8), rows - 8, FIELDS * SLABS * (rows - 8), p))]
            if not inner_rows:
                for which, start in ((0, ROW0 + 1), (1, ROW0 + rows)):
                    at = (cell * 2 + which) * 7
                    found.append((start, joined(*given_refs[2:], at, 7, FIELDS * SLABS * 14, p)))
            for start, value in found:
                given[p, f, c, start : start + value.shape[0], :] = value
                pa[p, f, c, start : start + value.shape[0], :] = gammas[-1] * value

    step8 = step_of_lane(lanes())

    def from_later(value, d, step):
        return jnp.where(step < SWEEPS - d, turn(value, -GROUP * d), 0.0)

    def set_side(refs_side, at, index, f, start):
        ours, theirs = (unpack_side(ref, at, index) for ref in refs_side)
        value = jnp.zeros((8, LANES), jnp.float32)
        for d in range(SWEEPS):
            value = value + from_later(other[d] * theirs + own[d] * ours, d, step8)
        hgiven[f, start : start + 8, :] = value
        hpa[f, start : start + 8, :] = gammas[-1] * value

    for f in range(FIELDS):
        for r in range(tiles - 1):
            set_side(given_refs[:2], cells * (rows - 8), f * (tiles - 1) + r, f, ROW0 + 8 + 8 * r)
        if not inner_rows:
            for which, start in ((0, ROW0), (1, ROW0 + rows)):
                set_side(given_refs[2:], cells * 14, which * FIELDS + f, f, start)
    sides.set_seams(seams, [hpa[f, sides.span, :] for f in range(FIELDS)])

    buffers = [(pa, hpa), (pb, hpb)]
    for k in range(1, SWEEPS):
        (old, hold), (new, hnew) = buffers[(k + 1) % 2], buffers[k % 2]
        gamma = gammas[SWEEPS - 1 - k]
        final = k == SWEEPS - 1
        turns, place = finals if final else places

        for t in range(turns):
            start = place(t)
            here = pl.ds(start, 8)
            seam = [seams[f, here, :] for f in range(FIELDS)]
            last = zeros(FIELDS)
            found = {}
            for p in range(SWEEPS):
                parts = neighbours(old, p, start, seam, p)
                if not final:
                    add_ends(last, parts[0], p)
                for c in range(SLABS):
                    value = off_diagonal(*slab(parts, c))
                    for f in range(FIELDS):
                        total = value[f]
                        if p + k < SWEEPS:
                            total = total + gamma * given[p + k, f, c, here, :]
                        if final:
                            found[p, f, c] = total * RATE ** (p + 1)
                        else:
                            new[p, f, c, here, :] = total
            if not final:
                for f in range(FIELDS):
                    ends[f, here, :] = last[f]
            else:
                at = pl.ds(8 * t, 8)
                from_chain = pl.ds(start - MAIN, 8)
                for f, c in EACH:
                    for n in range(steps):
                        total = (scale * RATE**n) * chained[n, f, c, from_chain, :]
                        for p in range(SWEEPS):
                            total = total + (binomial(n + p, p) * RATE**n) * found[p, f, c]
                        result[n, f, c, at, :] = state[n + 1, f, c, here, :] - total

        if not final:
            value = off_diagonal(*sides.parts(hold, ends))
            side_next = [
                value[f] + gamma * from_later(hgiven[f, sides.span, :], k, sides.step)
                for f in range(FIELDS)
            ]
            for f in range(FIELDS):
                hnew[f, sides.span, :] = side_next[f]
            sides.set_seams(seams, side_next)

    size = 8 * finals[0]
    for b in range(half):
        at = 0
        for c in range(SLABS):
            for i in range(steps_dev):
                n = steps_dev * (mine ^ b) + i
                for f in range(FIELDS):
                    outs[b][at : at + size, :] = result[n, f, c, :, :]
                    at += size


def unpack_kernel(width_tm, size, *refs):
    half = width_tm // 2
    out = refs[-1]
    steps_dev, fields, _, _ = out.shape
    mine = lax.axis_index("tm") & (half - 1)
    t = pl.program_id(0)
    for b in range(half):
        at = 0
        for c in range(SLABS):
            here = tile_at(SLABS * (mine ^ b) + c)
            for i in range(steps_dev):
                for f in range(fields):
                    out[i, f, :, here] = refs[b][pl.ds(pl.multiple_of(at + 8 * t, 8), 8), :]
                    at += size


def unpack(width_tm, shape, pieces, size, place, held=()):
    steps_dev, fields, _, columns = shape
    return pl.pallas_call(
        functools.partial(unpack_kernel, width_tm, size),
        grid=(size // 8,),
        out_shape=jax.ShapeDtypeStruct(shape, jnp.float32),
        in_specs=[pl.BlockSpec(memory_space=pltpu.VMEM)] * len(pieces)
        + [pl.BlockSpec(memory_space=pl.ANY)] * len(held),
        out_specs=pl.BlockSpec((steps_dev, fields, 8, columns), lambda t: (0, 0, place(t), 0)),
        input_output_aliases={len(pieces): 0} if held else {},
        compiler_params=pltpu.CompilerParams(vmem_limit_bytes=VMEM_BYTES),
    )(*pieces, *held)


def call(kernel, out_shapes, operands, scratch=(), aliases=None, after=()):
    whole = pl.BlockSpec(memory_space=pltpu.VMEM)
    shapes = [jax.ShapeDtypeStruct(shape, jnp.float32) for shape in out_shapes]
    moved = 4 * sum(math.prod(x.shape) for x in list(shapes) + list(operands))
    in_specs = [whole] * len(operands) + [pl.BlockSpec(memory_space=pl.ANY)] * len(after)
    operands = list(operands) + list(after)
    return pl.pallas_call(
        kernel,
        out_shape=shapes,
        in_specs=in_specs,
        out_specs=[whole] * len(shapes),
        scratch_shapes=[pltpu.VMEM(shape, jnp.float32) for shape in scratch],
        input_output_aliases=aliases or {},
        compiler_params=pltpu.CompilerParams(vmem_limit_bytes=VMEM_BYTES),
        cost_estimate=pl.CostEstimate(flops=moved, bytes_accessed=moved, transcendentals=0),
    )(*operands)


def swap(piece, b):
    count = lax.axis_size("tm")
    return lax.ppermute(piece, "tm", [(k, k ^ b) for k in range(count)])


def fast_on_device(state, initial):
    steps_dev, fields, rows, columns = state.shape
    width_tm = lax.axis_size("tm")
    bands = lax.axis_size("space")
    half = width_tm // 2
    steps = steps_dev * half
    main = SLABS * steps_dev * fields * rows
    words = -(-fields * rows // 8 // (LANES // (GROUP * steps_dev)))
    tall = rows + 2 * HALO + 2 * ROW0
    sized = (width_tm, steps_dev)
    pieces = call(
        functools.partial(pack_kernel, width_tm), [(main + 8 * words, LANES)] * half, [state]
    )
    pieces = [pieces[0]] + [swap(pieces[b], b) for b in range(1, half)]
    tiles, side_initial = call(
        functools.partial(place_initial, width_tm),
        [(fields, SLABS, rows, LANES), (fields, rows, LANES)],
        [initial],
        after=pieces[:1],
    )
    flat = (fields, tall, LANES)
    held_shapes = [
        (steps + 1, fields, SLABS, tall, LANES),
        (steps, fields, SLABS, tall, LANES),
        flat,
        flat,
    ]
    cells = SWEEPS * fields * SLABS
    inner_words = -(-fields * (rows - 8) // 8 // PER_WORD)
    outer_words = -(-2 * fields // PER_WORD)
    *held, side, inner = call(
        functools.partial(inner_kernel, *sized),
        held_shapes
        + [(fields, rows, LANES), (cells * (rows - 8) + 8 * inner_words, LANES)],
        pieces + [tiles, side_initial],
        [flat] * 2,
    )
    inner_other = swap(inner, half)
    edge_rows = -(-HALO * fields * (SLABS * (steps + 1) + 2) // 8) * 8
    up, down = call(
        functools.partial(edge_kernel, width_tm),
        [(edge_rows, LANES)] * 2,
        pieces + [tiles, side, side_initial],
    )
    above = lax.ppermute(down, "space", [(i, (i + 1) % bands) for i in range(bands)])
    below = lax.ppermute(up, "space", [((i + 1) % bands, i) for i in range(bands)])
    solved, rhs, _, hrhs, outer = call(
        functools.partial(outer_kernel, *sized, rows),
        held_shapes + [(cells * 14 + 8 * outer_words, LANES)],
        held + [side, side_initial, above, below],
        [flat] * 3,
        aliases={0: 0, 1: 1, 2: 2, 3: 3},
    )
    outer_other = swap(outer, half)
    (chained,) = call(
        functools.partial(chain_kernel, steps, rows),
        [(steps, fields, SLABS, rows, LANES)],
        [rhs, hrhs],
        [held_shapes[1]] * 2 + [flat] * 4,
    )
    four = (SWEEPS, fields, SLABS, tall, LANES)
    results = []
    for given, size in (
        ([inner, inner_other], rows - 16),
        ([inner, inner_other, outer, outer_other], 16),
    ):
        parts = call(
            functools.partial(join_kernel, *sized, rows, len(given) == 2),
            [(SLABS * steps_dev * fields * size, LANES)] * half,
            given + [chained, solved],
            [four] * 3 + [flat] * 5 + [(steps, fields, SLABS, size, LANES)],
            after=results[:1],
        )
        results += [parts[0]] + [swap(parts[b], b) for b in range(1, half)]
    updated = unpack(width_tm, state.shape, results[:half], rows - 16, lambda t: t + 1)
    updated = unpack(
        width_tm, state.shape, results[half:], 16, lambda t: t * (rows // 8 - 1), (updated,)
    )
    return updated


def choose(state, initial):
    if fits_fast_plan(state, lax.axis_size("tm")):
        return fast_on_device(state, initial)
    return on_device(state, initial)


def solution(mesh):
    in_specs = (P("tm", None, "space", None), P(None, "space", None))
    out_specs = P("tm", None, "space", None)
    return jax.shard_map(
        choose, mesh=mesh, in_specs=in_specs, out_specs=out_specs, check_vma=False
    )
```
